256 devices in a mesh: wide: 32 (over y, x, core), narrow: 8 (over z).
Axes of the slice: x: 4, y: 4, z: 8, core: 2. Of those that a mesh axis runs over, the one named last changes fastest.
Arguments:
- noise: float32 [1024, 1024, 128], P('narrow', 'wide'), may hold values from -6 to 6
- spectrum: float32 [128, 1024, 1024], P('wide', None, 'narrow'), may hold values from 0.1 to 8.5, as said below
- assay: bfloat16 [256, 512], P(('wide', 'narrow')), may hold values from -5 to 5
- measure_weights: bfloat16 [256, 512, 4, 128], P(('wide', 'narrow')), may hold values from -3 to 3
- measure_owner: int32 [256, 512], P(('wide', 'narrow')), may hold values from 0 to 255, as said below
- measure_cell: int32 [256, 512], P(('wide', 'narrow')), may hold values from 0 to 524287
- measure_pencils: int32 [256, 512, 4], P(('wide', 'narrow')), may hold values from 0 to 4095
Outputs:
- conditioned: float32 [1024, 1024, 128], P('narrow', 'wide')
The draws below stay inside these ranges and needn't reach their ends.
Inputs may be any that keep to these rules, and one draw needn't show every extreme that they name: `spectrum`: Positive, with rough factors from frequency to frequency. `measure_owner`: devices are numbered with narrow fastest. At most 8 measurements of one device share an owner; one owner, drawn from the seed, receives exactly 8 from every device. `measure_cell`: cells of the owner's block are numbered with z fastest, then y, then x. `measure_pencils`: pencils of the owner's block are numbered with y fastest.
All inputs are finite; a program needn't handle non-finite values.
Results may differ from the reference program's by a relative error of at most 0.0003.
Values may be sent and summed in bfloat16 or wider, within the bound.
A program may use at most 128 MiB of HBM per device.

```python
import math
import jax
import jax.numpy as jnp

CELLS_FIRST = 1024
CELLS_SECOND = 1024
CELLS_THIRD = 128
TARGET_PENCILS = 4
MEASURES_PER_CHIP = 512
SOURCE_DEVICES = 256
CAP = 8
CX = 128
CY = 32
HALF_Z = 2
N_NARROW = 8


def signed_freq(count):
    index = jnp.arange(count, dtype=jnp.int32)
    return ((index + count // 2) % count - count // 2).astype(jnp.float32) / count


def slot_freq():
    slots = jnp.arange(CELLS_THIRD, dtype=jnp.int32)
    span = 2 * HALF_Z
    base = slots // span * HALF_Z + slots % span % HALF_Z
    mirror = jnp.where(base > 0, CELLS_THIRD - base, CELLS_THIRD // 2)
    depth_of = jnp.where(slots % span < HALF_Z, base, mirror)
    return ((depth_of + CELLS_THIRD // 2) % CELLS_THIRD - CELLS_THIRD // 2).astype(jnp.float32) / CELLS_THIRD


def draw_spectrum(key, part):
    freq_z = slot_freq()[:, None, None]
    freq_x = signed_freq(CELLS_FIRST)[None, :, None]
    freq_y = signed_freq(CELLS_SECOND)[None, None, :]
    radius = freq_x * freq_x + freq_y * freq_y + 4.0 * freq_z * freq_z
    shape = (CELLS_THIRD, CELLS_FIRST, CELLS_SECOND)
    rough = jnp.exp(jax.random.uniform(key, shape, jnp.float32, -math.log(2.0), math.log(2.0)))
    envelope = 0.5 + 2.0 / (1.0 + 400.0 * radius)
    return (envelope * rough).astype(jnp.float32)


def permute_others(subkey):
    return jax.random.permutation(subkey, SOURCE_DEVICES - 1)


def permute_slots(subkey):
    return jax.random.permutation(subkey, MEASURES_PER_CHIP)


def draw_measure_owner(key, part):
    key_hot, key_perm, key_off, key_rows = jax.random.split(jax.random.fold_in(key, 17), 4)
    hot = jax.random.randint(key_hot, (), 0, SOURCE_DEVICES)
    others = jax.vmap(permute_others)(jax.random.split(key_perm, SOURCE_DEVICES))
    offsets = jax.random.randint(key_off, (SOURCE_DEVICES, 1), 0, CAP)
    row_index = jnp.arange(MEASURES_PER_CHIP, dtype=jnp.int32)[None, :]
    group = jnp.clip((row_index - CAP + offsets) // CAP, 0, SOURCE_DEVICES - 2)
    other = (hot + 1 + jnp.take_along_axis(others, jnp.broadcast_to(group, (SOURCE_DEVICES, MEASURES_PER_CHIP)), axis=1)) % SOURCE_DEVICES
    owner_device = jnp.where(row_index < CAP, hot, other)
    order = jax.vmap(permute_slots)(jax.random.split(key_rows, SOURCE_DEVICES))
    return jnp.take_along_axis(owner_device, order, axis=1).astype(jnp.int32)


def set_ends(values, own_key, low, largest):
    longest = values.shape.index(max(values.shape))
    spots = []
    for shift in (0, 1):
        where = [jax.random.randint(jax.random.fold_in(own_key, axis), (), 0, length) for axis, length in enumerate(values.shape)]
        where[longest] = (where[longest] + shift) % values.shape[longest]
        spots.append(tuple(where))
    return values.at[spots[0]].set(low).at[spots[1]].set(largest)


def level_of(key, dims, cuts, least, top_value):
    def one(dim, parts):
        draws = jax.random.uniform(jax.random.fold_in(jax.random.fold_in(key, 6), dim), (parts,), jnp.float32, least / len(cuts), top_value / len(cuts))
        return jnp.repeat(jnp.exp(draws), dims[dim] // parts).reshape((-1,) + (1,) * (len(dims) - dim - 1))

    loudness = one(*cuts[0])
    for cut in cuts[1:]:
        loudness = loudness * one(*cut)
    return loudness


def normal_values(rng, shape, deviation, bound, cuts=(), held_as=jnp.bfloat16):
    result = jax.random.normal(rng, shape, jnp.float32) * deviation
    if len(cuts) > 0:
        result = level_of(rng, shape, cuts, -0.22, 0.18) * result
    return jnp.clip(result, min=-bound, max=bound).astype(held_as)


def setup_inputs(seed: int = 0) -> dict:
    splits = jax.random.split(jax.random.key(seed), 8)
    noise = normal_values(splits[0], (CELLS_FIRST, CELLS_SECOND, CELLS_THIRD), 1.0, 6.0, ((0, 8), (1, 32)), jnp.float32)
    spectrum = draw_spectrum(jax.random.fold_in(splits[7], 71), 0)
    assay = normal_values(splits[2], (SOURCE_DEVICES, MEASURES_PER_CHIP), 1.0, 5.0, ((0, 256),))
    measure_weights = normal_values(splits[3], (SOURCE_DEVICES, MEASURES_PER_CHIP, TARGET_PENCILS, CELLS_THIRD), 0.5, 3.0, ((0, 256),))
    measure_owner = draw_measure_owner(jax.random.fold_in(splits[7], 71), 0)
    measure_cell = set_ends(jax.random.randint(splits[5], (SOURCE_DEVICES, MEASURES_PER_CHIP), 0, CELLS_FIRST * CELLS_SECOND * CELLS_THIRD // SOURCE_DEVICES), jax.random.fold_in(splits[5], 1), 0, (CELLS_FIRST * CELLS_SECOND * CELLS_THIRD // SOURCE_DEVICES) - 1).astype(jnp.int32)
    measure_pencils = set_ends(jax.random.randint(splits[6], (SOURCE_DEVICES, MEASURES_PER_CHIP, TARGET_PENCILS), 0, CELLS_FIRST * CELLS_SECOND // SOURCE_DEVICES), jax.random.fold_in(splits[6], 1), 0, (CELLS_FIRST * CELLS_SECOND // SOURCE_DEVICES) - 1).astype(jnp.int32)
    return dict(noise=noise, spectrum=spectrum, assay=assay, measure_weights=measure_weights, measure_owner=measure_owner, measure_cell=measure_cell, measure_pencils=measure_pencils)


def slot_depth():
    slots = jnp.arange(CELLS_THIRD, dtype=jnp.int32)
    span = 2 * HALF_Z
    base = (slots // span) * HALF_Z + (slots % span) % HALF_Z
    mirror = jnp.where(base > 0, CELLS_THIRD - base, CELLS_THIRD // 2)
    return jnp.where(slots % span < HALF_Z, base, mirror).astype(jnp.int32)


def reference(noise, spectrum, assay, measure_weights, measure_owner, measure_cell, measure_pencils):
    depth_of = slot_depth()
    natural = jnp.zeros((CELLS_THIRD, CELLS_FIRST, CELLS_SECOND), jnp.float32).at[depth_of].set(spectrum)
    filt = jnp.transpose(natural, (1, 2, 0))
    field = jnp.real(jnp.fft.ifftn(jnp.fft.fftn(noise) * filt)).astype(jnp.float32)
    owner_device = measure_owner.reshape(-1).astype(jnp.int32)
    owner_w = owner_device // N_NARROW
    owner_n = owner_device % N_NARROW
    cell_list = measure_cell.reshape(-1).astype(jnp.int32)
    cell_x = owner_n * CX + cell_list // (CY * CELLS_THIRD)
    cell_y = owner_w * CY + (cell_list // CELLS_THIRD) % CY
    cell_z = cell_list % CELLS_THIRD
    value = field[cell_x, cell_y, cell_z]
    resid = assay.reshape(-1).astype(jnp.float32) - value
    block_list = measure_pencils.reshape(-1, TARGET_PENCILS).astype(jnp.int32)
    block_x = owner_n[:, None] * CX + block_list // CY
    block_y = owner_w[:, None] * CY + block_list % CY
    target = (block_x * CELLS_SECOND + block_y).reshape(-1).astype(jnp.int32)
    kriging_weights = measure_weights.reshape(-1, TARGET_PENCILS, CELLS_THIRD).astype(jnp.float32)
    contrib = (resid[:, None, None] * kriging_weights).reshape(-1, CELLS_THIRD)
    correction = jnp.zeros((CELLS_FIRST * CELLS_SECOND, CELLS_THIRD), jnp.float32).at[target].add(contrib)
    return field + correction.reshape(CELLS_FIRST, CELLS_SECOND, CELLS_THIRD)
```

```python
import math

import jax
import jax.numpy as jnp
import ml_dtypes
import numpy as np
from jax import lax
from jax.experimental import pallas as pl
from jax.experimental.pallas import tpu as pltpu
from jax.sharding import PartitionSpec as P

NX, NY, NZ = 1024, 1024, 128
TARGETS = 4
WIDE, NARROW = 32, 8
SLOTS = 2
MESH = pl.DeviceIdType.MESH
f32, bf16, i32 = jnp.float32, jnp.bfloat16, jnp.int32

LN2 = math.log(2.0)
CODE = 16.0 / LN2
PEAK = 32600.0
TINY = 1e-30
SPEC_LOW = math.log(0.1)
SPEC_CODE = 65000.0 / math.log(85.0)
ROOT_HALF = math.sqrt(0.5)


def split(a):
    high = a.astype(ml_dtypes.bfloat16)
    low = (a - high.astype(np.float64)).astype(ml_dtypes.bfloat16)
    return high, low


def pair_matrix(sign):
    index = np.arange(128)
    angle = 2 * np.pi * (index[:, None] * index[None, :] % 128) / 128
    c, s = np.cos(angle), sign * np.sin(angle)
    return np.block([[c, -s], [s, c]])


def depth_forward():
    kz = 2 * np.arange(32)[None, :] + np.arange(2)[:, None]
    kz = kz.reshape(-1)
    z = np.arange(128)
    angle = 2 * np.pi * (kz[:, None] * z[None, :] % 128) / 128
    re, im = np.cos(angle), -np.sin(angle)
    im[kz == 0] = np.cos(np.pi * z)
    return np.concatenate([re, im], 0)


def depth_inverse():
    kz = (2 * np.arange(32)[None, :] + np.arange(2)[:, None]).reshape(-1)
    z = np.arange(128)
    angle = 2 * np.pi * (kz[:, None] * z[None, :] % 128) / 128
    re, im = 2 * np.cos(angle), -2 * np.sin(angle)
    re[kz == 0] = 1.0
    im[kz == 0] = np.cos(np.pi * z)
    return np.concatenate([re, im], 0)


def make_tables():
    h, l = split(depth_forward())
    tz = np.concatenate([h, l, h], 1)
    h, l = split(depth_inverse())
    tzi = np.concatenate([h, l, h], 0)
    yf = np.stack(split(pair_matrix(-1.0)))
    yi = np.stack(split(pair_matrix(1.0)))
    xf = np.stack(split(pair_matrix(-1.0).T))
    xi = np.stack(split(pair_matrix(1.0).T))
    c = np.arange(8)
    a = np.arange(128)
    angle = 2 * np.pi * c[:, None] * a[None, :] / 1024
    tx = np.stack([np.cos(angle), np.sin(angle)]).astype(np.float32)
    row = np.arange(128)
    lane_of = 8 * (row % 16) + row // 16
    own = np.zeros((128, 128))
    own[row, lane_of] = 1
    mir = np.zeros((128, 128))
    mir[row, (128 - lane_of) % 128] = 1
    own2 = np.concatenate([own, own], 1).astype(ml_dtypes.bfloat16)
    flips = np.zeros((2, 128, 128))
    flips[0, (128 - row) % 128, row] = 1
    flips[1, 127 - row, row] = 1
    flips = np.concatenate([flips, flips], 1).astype(ml_dtypes.bfloat16)
    return dict(
        tz=tz, tzi=tzi, yf=yf, yi=yi, xf=xf, xi=xi, tx=tx, own2=own2,
        mir=mir.astype(ml_dtypes.bfloat16), flips=flips,
    )


TABLES = make_tables()


def halves(v):
    h = v.astype(bf16)
    return h, (v - h.astype(f32)).astype(bf16)


def times_i(v, sign):
    re, im = v
    return (-im, re) if sign > 0 else (im, -re)


def add(a, b):
    return a[0] + b[0], a[1] + b[1]


def sub(a, b):
    return a[0] - b[0], a[1] - b[1]


def dft4(v, sign):
    s, d = add(v[0], v[2]), sub(v[0], v[2])
    t, u = add(v[1], v[3]), times_i(sub(v[1], v[3]), sign)
    return [add(s, t), add(d, u), sub(s, t), sub(d, u)]


def dft8(v, sign):
    e = dft4(v[0::2], sign)
    o = dft4(v[1::2], sign)
    g = float(sign)
    re, im = o[1]
    o[1] = ((re - g * im) * ROOT_HALF, (im + g * re) * ROOT_HALF)
    o[2] = times_i(o[2], sign)
    re, im = o[3]
    o[3] = ((-re - g * im) * ROOT_HALF, (g * re - im) * ROOT_HALF)
    return [add(e[c], o[c]) for c in range(4)] + [sub(e[c], o[c]) for c in range(4)]


def turn(v, cos, sin, sign):
    re, im = v
    if sign < 0:
        return re * cos + im * sin, im * cos - re * sin
    return re * cos - im * sin, im * cos + re * sin


def scale_code(m):
    return jnp.ceil(jnp.log(jnp.maximum(m, TINY)) * CODE).astype(i32)


def encode_factor(code):
    return jnp.exp(code.astype(f32) * (-1.0 / CODE)) * PEAK


def decode_factor(code):
    return jnp.exp(code.astype(f32) * (1.0 / CODE)) * (1.0 / PEAK)


def pack(re, im):
    a = jnp.round(re).astype(i32)
    b = jnp.round(im).astype(i32)
    return (a << 16) | (b & 0xFFFF)


def unpack(word):
    return (word >> 16).astype(f32), ((word << 16) >> 16).astype(f32)


def tile_max(tiles):
    tiles = [jnp.abs(t) for t in tiles]
    while len(tiles) > 1:
        tiles = [jnp.maximum(a, b) for a, b in zip(tiles[0::2], tiles[1::2])] + (
            tiles[-1:] if len(tiles) % 2 else []
        )
    return tiles[0]


def mm(a, b):
    return jnp.dot(a, b, preferred_element_type=f32)


def mm_t(a, b):
    return lax.dot_general(a, b, (((1,), (1,)), ((), ())), preferred_element_type=f32)


def rows(start, size):
    return pl.ds(pl.multiple_of(start, 8), size)


def rows16(start, size):
    return pl.ds(pl.multiple_of(start, 16), size)


def spectral_kernel(
    noise, spec, tz, yf, yi, xf, xi, tyc, tys, tx, own2, mir, flips,
    out,
    zre, zim, ws, wr, bh, bl, big, big2, ns, nr, lh, ll, ms, mr, us,
    ear, bsp, vs, vr, vc,
    w_send, w_recv, n_send, n_recv, m_send, m_recv, u_send, u_recv, v_send, v_recv,
):
    me_w = lax.axis_index("wide")
    me_n = lax.axis_index("narrow")
    special = me_w == 0
    edge = special & ((me_n == 0) | (me_n == 4))

    barrier = pltpu.get_barrier_semaphore()

    def greet_wide(i, _):
        pl.semaphore_signal(
            barrier, inc=1, device_id={"wide": lax.rem(me_w + i, WIDE)}, device_id_type=MESH
        )
        return 0

    def greet_narrow(i, _):
        pl.semaphore_signal(
            barrier, inc=1, device_id={"narrow": lax.rem(me_n + i, NARROW)}, device_id_type=MESH
        )
        return 0

    lax.fori_loop(1, WIDE, greet_wide, 0)
    lax.fori_loop(1, NARROW, greet_narrow, 0)

    def wide_copy(src, dst, sends, recvs, s, peer, slot):
        return pltpu.make_async_remote_copy(
            src_ref=src.at[s, peer], dst_ref=dst.at[s, slot], send_sem=sends.at[s, peer],
            recv_sem=recvs.at[s, slot], device_id={"wide": peer}, device_id_type=MESH,
        )

    def narrow_copy(src, dst, sends, recvs, s, peer, slot):
        return pltpu.make_async_remote_copy(
            src_ref=src.at[s, peer], dst_ref=dst.at[s, slot], send_sem=sends.at[s, peer],
            recv_sem=recvs.at[s, slot], device_id={"narrow": peer}, device_id_type=MESH,
        )

    def send_all(make, count, me, args, s):
        def one(i, _):
            make(*args, s, lax.rem(me + i, count), me).start()
            return 0

        lax.fori_loop(1, count, one, 0)

    def recv_all(make, count, me, args, s):
        def one(i, _):
            peer = lax.rem(me + i, count)
            make(*args, s, peer, peer).wait_recv()
            return 0

        lax.fori_loop(1, count, one, 0)

    def sent_all(make, count, me, args, s):
        def one(i, _):
            peer = lax.rem(me + i, count)
            make(*args, s, peer, peer).wait_send()
            return 0

        lax.fori_loop(1, count, one, 0)

    w_args = (ws, wr, w_send, w_recv)
    n_args = (ns, nr, n_send, n_recv)
    m_args = (ms, mr, m_send, m_recv)
    u_args = (us, out, u_send, u_recv)

    def depth(y, _):
        h, l = halves(noise[pl.ds(y, 128, stride=32), :])
        res = mm_t(tz[...], jnp.concatenate([h, h, l], axis=1))
        zre[pl.ds(y, 64, stride=32), :] = res[:64]
        zim[pl.ds(y, 64, stride=32), :] = res[64:]
        return 0

    lax.fori_loop(0, 32, depth, 0)

    def code_wide(read, dst, s, w, to):
        re, im = read(w)
        m = tile_max([re[8 * t : 8 * t + 8] for t in range(4)] + [im[8 * t : 8 * t + 8] for t in range(4)])
        code = scale_code(m)
        fac = encode_factor(code)
        for t in range(4):
            sl = slice(8 * t, 8 * t + 8)
            dst[s, to, 8 * t : 8 * t + 8, :] = pack(re[sl] * fac, im[sl] * fac)
        dst[s, to, 32:40, :] = code

    for s in range(SLOTS):
        def read_depth(w, s=s):
            at = rows((s * 32 + w) * 32, 32)
            return zre[at, :], zim[at, :]

        def code_one(w, _, s=s, read=read_depth):
            code_wide(read, ws, s, w, w)
            return 0

        lax.fori_loop(0, WIDE, code_one, 0)
        wr[s, me_w] = ws[s, me_w]
        if s == 0:
            pl.semaphore_wait(barrier, WIDE - 1 + NARROW - 1)
        send_all(wide_copy, WIDE, me_w, w_args, s)

    late = special & (me_n >= 4)
    own_slots = (jnp.where(late, 2, 0), 1)
    mir_slots = (jnp.where(special & (me_n < 4), 2, jnp.where(special, 0, 2)), 3)

    def spectrum_rows(slot, e):
        return halves(spec[pl.ds(slot * 1024 + e, 128, stride=8), :])

    for e in range(8):
        back = (8 - e) % 8
        flip = flips[0 if e == 0 else 1]
        codes = []
        for s in range(SLOTS):
            h, l = spectrum_rows(own_slots[s], e)
            ear[s, e] = mm_t(own2[...], jnp.concatenate([h, l], axis=1))
            h, l = spectrum_rows(mir_slots[s], back)
            gh = mm_t(mir[...], h).astype(bf16)
            gl = mm_t(mir[...], l).astype(bf16)
            v = mm(jnp.concatenate([gh, gl], axis=1), flip)
            q = jnp.round((jnp.log(v) - SPEC_LOW) * SPEC_CODE - 32500.0)
            codes.append(jnp.clip(q, -32767.0, 32767.0))
        vs[e] = pack(codes[0], codes[1])

    v_main = pltpu.make_async_remote_copy(
        src_ref=vs, dst_ref=vr, send_sem=v_send.at[0], recv_sem=v_recv.at[0],
        device_id={"narrow": 7 - me_n}, device_id_type=MESH,
    )
    v_side = pltpu.make_async_remote_copy(
        src_ref=vs.at[:, pl.ds(0, 8), :], dst_ref=vc, send_sem=v_send.at[1], recv_sem=v_recv.at[1],
        device_id={"narrow": lax.rem(8 - me_n, 8)}, device_id_type=MESH,
    )
    v_main.start()
    alone = (me_n == 0) | (me_n == 4)

    @pl.when(jnp.logical_not(alone))
    def _():
        v_side.start()

    @pl.when(alone)
    def _():
        vc[...] = vs[:, 0:8, :]

    def second_forward(s, p, q, r):
        def group(g, _):
            dec = [decode_factor(wr[s, 4 * b + g, 32:40, :]) for b in range(8)]
            dec = [jnp.concatenate([d, d], axis=0) for d in dec]
            for t in range(2):
                v = []
                for b in range(8):
                    re, im = unpack(wr[s, 4 * b + g, 16 * t : 16 * t + 16, :])
                    re, im = re * dec[b], im * dec[b]
                    if p is not None:
                        re, im = re * p + im * q, im * r
                    v.append((re, im))
                v = dft8(v, -1)
                at = rows16(g * 32 + 16 * t, 16)
                at_im = rows16(128 + g * 32 + 16 * t, 16)
                for c in range(8):
                    w = v[c] if c == 0 else turn(v[c], tyc[c, at, :], tys[c, at, :], -1)
                    lanes = slice(128 * (c % 2), 128 * (c % 2) + 128)
                    for dst, part in ((at, w[0]), (at_im, w[1])):
                        h, l = halves(part)
                        bh[c // 2, dst, lanes] = h
                        bl[c // 2, dst, lanes] = l
            return 0

        lax.fori_loop(0, 4, group, 0)
        for cp in range(4):
            big[cp] = mm(yf[0], bh[cp]) + mm(yf[1], bh[cp]) + mm(yf[0], bl[cp])

    first_row = lax.broadcasted_iota(i32, (8, 128), 0) == 0

    def code_narrow(s, n):
        tiles = []
        for c in range(8):
            lanes = slice(128 * (c % 2), 128 * (c % 2) + 128)
            for t in range(2):
                tiles.append((
                    big[c // 2, rows(16 * n + 8 * t, 8), lanes],
                    big[c // 2, rows(128 + 16 * n + 8 * t, 8), lanes],
                ))
        code = scale_code(tile_max([x for pair in tiles for x in pair]))
        fac = encode_factor(code)
        for k, (re, im) in enumerate(tiles):
            ns[s, n, 8 * k : 8 * k + 8, :] = pack(re * fac, im * fac)
        ns[s, n, 128:136, :] = code

    for s in range(SLOTS):
        recv_all(wide_copy, WIDE, me_w, w_args, s)
        if s == 0:
            one = jnp.where(special, 0.0, 1.0)
            second_forward(s, 1.0, 0.0, one)

            @pl.when(special)
            def _():
                big2[...] = big[...]
                second_forward(0, 0.0, 1.0, 0.0)
                top = big[0, 0:8, 0:128]
                mid = big[0, 64:72, 0:128]
                big[:, 0:64, :] = big2[:, 0:64, :]
                big[:, 128:192, :] = big2[:, 128:192, :]
                big[0, 128:136, 0:128] = jnp.where(first_row, top, big[0, 128:136, 0:128])
                big[0, 192:200, 0:128] = jnp.where(first_row, mid, big[0, 192:200, 0:128])
                big[0, 64:72, 0:128] = jnp.where(first_row, big2[0, 64:72, 0:128], mid)
        else:
            second_forward(s, None, None, None)

        def code_n(n, _, s=s):
            code_narrow(s, n)
            return 0

        lax.fori_loop(0, NARROW, code_n, 0)
        nr[s, me_n] = ns[s, me_n]
        send_all(narrow_copy, NARROW, me_n, n_args, s)

    total = 1.0 / (NX * NY * NZ)
    v_main.wait_recv()

    @pl.when(jnp.logical_not(alone))
    def _():
        v_side.wait_recv()

    def decode_spectrum(q):
        return jnp.exp((q + 32500.0) * (1.0 / SPEC_CODE) + SPEC_LOW)

    bsp[...] = jnp.zeros_like(bsp)

    @pl.when(edge)
    def _():
        sigma = jnp.where(me_n == 0, 1.0, -1.0)
        xs, vv = [], []
        for e in range(8):
            xs.append(ear[0, e, 0:8, :])
            vv.append(decode_spectrum(unpack(vc[e])[0]))

        def even(list_of, e):
            h, l = halves(list_of[(8 - e) % 8])
            pair = jnp.concatenate([h, l], axis=1)
            flip = flips[0 if e == 0 else 1]
            return (mm(pair, flip) + list_of[e]) * 0.5

        for e in range(8):
            a, b = even(xs, e), even(vv, e)
            bsp[e, 0:8, :] = jnp.where(first_row, (a - b) * (0.5 * total) * sigma, 0.0)
            big2[0, 8 * e : 8 * e + 8, 0:128] = (a + b) * (0.5 * total)

    for e in range(8):
        m0, m1 = unpack(vr[e])
        s0, s1 = unpack(vc[e])
        for s, m, side in ((0, m0, s0), (1, m1, s1)):
            m, side = decode_spectrum(m), decode_spectrum(side)
            ear_e = ear[s, e]
            lead = jnp.where(first_row, side, m[0:8])
            ear[s, e, 8:128, :] = (ear_e[8:128] + m[8:128]) * (0.5 * total)
            ear[s, e, 0:8, :] = (ear_e[0:8] + lead) * (0.5 * total)

    @pl.when(edge)
    def _():
        for e in range(8):
            ear[0, e, 0:8, :] = jnp.where(
                first_row, big2[0, 8 * e : 8 * e + 8, 0:128], ear[0, e, 0:8, :]
            )

    def first_both(s):
        def decs(n):
            d = decode_factor(nr[s, n, 128:136, :])
            return jnp.concatenate([d, d], axis=0)

        for n in range(8):
            big2[0, 16 * n : 16 * n + 16, 0:128] = decs(n)

        def load(c):
            v = []
            for n in range(8):
                re, im = unpack(nr[s, n, rows16(16 * c, 16), :])
                d = big2[0, 16 * n : 16 * n + 16, 0:128]
                v.append((re * d, im * d))
            return v

        def put(v, at):
            v = dft8(v, -1)
            for e in range(8):
                w = v[e] if e == 0 else turn(v[e], tx[0, e : e + 1, :], tx[1, e : e + 1, :], -1)
                for lanes, part in ((slice(0, 128), w[0]), (slice(128, 256), w[1])):
                    h, l = halves(part)
                    lh[e, at, lanes] = h
                    ll[e, at, lanes] = l

        def block(c, _):
            put(load(c), rows16(16 * c, 16))
            return 0

        lax.fori_loop(0, 8, block, 0)
        if s == 0:
            put([(re, -im) for re, im in load(0)], slice(128, 144))
        count = 144 if s == 0 else 128
        for e in range(8):
            h, l = lh[e, 0:count, :], ll[e, 0:count, :]
            z = mm(h, xf[0]) + mm(h, xf[1]) + mm(l, xf[0])
            fil = jnp.concatenate([ear[s, e], ear[s, e]], axis=1)
            g = z[0:128] * fil
            if s == 0:
                extra = jnp.concatenate([bsp[e], bsp[e]], axis=1)
                g = jnp.concatenate([g[0:16] + z[128:144] * extra, g[16:128]], axis=0)
            h, l = halves(g)
            big[e // 2, 128 * (e % 2) : 128 * (e % 2) + 128, :] = (
                mm(h, xi[0]) + mm(h, xi[1]) + mm(l, xi[0])
            )

        def unblock(c, _):
            v = []
            for e in range(8):
                at = rows16(128 * (e % 2) + 16 * c, 16)
                y = (big[e // 2, at, 0:128], big[e // 2, at, 128:256])
                v.append(y if e == 0 else turn(y, tx[0, e : e + 1, :], tx[1, e : e + 1, :], 1))
            v = dft8(v, 1)
            for n in range(8):
                at = rows16(128 * (n % 2) + 16 * c, 16)
                big2[n // 2, at, 0:128] = v[n][0]
                big2[n // 2, at, 128:256] = v[n][1]
            return 0

        lax.fori_loop(0, 8, unblock, 0)
        for n in range(8):
            base = 128 * (n % 2)
            tiles = [
                (big2[n // 2, base + 8 * k : base + 8 * k + 8, 0:128],
                 big2[n // 2, base + 8 * k : base + 8 * k + 8, 128:256])
                for k in range(16)
            ]
            code = scale_code(tile_max([x for pair in tiles for x in pair]))
            fac = encode_factor(code)
            for k, (re, im) in enumerate(tiles):
                ms[s, n, 8 * k : 8 * k + 8, :] = pack(re * fac, im * fac)
            ms[s, n, 128:136, :] = code

    for s in range(SLOTS):
        recv_all(narrow_copy, NARROW, me_n, n_args, s)
        first_both(s)
        mr[s, me_n] = ms[s, me_n]
        send_all(narrow_copy, NARROW, me_n, m_args, s)

    row16 = lax.broadcasted_iota(i32, (16, 128), 0)

    def second_back(s, part):
        def fill(n, _):
            d = decode_factor(mr[s, n, 128:136, :])
            d = jnp.concatenate([d, d], axis=0)
            if part is not None:
                if part == 0:
                    f = jnp.where(special, jnp.where(n < 4, 2.0, 0.0), 1.0)
                else:
                    f = jnp.where(n < 4, 0.0, 2.0)
                hit = (row16 == 0) & (special & ((n == 0) | (n == 4)))
            for c in range(8):
                re, im = unpack(mr[s, n, 16 * c : 16 * c + 16, :])
                re, im = re * d, im * d
                if part == 0:
                    if c == 0:
                        re, im = jnp.where(hit, re, re * f), jnp.where(hit, 0.0, im * f)
                    else:
                        re, im = re * f, im * f
                elif part == 1:
                    if c == 0:
                        re, im = jnp.where(hit, im, re * f), jnp.where(hit, 0.0, im * f)
                    else:
                        re, im = re * f, im * f
                lanes = slice(128 * (c % 2), 128 * (c % 2) + 128)
                for dst, x in ((rows16(16 * n, 16), re), (rows16(128 + 16 * n, 16), im)):
                    h, l = halves(x)
                    bh[c // 2, dst, lanes] = h
                    bl[c // 2, dst, lanes] = l
            return 0

        lax.fori_loop(0, 8, fill, 0)
        for cp in range(4):
            big[cp] = mm(yi[0], bh[cp]) + mm(yi[1], bh[cp]) + mm(yi[0], bl[cp])

        def spread(t, _):
            v = []
            at = rows16(16 * t, 16)
            for c in range(8):
                lanes = slice(128 * (c % 2), 128 * (c % 2) + 128)
                y = (big[c // 2, at, lanes], big[c // 2, rows16(128 + 16 * t, 16), lanes])
                v.append(y if c == 0 else turn(y, tyc[c, at, :], tys[c, at, :], 1))
            v = dft8(v, 1)
            for b in range(8):
                to = rows16(128 * (b % 2) + 16 * t, 16)
                if part == 1:
                    big2[b // 2, to, 128:256] = v[b][0]
                else:
                    big2[b // 2, to, 0:128] = v[b][0]
                    big2[b // 2, to, 128:256] = v[b][1]
            return 0

        lax.fori_loop(0, 8, spread, 0)

    for s in range(SLOTS):
        recv_all(narrow_copy, NARROW, me_n, m_args, s)
        second_back(s, 0 if s == 0 else None)
        if s == 0:
            @pl.when(special)
            def _():
                second_back(0, 1)

        def read_back(w):
            b = w // 4
            at = rows((b % 2) * 128 + (w % 4) * 32, 32)
            return big2[b // 2, at, 0:128], big2[b // 2, at, 128:256]

        def code_back(w, _, s=s):
            code_wide(read_back, us, s, w, w)
            return 0

        lax.fori_loop(0, WIDE, code_back, 0)
        keep = pltpu.make_async_copy(us.at[s, me_w], out.at[s, me_w], u_recv.at[s, me_w])
        keep.start()
        send_all(wide_copy, WIDE, me_w, u_args, s)

    for s in range(SLOTS):
        pltpu.make_async_copy(us.at[s, me_w], out.at[s, me_w], u_recv.at[s, me_w]).wait()
        recv_all(wide_copy, WIDE, me_w, u_args, s)
        sent_all(wide_copy, WIDE, me_w, w_args, s)
        sent_all(narrow_copy, NARROW, me_n, n_args, s)
        sent_all(narrow_copy, NARROW, me_n, m_args, s)
        sent_all(wide_copy, WIDE, me_w, u_args, s)
    v_main.wait_send()

    @pl.when(jnp.logical_not(alone))
    def _():
        v_side.wait_send()


def spectral(noise, spectrum):
    t = TABLES
    angle = 2 * np.pi * np.arange(8)[:, None] * np.arange(128)[None, :] / 1024
    tyc = jnp.broadcast_to(jnp.asarray(np.cos(angle), f32)[:, :, None], (8, 128, 128))
    tys = jnp.broadcast_to(jnp.asarray(np.sin(angle), f32)[:, :, None], (8, 128, 128))
    vmem = pl.BlockSpec(memory_space=pltpu.VMEM)
    dma = pltpu.SemaphoreType.DMA
    return pl.pallas_call(
        spectral_kernel,
        out_shape=jax.ShapeDtypeStruct((SLOTS, WIDE, 40, 128), i32),
        in_specs=[vmem] * 13,
        out_specs=pl.BlockSpec(memory_space=pl.ANY),
        scratch_shapes=[
            pltpu.VMEM((2048, 128), f32),
            pltpu.VMEM((2048, 128), f32),
            pltpu.VMEM((SLOTS, WIDE, 40, 128), i32),
            pltpu.VMEM((SLOTS, WIDE, 40, 128), i32),
            pltpu.VMEM((4, 256, 256), bf16),
            pltpu.VMEM((4, 256, 256), bf16),
            pltpu.VMEM((4, 256, 256), f32),
            pltpu.VMEM((4, 256, 256), f32),
            pltpu.VMEM((SLOTS, NARROW, 136, 128), i32),
            pltpu.VMEM((SLOTS, NARROW, 136, 128), i32),
            pltpu.VMEM((8, 144, 256), bf16),
            pltpu.VMEM((8, 144, 256), bf16),
            pltpu.VMEM((SLOTS, NARROW, 136, 128), i32),
            pltpu.VMEM((SLOTS, NARROW, 136, 128), i32),
            pltpu.VMEM((SLOTS, WIDE, 40, 128), i32),
            pltpu.VMEM((SLOTS, 8, 128, 128), f32),
            pltpu.VMEM((8, 16, 128), f32),
            pltpu.VMEM((8, 128, 128), i32),
            pltpu.VMEM((8, 128, 128), i32),
            pltpu.VMEM((8, 8, 128), i32),
            dma((SLOTS, WIDE)), dma((SLOTS, WIDE)),
            dma((SLOTS, NARROW)), dma((SLOTS, NARROW)),
            dma((SLOTS, NARROW)), dma((SLOTS, NARROW)),
            dma((SLOTS, WIDE)), dma((SLOTS, WIDE)),
            dma((2,)), dma((2,)),
        ],
        compiler_params=pltpu.CompilerParams(
            collective_id=0, has_side_effects=True, vmem_limit_bytes=56 * 1024 * 1024
        ),
    )(
        noise.reshape(4096, 128), spectrum.reshape(4096, 128), t["tz"], t["yf"], t["yi"],
        t["xf"], t["xi"], tyc, tys, t["tx"], t["own2"], t["mir"], t["flips"],
    )


def finish_kernel(
    cell_row, target, freq, tzi, depth_at, assay, weight, out,
    got, contrib, *accs,
):
    for acc in accs:
        acc[...] = jnp.zeros_like(acc)

    def depth(y, _):
        re, im = unpack(freq[pl.ds(y, 64, stride=40), :])
        d = decode_factor(freq[pl.ds(32 + lax.rem(y, 8), 64, stride=40), :])
        h, l = halves(jnp.concatenate([re * d, im * d], axis=0))
        u = jnp.concatenate([h, h, l], axis=0)
        out[pl.ds(y, 128, stride=32), :] = lax.dot_general(
            u, tzi[...], (((0,), (0,)), ((), ())), preferred_element_type=f32
        )
        return 0

    lax.fori_loop(0, 32, depth, 0)
    count = got.shape[0]

    def gather(g, _):
        for k in range(16):
            i = g * 16 + k
            got[pl.ds(i, 1), :] = out[pl.ds(cell_row[i], 1), :]
        return 0

    lax.fori_loop(0, count // 16, gather, 0)
    lane = lax.broadcasted_iota(i32, (128, 128), 1)

    def residual(g, _):
        at = rows16(g * 128, 128)
        value = jnp.sum(jnp.where(lane == depth_at[at, :], got[at, :], 0.0), axis=1, keepdims=True)
        resid = assay[at, :] - value
        for k in range(TARGETS):
            contrib[k, at, :] = resid * weight[at, 128 * k : 128 * k + 128].astype(f32)
        return 0

    lax.fori_loop(0, count // 128, residual, 0)

    def scatter(g, _):
        for k in range(4):
            i = g * 4 + k
            for t in range(TARGETS):
                acc = accs[t + TARGETS * (k % 2)]
                at = pl.ds(target[i * TARGETS + t], 1)
                acc[at, :] = acc[at, :] + contrib[t, pl.ds(i, 1), :]
        return 0

    lax.fori_loop(0, count // 4, scatter, 0)

    def combine(g, _):
        at = rows(g * 64, 64)
        v = out[at, :]
        for acc in accs:
            v = v + acc[at, :]
        out[at, :] = v
        return 0

    lax.fori_loop(0, 64, combine, 0)


def finish(freq, cell, target, assay, weight):
    vmem = pl.BlockSpec(memory_space=pltpu.VMEM)
    smem = pl.BlockSpec(memory_space=pltpu.SMEM)
    count = cell.shape[0]
    return pl.pallas_call(
        finish_kernel,
        out_shape=jax.ShapeDtypeStruct((4096, 128), f32),
        in_specs=[smem, smem] + [vmem] * 5,
        out_specs=vmem,
        scratch_shapes=[pltpu.VMEM((count, 128), f32), pltpu.VMEM((TARGETS, count, 128), f32)]
        + [pltpu.VMEM((4096, 128), f32)] * 8,
        compiler_params=pltpu.CompilerParams(vmem_limit_bytes=56 * 1024 * 1024),
    )(
        cell // NZ, target.reshape(-1), freq.reshape(-1, 128), TABLES["tzi"],
        (cell % NZ)[:, None], assay[:, None], weight,
    )


def deliver(assay, weights, owner, cell, pencils):
    count = owner.shape[0]
    capacity = max(4, 4 * count // (WIDE * NARROW))
    order = jnp.arange(count, dtype=i32)
    earlier = (order[None, :] < order[:, None]) & (owner[None, :] == owner[:, None])
    slot = owner * capacity + jnp.sum(earlier, axis=1, dtype=i32)
    total = WIDE * NARROW * capacity
    hot = jnp.arange(total, dtype=i32)[:, None] == slot[None, :]
    placed = jnp.dot(hot.astype(bf16), weights, preferred_element_type=bf16)
    fields = jnp.concatenate(
        [cell[None], pencils.T, jnp.zeros((3, count), i32)], axis=0
    ).astype(f32)
    numbers = lax.dot_general(
        fields, hot.astype(f32), (((1,), (1,)), ((), ())), precision=lax.Precision.HIGHEST
    )
    numbers = jnp.round(numbers).astype(i32)
    grade = jnp.sum(jnp.where(hot, assay.astype(f32)[None, :], 0.0), axis=1).astype(bf16)

    def both(x):
        x = lax.all_to_all(x, "wide", split_axis=0, concat_axis=0, tiled=True)
        return lax.all_to_all(x, "narrow", split_axis=1, concat_axis=1, tiled=True)

    placed = both(placed.reshape(WIDE, NARROW, capacity, TARGETS * NZ)).reshape(total, TARGETS * NZ)
    numbers = numbers.reshape(8, WIDE, NARROW, capacity).transpose(1, 2, 0, 3)
    numbers = both(numbers.reshape(WIDE, NARROW, 8 * capacity))
    numbers = numbers.reshape(WIDE * NARROW, 8, capacity).transpose(1, 0, 2).reshape(8, total)
    grade = both(grade.reshape(WIDE, NARROW, capacity)).reshape(total)
    return numbers[0], numbers[1 : 1 + TARGETS].T, grade.astype(f32), placed


def local(noise, spectrum, assay, measure_weights, measure_owner, measure_cell, measure_pencils):
    count = measure_owner.shape[1]
    cell, target, grade, placed = deliver(
        assay[0], measure_weights[0].reshape(count, TARGETS * NZ), measure_owner[0],
        measure_cell[0], measure_pencils[0],
    )
    freq = spectral(noise, spectrum)
    field = finish(freq, cell, target, grade, placed)
    return field.reshape(noise.shape)


def solution(mesh):
    placed = (
        P("narrow", "wide", None),
        P("wide", None, "narrow"),
        P(("wide", "narrow"), None),
        P(("wide", "narrow"), None, None, None),
        P(("wide", "narrow"), None),
        P(("wide", "narrow"), None),
        P(("wide", "narrow"), None, None),
    )
    return jax.shard_map(
        local, mesh=mesh, in_specs=placed, out_specs=P("narrow", "wide", None), check_vma=False
    )
```

```python
import math

import jax
import jax.numpy as jnp
import ml_dtypes
import numpy as np
from jax import lax
from jax.experimental import pallas as pl
from jax.experimental.pallas import tpu as pltpu
from jax.sharding import PartitionSpec as P

NX, NY, NZ = 1024, 1024, 128
TARGETS = 4
WIDE, NARROW = 32, 8
SLOTS = 2
MESH = pl.DeviceIdType.MESH
f32, bf16, i32 = jnp.float32, jnp.bfloat16, jnp.int32

LN2 = math.log(2.0)
CODE = 16.0 / LN2
PEAK = 32600.0
TINY = 1e-30
SPEC_LOW = math.log(0.1)
SPEC_CODE = 65000.0 / math.log(85.0)
ROOT_HALF = math.sqrt(0.5)


def split(a):
    high = a.astype(ml_dtypes.bfloat16)
    low = (a - high.astype(np.float64)).astype(ml_dtypes.bfloat16)
    return high, low


def pair_matrix(sign):
    index = np.arange(128)
    angle = 2 * np.pi * (index[:, None] * index[None, :] % 128) / 128
    c, s = np.cos(angle), sign * np.sin(angle)
    return np.block([[c, -s], [s, c]])


def depth_forward():
    kz = 2 * np.arange(32)[None, :] + np.arange(2)[:, None]
    kz = kz.reshape(-1)
    z = np.arange(128)
    angle = 2 * np.pi * (kz[:, None] * z[None, :] % 128) / 128
    re, im = np.cos(angle), -np.sin(angle)
    im[kz == 0] = np.cos(np.pi * z)
    return np.concatenate([re, im], 0)


def depth_inverse():
    kz = (2 * np.arange(32)[None, :] + np.arange(2)[:, None]).reshape(-1)
    z = np.arange(128)
    angle = 2 * np.pi * (kz[:, None] * z[None, :] % 128) / 128
    re, im = 2 * np.cos(angle), -2 * np.sin(angle)
    re[kz == 0] = 1.0
    im[kz == 0] = np.cos(np.pi * z)
    return np.concatenate([re, im], 0)


def make_tables():
    h, l = split(depth_forward())
    tz = np.concatenate([h, l, h], 1)
    h, l = split(depth_inverse())
    tzi = np.concatenate([h, l, h], 0)
    yf = np.stack(split(pair_matrix(-1.0)))
    yi = np.stack(split(pair_matrix(1.0)))
    xf = np.stack(split(pair_matrix(-1.0).T))
    xi = np.stack(split(pair_matrix(1.0).T))
    c = np.arange(8)
    a = np.arange(128)
    angle = 2 * np.pi * c[:, None] * a[None, :] / 1024
    tx = np.stack([np.cos(angle), np.sin(angle)]).astype(np.float32)
    row = np.arange(128)
    lane_of = 8 * (row % 16) + row // 16
    own = np.zeros((128, 128))
    own[row, lane_of] = 1
    mir = np.zeros((128, 128))
    mir[row, (128 - lane_of) % 128] = 1
    own2 = np.concatenate([own, own], 1).astype(ml_dtypes.bfloat16)
    flips = np.zeros((2, 128, 128))
    flips[0, (128 - row) % 128, row] = 1
    flips[1, 127 - row, row] = 1
    flips = np.concatenate([flips, flips], 1).astype(ml_dtypes.bfloat16)
    return dict(
        tz=tz, tzi=tzi, yf=yf, yi=yi, xf=xf, xi=xi, tx=tx, own2=own2,
        mir=mir.astype(ml_dtypes.bfloat16), flips=flips,
    )


TABLES = make_tables()
ROOM = 256


def join_matrix():
    m = np.zeros((8, 128))
    m[0, 1], m[0, 2] = 256, 1
    for k in range(TARGETS):
        m[1 + k, 4 + 2 * k], m[1 + k, 5 + 2 * k] = 256, 1
    return m.astype(ml_dtypes.bfloat16)


JOIN = join_matrix()


def halves(v):
    h = v.astype(bf16)
    return h, (v - h.astype(f32)).astype(bf16)


def times_i(v, sign):
    re, im = v
    return (-im, re) if sign > 0 else (im, -re)


def add(a, b):
    return a[0] + b[0], a[1] + b[1]


def sub(a, b):
    return a[0] - b[0], a[1] - b[1]


def dft4(v, sign):
    s, d = add(v[0], v[2]), sub(v[0], v[2])
    t, u = add(v[1], v[3]), times_i(sub(v[1], v[3]), sign)
    return [add(s, t), add(d, u), sub(s, t), sub(d, u)]


def dft8(v, sign):
    e = dft4(v[0::2], sign)
    o = dft4(v[1::2], sign)
    g = float(sign)
    re, im = o[1]
    o[1] = ((re - g * im) * ROOT_HALF, (im + g * re) * ROOT_HALF)
    o[2] = times_i(o[2], sign)
    re, im = o[3]
    o[3] = ((-re - g * im) * ROOT_HALF, (g * re - im) * ROOT_HALF)
    return [add(e[c], o[c]) for c in range(4)] + [sub(e[c], o[c]) for c in range(4)]


def turn(v, cos, sin, sign):
    re, im = v
    if sign < 0:
        return re * cos + im * sin, im * cos - re * sin
    return re * cos - im * sin, im * cos + re * sin


def scale_code(m):
    return jnp.ceil(jnp.log(jnp.maximum(m, TINY)) * CODE).astype(i32)


def encode_factor(code):
    return jnp.exp(code.astype(f32) * (-1.0 / CODE)) * PEAK


def decode_factor(code):
    return jnp.exp(code.astype(f32) * (1.0 / CODE)) * (1.0 / PEAK)


def pack(re, im):
    a = jnp.round(re).astype(i32)
    b = jnp.round(im).astype(i32)
    return (a << 16) | (b & 0xFFFF)


def unpack(word):
    return (word >> 16).astype(f32), ((word << 16) >> 16).astype(f32)


def tile_max(tiles):
    tiles = [jnp.abs(t) for t in tiles]
    while len(tiles) > 1:
        tiles = [jnp.maximum(a, b) for a, b in zip(tiles[0::2], tiles[1::2])] + (
            tiles[-1:] if len(tiles) % 2 else []
        )
    return tiles[0]


def mm(a, b):
    return jnp.dot(a, b, preferred_element_type=f32)


def mm_t(a, b):
    return lax.dot_general(a, b, (((1,), (1,)), ((), ())), preferred_element_type=f32)


def rows(start, size):
    return pl.ds(pl.multiple_of(start, 8), size)


def rows16(start, size):
    return pl.ds(pl.multiple_of(start, 16), size)


def spectral_kernel(
    noise, spec, tz, yf, yi, xf, xi, tyc, tys, tx, own2, mir, flips, place, parts, weights, join,
    out, got, numbers,
    zre, zim, ws, wr, bh, bl, big, big2, ns, nr, lh, ll, ms, mr, us,
    ear, bsp, vs, vr, vc, asend, arecv, psend, precv, bsend, brecv,
    w_send, w_recv, n_send, n_recv, m_send, m_recv, u_send, u_recv, v_send, v_recv,
    a_send, a_recv, p_send, p_recv, b_send, b_recv, g_sem,
):
    me_w = lax.axis_index("wide")
    me_n = lax.axis_index("narrow")
    special = me_w == 0
    edge = special & ((me_n == 0) | (me_n == 4))

    barrier = pltpu.get_barrier_semaphore()

    def greet_wide(i, _):
        pl.semaphore_signal(
            barrier, inc=1, device_id={"wide": lax.rem(me_w + i, WIDE)}, device_id_type=MESH
        )
        return 0

    def greet_narrow(i, _):
        pl.semaphore_signal(
            barrier, inc=1, device_id={"narrow": lax.rem(me_n + i, NARROW)}, device_id_type=MESH
        )
        return 0

    lax.fori_loop(1, WIDE, greet_wide, 0)
    lax.fori_loop(1, NARROW, greet_narrow, 0)

    def wide_copy(src, dst, sends, recvs, s, peer, slot):
        return pltpu.make_async_remote_copy(
            src_ref=src.at[s, peer], dst_ref=dst.at[s, slot], send_sem=sends.at[s, peer],
            recv_sem=recvs.at[s, slot], device_id={"wide": peer}, device_id_type=MESH,
        )

    def narrow_copy(src, dst, sends, recvs, s, peer, slot):
        return pltpu.make_async_remote_copy(
            src_ref=src.at[s, peer], dst_ref=dst.at[s, slot], send_sem=sends.at[s, peer],
            recv_sem=recvs.at[s, slot], device_id={"narrow": peer}, device_id_type=MESH,
        )

    def send_all(make, count, me, args, s):
        def one(i, _):
            make(*args, s, lax.rem(me + i, count), me).start()
            return 0

        lax.fori_loop(1, count, one, 0)

    def recv_all(make, count, me, args, s):
        def one(i, _):
            peer = lax.rem(me + i, count)
            make(*args, s, peer, peer).wait_recv()
            return 0

        lax.fori_loop(1, count, one, 0)

    def sent_all(make, count, me, args, s):
        def one(i, _):
            peer = lax.rem(me + i, count)
            make(*args, s, peer, peer).wait_send()
            return 0

        lax.fori_loop(1, count, one, 0)

    w_args = (ws, wr, w_send, w_recv)
    n_args = (ns, nr, n_send, n_recv)
    m_args = (ms, mr, m_send, m_recv)
    u_args = (us, out, u_send, u_recv)

    late = special & (me_n >= 4)
    own_slots = (jnp.where(late, 2, 0), 1)
    mir_slots = (jnp.where(special & (me_n < 4), 2, jnp.where(special, 0, 2)), 3)

    def spectrum_rows(slot, e):
        return halves(spec[pl.ds(slot * 1024 + e, 128, stride=8), :])

    for e in range(8):
        back = (8 - e) % 8
        flip = flips[0 if e == 0 else 1]
        codes = []
        for s in range(SLOTS):
            h, l = spectrum_rows(own_slots[s], e)
            ear[s, e] = mm_t(own2[...], jnp.concatenate([h, l], axis=1))
            h, l = spectrum_rows(mir_slots[s], back)
            gh = mm_t(mir[...], h).astype(bf16)
            gl = mm_t(mir[...], l).astype(bf16)
            v = mm(jnp.concatenate([gh, gl], axis=1), flip)
            q = jnp.round((jnp.log(v) - SPEC_LOW) * SPEC_CODE - 32500.0)
            codes.append(jnp.clip(q, -32767.0, 32767.0))
        vs[e] = pack(codes[0], codes[1])

    v_main = pltpu.make_async_remote_copy(
        src_ref=vs, dst_ref=vr, send_sem=v_send.at[0], recv_sem=v_recv.at[0],
        device_id={"narrow": 7 - me_n}, device_id_type=MESH,
    )
    v_side = pltpu.make_async_remote_copy(
        src_ref=vs.at[:, pl.ds(0, 8), :], dst_ref=vc, send_sem=v_send.at[1], recv_sem=v_recv.at[1],
        device_id={"narrow": lax.rem(8 - me_n, 8)}, device_id_type=MESH,
    )

    alone = (me_n == 0) | (me_n == 4)

    @pl.when(alone)
    def _():
        vc[...] = vs[:, 0:8, :]

    room = asend.shape[1]
    count = place.shape[1]
    room_row = lax.broadcasted_iota(i32, (room, count), 0)

    def pack_measures(n, _):
        hot = jnp.where(room_row + n * room == place[...], 1.0, 0.0).astype(bf16)
        asend[n] = mm(hot, weights[...]).astype(bf16)
        psend[n] = mm_t(parts[...], hot).astype(bf16)
        return 0

    lax.fori_loop(0, NARROW, pack_measures, 0)
    arecv[me_n] = asend[me_n]
    precv[me_n] = psend[me_n]

    def to_narrow(src, dst, sends, recvs, peer, slot):
        return pltpu.make_async_remote_copy(
            src_ref=src.at[peer], dst_ref=dst.at[slot], send_sem=sends.at[peer],
            recv_sem=recvs.at[slot], device_id={"narrow": peer}, device_id_type=MESH,
        )

    def to_wide(peer, slot):
        return pltpu.make_async_remote_copy(
            src_ref=bsend.at[peer], dst_ref=brecv.at[slot], send_sem=b_send.at[peer],
            recv_sem=b_recv.at[slot], device_id={"wide": peer}, device_id_type=MESH,
        )

    a_args = (asend, arecv, a_send, a_recv)
    p_args = (psend, precv, p_send, p_recv)

    def send_measures(i, _):
        peer = lax.rem(me_n + i, NARROW)
        to_narrow(*p_args, peer, me_n).start()
        to_narrow(*a_args, peer, me_n).start()
        return 0

    def recv_measures(i, _):
        peer = lax.rem(me_n + i, NARROW)
        to_narrow(*p_args, peer, peer).wait_recv()
        to_narrow(*a_args, peer, peer).wait_recv()
        return 0

    def sent_measures(i, _):
        peer = lax.rem(me_n + i, NARROW)
        to_narrow(*p_args, peer, peer).wait_send()
        to_narrow(*a_args, peer, peer).wait_send()
        return 0

    def send_groups(i, _):
        to_wide(lax.rem(me_w + i, WIDE), me_w).start()
        return 0

    def recv_groups(i, _):
        peer = lax.rem(me_w + i, WIDE)
        to_wide(peer, peer).wait_recv()
        return 0

    def sent_groups(i, _):
        peer = lax.rem(me_w + i, WIDE)
        to_wide(peer, peer).wait_send()
        return 0

    def depth(y, _):
        cells = [y * 4 + k for k in range(4)]
        pieces = []
        for k in cells:
            h, l = halves(noise[pl.ds(k, 128, stride=32), :])
            pieces.append(jnp.concatenate([h, h, l], axis=1))
        res = mm_t(tz[...], jnp.concatenate(pieces, axis=0))
        for i, k in enumerate(cells):
            zre[pl.ds(k, 64, stride=32), :] = res[:64, 128 * i : 128 * i + 128]
            zim[pl.ds(k, 64, stride=32), :] = res[64:, 128 * i : 128 * i + 128]
        return 0

    lax.fori_loop(0, 8, depth, 0)

    def code_wide(read, dst, s, w, to):
        re, im = read(w)
        m = tile_max([re[8 * t : 8 * t + 8] for t in range(4)] + [im[8 * t : 8 * t + 8] for t in range(4)])
        code = scale_code(m)
        fac = encode_factor(code)
        for t in range(4):
            sl = slice(8 * t, 8 * t + 8)
            dst[s, to, 8 * t : 8 * t + 8, :] = pack(re[sl] * fac, im[sl] * fac)
        dst[s, to, 32:40, :] = code

    for s in range(SLOTS):
        def read_depth(w, s=s):
            at = rows((s * 32 + w) * 32, 32)
            return zre[at, :], zim[at, :]

        def code_one(w, _, s=s, read=read_depth):
            code_wide(read, ws, s, w, w)
            return 0

        lax.fori_loop(0, WIDE, code_one, 0)
        wr[s, me_w] = ws[s, me_w]
        if s == 0:
            pl.semaphore_wait(barrier, WIDE - 1 + NARROW - 1)
        send_all(wide_copy, WIDE, me_w, w_args, s)
        if s == 0:
            v_main.start()

            @pl.when(jnp.logical_not(alone))
            def _():
                v_side.start()

            lax.fori_loop(1, NARROW, send_measures, 0)

    def second_forward(s, p, q, r):
        def group(g, _):
            dec = [decode_factor(wr[s, 4 * b + g, 32:40, :]) for b in range(8)]
            dec = [jnp.concatenate([d, d], axis=0) for d in dec]
            for t in range(2):
                v = []
                for b in range(8):
                    re, im = unpack(wr[s, 4 * b + g, 16 * t : 16 * t + 16, :])
                    re, im = re * dec[b], im * dec[b]
                    if p is not None:
                        re, im = re * p + im * q, im * r
                    v.append((re, im))
                v = dft8(v, -1)
                at = rows16(g * 32 + 16 * t, 16)
                at_im = rows16(128 + g * 32 + 16 * t, 16)
                for c in range(8):
                    w = v[c] if c == 0 else turn(v[c], tyc[c, at, :], tys[c, at, :], -1)
                    lanes = slice(128 * (c % 2), 128 * (c % 2) + 128)
                    for dst, part in ((at, w[0]), (at_im, w[1])):
                        h, l = halves(part)
                        bh[c // 2, dst, lanes] = h
                        bl[c // 2, dst, lanes] = l
            return 0

        lax.fori_loop(0, 4, group, 0)
        for cp in range(4):
            big[cp] = mm(yf[0], bh[cp]) + mm(yf[1], bh[cp]) + mm(yf[0], bl[cp])

    first_row = lax.broadcasted_iota(i32, (8, 128), 0) == 0

    def code_narrow(s, n):
        tiles = []
        for c in range(8):
            lanes = slice(128 * (c % 2), 128 * (c % 2) + 128)
            for t in range(2):
                tiles.append((
                    big[c // 2, rows(16 * n + 8 * t, 8), lanes],
                    big[c // 2, rows(128 + 16 * n + 8 * t, 8), lanes],
                ))
        code = scale_code(tile_max([x for pair in tiles for x in pair]))
        fac = encode_factor(code)
        for k, (re, im) in enumerate(tiles):
            ns[s, n, 8 * k : 8 * k + 8, :] = pack(re * fac, im * fac)
        ns[s, n, 128:136, :] = code

    for s in range(SLOTS):
        recv_all(wide_copy, WIDE, me_w, w_args, s)
        if s == 0:
            one = jnp.where(special, 0.0, 1.0)
            second_forward(s, 1.0, 0.0, one)

            @pl.when(special)
            def _():
                big2[...] = big[...]
                second_forward(0, 0.0, 1.0, 0.0)
                top = big[0, 0:8, 0:128]
                mid = big[0, 64:72, 0:128]
                big[:, 0:64, :] = big2[:, 0:64, :]
                big[:, 128:192, :] = big2[:, 128:192, :]
                big[0, 128:136, 0:128] = jnp.where(first_row, top, big[0, 128:136, 0:128])
                big[0, 192:200, 0:128] = jnp.where(first_row, mid, big[0, 192:200, 0:128])
                big[0, 64:72, 0:128] = jnp.where(first_row, big2[0, 64:72, 0:128], mid)
        else:
            second_forward(s, None, None, None)

        def code_n(n, _, s=s):
            code_narrow(s, n)
            return 0

        lax.fori_loop(0, NARROW, code_n, 0)
        nr[s, me_n] = ns[s, me_n]
        send_all(narrow_copy, NARROW, me_n, n_args, s)


    lax.fori_loop(1, NARROW, recv_measures, 0)
    row = lax.broadcasted_iota(i32, (512, room), 0)
    want = (((row >> 4) << 3) + (row & 7) + 1).astype(f32)
    for q in range(4):
        hot = []
        for k in range(2):
            key = precv[2 * q + k, 0:1, :].astype(f32)
            match = (((row >> 3) & 1) == k) & (want == key)
            hot.append(jnp.where(match, 1.0, 0.0).astype(bf16))
        hot = jnp.concatenate(hot, axis=1)
        held = jnp.concatenate([arecv[2 * q], arecv[2 * q + 1]], axis=0)
        names = jnp.concatenate([precv[2 * q], precv[2 * q + 1]], axis=1)
        moved = mm(hot, held).astype(bf16).reshape(WIDE, 16, 512)
        named = mm_t(hot, names)
        named = jnp.concatenate([named, jnp.zeros((512, 112), f32)], axis=1)
        bsend[:, 16 * q : 16 * q + 16, 0:512] = moved
        bsend[:, 16 * q : 16 * q + 16, 512:640] = named.astype(bf16).reshape(WIDE, 16, 128)
    brecv[me_w] = bsend[me_w]
    lax.fori_loop(1, WIDE, send_groups, 0)

    total = 1.0 / (NX * NY * NZ)
    v_main.wait_recv()

    @pl.when(jnp.logical_not(alone))
    def _():
        v_side.wait_recv()

    def decode_spectrum(q):
        return jnp.exp((q + 32500.0) * (1.0 / SPEC_CODE) + SPEC_LOW)

    bsp[...] = jnp.zeros_like(bsp)

    @pl.when(edge)
    def _():
        sigma = jnp.where(me_n == 0, 1.0, -1.0)
        xs, vv = [], []
        for e in range(8):
            xs.append(ear[0, e, 0:8, :])
            vv.append(decode_spectrum(unpack(vc[e])[0]))

        def even(list_of, e):
            h, l = halves(list_of[(8 - e) % 8])
            pair = jnp.concatenate([h, l], axis=1)
            flip = flips[0 if e == 0 else 1]
            return (mm(pair, flip) + list_of[e]) * 0.5

        for e in range(8):
            a, b = even(xs, e), even(vv, e)
            bsp[e, 0:8, :] = jnp.where(first_row, (a - b) * (0.5 * total) * sigma, 0.0)
            big2[0, 8 * e : 8 * e + 8, 0:128] = (a + b) * (0.5 * total)

    for e in range(8):
        m0, m1 = unpack(vr[e])
        s0, s1 = unpack(vc[e])
        for s, m, side in ((0, m0, s0), (1, m1, s1)):
            m, side = decode_spectrum(m), decode_spectrum(side)
            ear_e = ear[s, e]
            lead = jnp.where(first_row, side, m[0:8])
            ear[s, e, 8:128, :] = (ear_e[8:128] + m[8:128]) * (0.5 * total)
            ear[s, e, 0:8, :] = (ear_e[0:8] + lead) * (0.5 * total)

    @pl.when(edge)
    def _():
        for e in range(8):
            ear[0, e, 0:8, :] = jnp.where(
                first_row, big2[0, 8 * e : 8 * e + 8, 0:128], ear[0, e, 0:8, :]
            )

    def first_both(s):
        def decs(n):
            d = decode_factor(nr[s, n, 128:136, :])
            return jnp.concatenate([d, d], axis=0)

        for n in range(8):
            big2[0, 16 * n : 16 * n + 16, 0:128] = decs(n)

        def load(c):
            v = []
            for n in range(8):
                re, im = unpack(nr[s, n, rows16(16 * c, 16), :])
                d = big2[0, 16 * n : 16 * n + 16, 0:128]
                v.append((re * d, im * d))
            return v

        def put(v, at):
            v = dft8(v, -1)
            for e in range(8):
                w = v[e] if e == 0 else turn(v[e], tx[0, e : e + 1, :], tx[1, e : e + 1, :], -1)
                for lanes, part in ((slice(0, 128), w[0]), (slice(128, 256), w[1])):
                    h, l = halves(part)
                    lh[e, at, lanes] = h
                    ll[e, at, lanes] = l

        def block(c, _):
            put(load(c), rows16(16 * c, 16))
            return 0

        lax.fori_loop(0, 8, block, 0)
        if s == 0:
            put([(re, -im) for re, im in load(0)], slice(128, 144))
        count = 144 if s == 0 else 128
        for e in range(8):
            h, l = lh[e, 0:count, :], ll[e, 0:count, :]
            z = mm(h, xf[0]) + mm(h, xf[1]) + mm(l, xf[0])
            fil = jnp.concatenate([ear[s, e], ear[s, e]], axis=1)
            g = z[0:128] * fil
            if s == 0:
                extra = jnp.concatenate([bsp[e], bsp[e]], axis=1)
                g = jnp.concatenate([g[0:16] + z[128:144] * extra, g[16:128]], axis=0)
            h, l = halves(g)
            big[e // 2, 128 * (e % 2) : 128 * (e % 2) + 128, :] = (
                mm(h, xi[0]) + mm(h, xi[1]) + mm(l, xi[0])
            )

        def unblock(c, _):
            v = []
            for e in range(8):
                at = rows16(128 * (e % 2) + 16 * c, 16)
                y = (big[e // 2, at, 0:128], big[e // 2, at, 128:256])
                v.append(y if e == 0 else turn(y, tx[0, e : e + 1, :], tx[1, e : e + 1, :], 1))
            v = dft8(v, 1)
            for n in range(8):
                at = rows16(128 * (n % 2) + 16 * c, 16)
                big2[n // 2, at, 0:128] = v[n][0]
                big2[n // 2, at, 128:256] = v[n][1]
            return 0

        lax.fori_loop(0, 8, unblock, 0)
        for n in range(8):
            base = 128 * (n % 2)
            tiles = [
                (big2[n // 2, base + 8 * k : base + 8 * k + 8, 0:128],
                 big2[n // 2, base + 8 * k : base + 8 * k + 8, 128:256])
                for k in range(16)
            ]
            code = scale_code(tile_max([x for pair in tiles for x in pair]))
            fac = encode_factor(code)
            for k, (re, im) in enumerate(tiles):
                ms[s, n, 8 * k : 8 * k + 8, :] = pack(re * fac, im * fac)
            ms[s, n, 128:136, :] = code

    for s in range(SLOTS):
        recv_all(narrow_copy, NARROW, me_n, n_args, s)
        first_both(s)
        mr[s, me_n] = ms[s, me_n]
        send_all(narrow_copy, NARROW, me_n, m_args, s)

    row16 = lax.broadcasted_iota(i32, (16, 128), 0)

    def second_back(s, part):
        def fill(n, _):
            d = decode_factor(mr[s, n, 128:136, :])
            d = jnp.concatenate([d, d], axis=0)
            if part is not None:
                if part == 0:
                    f = jnp.where(special, jnp.where(n < 4, 2.0, 0.0), 1.0)
                else:
                    f = jnp.where(n < 4, 0.0, 2.0)
                hit = (row16 == 0) & (special & ((n == 0) | (n == 4)))
            for c in range(8):
                re, im = unpack(mr[s, n, 16 * c : 16 * c + 16, :])
                re, im = re * d, im * d
                if part == 0:
                    if c == 0:
                        re, im = jnp.where(hit, re, re * f), jnp.where(hit, 0.0, im * f)
                    else:
                        re, im = re * f, im * f
                elif part == 1:
                    if c == 0:
                        re, im = jnp.where(hit, im, re * f), jnp.where(hit, 0.0, im * f)
                    else:
                        re, im = re * f, im * f
                lanes = slice(128 * (c % 2), 128 * (c % 2) + 128)
                for dst, x in ((rows16(16 * n, 16), re), (rows16(128 + 16 * n, 16), im)):
                    h, l = halves(x)
                    bh[c // 2, dst, lanes] = h
                    bl[c // 2, dst, lanes] = l
            return 0

        lax.fori_loop(0, 8, fill, 0)
        for cp in range(4):
            big[cp] = mm(yi[0], bh[cp]) + mm(yi[1], bh[cp]) + mm(yi[0], bl[cp])

        def spread(t, _):
            v = []
            at = rows16(16 * t, 16)
            for c in range(8):
                lanes = slice(128 * (c % 2), 128 * (c % 2) + 128)
                y = (big[c // 2, at, lanes], big[c // 2, rows16(128 + 16 * t, 16), lanes])
                v.append(y if c == 0 else turn(y, tyc[c, at, :], tys[c, at, :], 1))
            v = dft8(v, 1)
            for b in range(8):
                to = rows16(128 * (b % 2) + 16 * t, 16)
                if part == 1:
                    big2[b // 2, to, 128:256] = v[b][0]
                else:
                    big2[b // 2, to, 0:128] = v[b][0]
                    big2[b // 2, to, 128:256] = v[b][1]
            return 0

        lax.fori_loop(0, 8, spread, 0)

    for s in range(SLOTS):
        recv_all(narrow_copy, NARROW, me_n, m_args, s)
        second_back(s, 0 if s == 0 else None)
        if s == 0:
            @pl.when(special)
            def _():
                second_back(0, 1)

        def read_back(w):
            b = w // 4
            at = rows((b % 2) * 128 + (w % 4) * 32, 32)
            return big2[b // 2, at, 0:128], big2[b // 2, at, 128:256]

        def code_back(w, _, s=s):
            code_wide(read_back, us, s, w, w)
            return 0

        lax.fori_loop(0, WIDE, code_back, 0)
        keep = pltpu.make_async_copy(us.at[s, me_w], out.at[s, me_w], u_recv.at[s, me_w])
        keep.start()
        send_all(wide_copy, WIDE, me_w, u_args, s)

    lax.fori_loop(1, WIDE, recv_groups, 0)
    pltpu.make_async_copy(brecv, got, g_sem.at[0]).start()
    for g in range(16):
        named = jnp.concatenate(
            [brecv[2 * g, :, 512:640], brecv[2 * g + 1, :, 512:640]], axis=0
        )
        numbers[g] = jnp.round(mm_t(join[...], named)).astype(i32)
    lax.fori_loop(1, WIDE, sent_groups, 0)
    lax.fori_loop(1, NARROW, sent_measures, 0)
    pltpu.make_async_copy(brecv, got, g_sem.at[0]).wait()

    for s in range(SLOTS):
        pltpu.make_async_copy(us.at[s, me_w], out.at[s, me_w], u_recv.at[s, me_w]).wait()
        recv_all(wide_copy, WIDE, me_w, u_args, s)
        sent_all(wide_copy, WIDE, me_w, w_args, s)
        sent_all(narrow_copy, NARROW, me_n, n_args, s)
        sent_all(narrow_copy, NARROW, me_n, m_args, s)
        sent_all(wide_copy, WIDE, me_w, u_args, s)
    v_main.wait_send()

    @pl.when(jnp.logical_not(alone))
    def _():
        v_side.wait_send()


def spectral(noise, spectrum, place, parts, weights):
    t = TABLES
    angle = 2 * np.pi * np.arange(8)[:, None] * np.arange(128)[None, :] / 1024
    tyc = jnp.broadcast_to(jnp.asarray(np.cos(angle), f32)[:, :, None], (8, 128, 128))
    tys = jnp.broadcast_to(jnp.asarray(np.sin(angle), f32)[:, :, None], (8, 128, 128))
    vmem = pl.BlockSpec(memory_space=pltpu.VMEM)
    dma = pltpu.SemaphoreType.DMA
    return pl.pallas_call(
        spectral_kernel,
        out_shape=(
            jax.ShapeDtypeStruct((SLOTS, WIDE, 40, 128), i32),
            jax.ShapeDtypeStruct((WIDE, 64, 640), bf16),
            jax.ShapeDtypeStruct((16, 8, 128), i32),
        ),
        in_specs=[vmem] * 17,
        out_specs=(pl.BlockSpec(memory_space=pl.ANY), pl.BlockSpec(memory_space=pl.ANY), vmem),
        scratch_shapes=[
            pltpu.VMEM((2048, 128), f32),
            pltpu.VMEM((2048, 128), f32),
            pltpu.VMEM((SLOTS, WIDE, 40, 128), i32),
            pltpu.VMEM((SLOTS, WIDE, 40, 128), i32),
            pltpu.VMEM((4, 256, 256), bf16),
            pltpu.VMEM((4, 256, 256), bf16),
            pltpu.VMEM((4, 256, 256), f32),
            pltpu.VMEM((4, 256, 256), f32),
            pltpu.VMEM((SLOTS, NARROW, 136, 128), i32),
            pltpu.VMEM((SLOTS, NARROW, 136, 128), i32),
            pltpu.VMEM((8, 144, 256), bf16),
            pltpu.VMEM((8, 144, 256), bf16),
            pltpu.VMEM((SLOTS, NARROW, 136, 128), i32),
            pltpu.VMEM((SLOTS, NARROW, 136, 128), i32),
            pltpu.VMEM((SLOTS, WIDE, 40, 128), i32),
            pltpu.VMEM((SLOTS, 8, 128, 128), f32),
            pltpu.VMEM((8, 16, 128), f32),
            pltpu.VMEM((8, 128, 128), i32),
            pltpu.VMEM((8, 128, 128), i32),
            pltpu.VMEM((8, 8, 128), i32),
            pltpu.VMEM((NARROW, ROOM, 512), bf16),
            pltpu.VMEM((NARROW, ROOM, 512), bf16),
            pltpu.VMEM((NARROW, 16, ROOM), bf16),
            pltpu.VMEM((NARROW, 16, ROOM), bf16),
            pltpu.VMEM((WIDE, 64, 640), bf16),
            pltpu.VMEM((WIDE, 64, 640), bf16),
            dma((SLOTS, WIDE)), dma((SLOTS, WIDE)),
            dma((SLOTS, NARROW)), dma((SLOTS, NARROW)),
            dma((SLOTS, NARROW)), dma((SLOTS, NARROW)),
            dma((SLOTS, WIDE)), dma((SLOTS, WIDE)),
            dma((2,)), dma((2,)),
            dma((NARROW,)), dma((NARROW,)), dma((NARROW,)), dma((NARROW,)),
            dma((WIDE,)), dma((WIDE,)), dma((1,)),
        ],
        compiler_params=pltpu.CompilerParams(
            collective_id=0, has_side_effects=True, vmem_limit_bytes=56 * 1024 * 1024
        ),
    )(
        noise.reshape(4096, 128), spectrum.reshape(4096, 128), t["tz"], t["yf"], t["yi"],
        t["xf"], t["xi"], tyc, tys, t["tx"], t["own2"], t["mir"], t["flips"],
        place, parts, weights, JOIN,
    )


def finish_kernel(numbers, freq, tzi, held, out, gathered, contrib, *accs):
    for acc in accs:
        acc[...] = jnp.zeros_like(acc)

    def depth(g, _):
        for j in range(4):
            y = g * 4 + j
            re, im = unpack(freq[pl.ds(y, 64, stride=40), :])
            d = decode_factor(freq[pl.ds(32 + lax.rem(y, 8), 64, stride=40), :])
            h, l = halves(jnp.concatenate([re * d, im * d], axis=0))
            u = jnp.concatenate([h, h, l], axis=0)
            out[pl.ds(y, 128, stride=32), :] = lax.dot_general(
                u, tzi[...], (((0,), (0,)), ((), ())), preferred_element_type=f32
            )
        return 0

    lax.fori_loop(0, 8, depth, 0)
    groups = numbers.shape[0]

    def gather(g, _):
        for j in range(128):
            gathered[pl.ds(g * 128 + j, 1), :] = out[pl.ds(numbers[g, 0, j], 1), :]
        return 0

    lax.fori_loop(0, groups, gather, 0)
    lane = lax.broadcasted_iota(i32, (128, 128), 1)

    def residual(g, _):
        at = rows16(g * 128, 128)
        depth_at = held[at, 515:516].astype(i32)
        grade = held[at, 524:525].astype(f32)
        value = jnp.sum(jnp.where(lane == depth_at, gathered[at, :], 0.0), axis=1, keepdims=True)
        resid = grade - value
        for k in range(TARGETS):
            contrib[k, at, :] = resid * held[at, 128 * k : 128 * k + 128].astype(f32)
        return 0

    lax.fori_loop(0, groups, residual, 0)

    def scatter(g, _):
        for j in range(128):
            for t in range(TARGETS):
                acc = accs[t + TARGETS * (j % 2)]
                at = pl.ds(numbers[g, 1 + t, j], 1)
                acc[at, :] = acc[at, :] + contrib[t, pl.ds(g * 128 + j, 1), :]
        return 0

    lax.fori_loop(0, groups, scatter, 0)

    def combine(g, _):
        at = rows(g * 64, 64)
        v = out[at, :]
        for acc in accs:
            v = v + acc[at, :]
        out[at, :] = v
        return 0

    lax.fori_loop(0, 64, combine, 0)


def finish(freq, held, numbers):
    vmem = pl.BlockSpec(memory_space=pltpu.VMEM)
    smem = pl.BlockSpec(memory_space=pltpu.SMEM)
    count = held.shape[0] * held.shape[1]
    return pl.pallas_call(
        finish_kernel,
        out_shape=jax.ShapeDtypeStruct((4096, 128), f32),
        in_specs=[smem] + [vmem] * 3,
        out_specs=vmem,
        scratch_shapes=[pltpu.VMEM((count, 128), f32), pltpu.VMEM((TARGETS, count, 128), f32)]
        + [pltpu.VMEM((4096, 128), f32)] * 8,
        compiler_params=pltpu.CompilerParams(vmem_limit_bytes=56 * 1024 * 1024),
    )(numbers, freq.reshape(-1, 128), TABLES["tzi"], held.reshape(count, -1))


def describe(assay, owner, cell, pencils):
    count = owner.shape[0]
    order = jnp.arange(count, dtype=i32)
    earlier = order[:, None] < order[None, :]
    narrow = owner % NARROW
    rank = jnp.sum(earlier & (narrow[:, None] == narrow[None, :]), axis=0, dtype=i32)
    same = jnp.sum(earlier & (owner[:, None] == owner[None, :]), axis=0, dtype=i32)
    place = (narrow * ROOM + rank)[None]
    key = owner // NARROW * 8 + same + 1
    row = cell // NZ
    fields = [key, row // 256, row % 256, cell % NZ]
    for k in range(TARGETS):
        fields += [pencils[:, k] // 256, pencils[:, k] % 256]
    fields = [x.astype(bf16) for x in fields] + [assay] + [jnp.zeros((count,), bf16)] * 3
    return place, jnp.stack(fields)


def local(noise, spectrum, assay, measure_weights, measure_owner, measure_cell, measure_pencils):
    count = measure_owner.shape[1]
    place, parts = describe(assay[0], measure_owner[0], measure_cell[0], measure_pencils[0])
    weights = measure_weights[0].reshape(count, TARGETS * NZ)
    freq, held, numbers = spectral(noise, spectrum, place, parts, weights)
    return finish(freq, held, numbers).reshape(noise.shape)


def solution(mesh):
    placed = (
        P("narrow", "wide", None),
        P("wide", None, "narrow"),
        P(("wide", "narrow"), None),
        P(("wide", "narrow"), None, None, None),
        P(("wide", "narrow"), None),
        P(("wide", "narrow"), None),
        P(("wide", "narrow"), None, None),
    )
    return jax.shard_map(
        local, mesh=mesh, in_specs=placed, out_specs=P("narrow", "wide", None), check_vma=False
    )
```

```python
import math

import jax
import jax.numpy as jnp
import ml_dtypes
import numpy as np
from jax import lax
from jax.experimental import pallas as pl
from jax.experimental.pallas import tpu as pltpu
from jax.sharding import PartitionSpec as P

NX, NY, NZ = 1024, 1024, 128
TARGETS = 4
WIDE, NARROW = 32, 8
SLOTS = 2
MESH = pl.DeviceIdType.MESH
f32, bf16, i32 = jnp.float32, jnp.bfloat16, jnp.int32

LN2 = math.log(2.0)
CODE = 16.0 / LN2
PEAK = 32600.0
TINY = 1e-30
SPEC_LOW = math.log(0.1)
SPEC_CODE = 65000.0 / math.log(85.0)
ROOT_HALF = math.sqrt(0.5)


def split(a):
    high = a.astype(ml_dtypes.bfloat16)
    low = (a - high.astype(np.float64)).astype(ml_dtypes.bfloat16)
    return high, low


def pair_matrix(sign):
    index = np.arange(128)
    angle = 2 * np.pi * (index[:, None] * index[None, :] % 128) / 128
    c, s = np.cos(angle), sign * np.sin(angle)
    return np.block([[c, -s], [s, c]])


def depth_forward():
    kz = 2 * np.arange(32)[None, :] + np.arange(2)[:, None]
    kz = kz.reshape(-1)
    z = np.arange(128)
    angle = 2 * np.pi * (kz[:, None] * z[None, :] % 128) / 128
    re, im = np.cos(angle), -np.sin(angle)
    im[kz == 0] = np.cos(np.pi * z)
    return np.concatenate([re, im], 0)


def depth_inverse():
    kz = (2 * np.arange(32)[None, :] + np.arange(2)[:, None]).reshape(-1)
    z = np.arange(128)
    angle = 2 * np.pi * (kz[:, None] * z[None, :] % 128) / 128
    re, im = 2 * np.cos(angle), -2 * np.sin(angle)
    re[kz == 0] = 1.0
    im[kz == 0] = np.cos(np.pi * z)
    return np.concatenate([re, im], 0)


def make_tables():
    h, l = split(depth_forward())
    tz = np.concatenate([h, l, h], 1)
    h, l = split(depth_inverse())
    tzi = np.concatenate([h, l, h], 0)
    yf = np.stack(split(pair_matrix(-1.0)))
    yi = np.stack(split(pair_matrix(1.0)))
    xf = np.stack(split(pair_matrix(-1.0).T))
    xi = np.stack(split(pair_matrix(1.0).T))
    c = np.arange(8)
    a = np.arange(128)
    angle = 2 * np.pi * c[:, None] * a[None, :] / 1024
    tx = np.stack([np.cos(angle), np.sin(angle)]).astype(np.float32)
    row = np.arange(128)
    lane_of = 8 * (row % 16) + row // 16
    own = np.zeros((128, 128))
    own[row, lane_of] = 1
    mir = np.zeros((128, 128))
    mir[row, (128 - lane_of) % 128] = 1
    own2 = np.concatenate([own, own], 1).astype(ml_dtypes.bfloat16)
    flips = np.zeros((2, 128, 128))
    flips[0, (128 - row) % 128, row] = 1
    flips[1, 127 - row, row] = 1
    flips = np.concatenate([flips, flips], 1).astype(ml_dtypes.bfloat16)
    return dict(
        tz=tz, tzi=tzi, yf=yf, yi=yi, xf=xf, xi=xi, tx=tx, own2=own2,
        mir=mir.astype(ml_dtypes.bfloat16), flips=flips,
    )


TABLES = make_tables()
ROOM = 160


def join_matrix():
    m = np.zeros((8, 128))
    m[0, 1], m[0, 2] = 256, 1
    for k in range(TARGETS):
        m[1 + k, 4 + 2 * k], m[1 + k, 5 + 2 * k] = 256, 1
    m[5, 13] = 1
    return m.astype(ml_dtypes.bfloat16)


JOIN = join_matrix()


def halves(v):
    h = v.astype(bf16)
    return h, (v - h.astype(f32)).astype(bf16)


def times_i(v, sign):
    re, im = v
    return (-im, re) if sign > 0 else (im, -re)


def add(a, b):
    return a[0] + b[0], a[1] + b[1]


def sub(a, b):
    return a[0] - b[0], a[1] - b[1]


def dft4(v, sign):
    s, d = add(v[0], v[2]), sub(v[0], v[2])
    t, u = add(v[1], v[3]), times_i(sub(v[1], v[3]), sign)
    return [add(s, t), add(d, u), sub(s, t), sub(d, u)]


def dft8(v, sign):
    e = dft4(v[0::2], sign)
    o = dft4(v[1::2], sign)
    g = float(sign)
    re, im = o[1]
    o[1] = ((re - g * im) * ROOT_HALF, (im + g * re) * ROOT_HALF)
    o[2] = times_i(o[2], sign)
    re, im = o[3]
    o[3] = ((-re - g * im) * ROOT_HALF, (g * re - im) * ROOT_HALF)
    return [add(e[c], o[c]) for c in range(4)] + [sub(e[c], o[c]) for c in range(4)]


def turn(v, cos, sin, sign):
    re, im = v
    if sign < 0:
        return re * cos + im * sin, im * cos - re * sin
    return re * cos - im * sin, im * cos + re * sin


def scale_code(m):
    return jnp.ceil(jnp.log(jnp.maximum(m, TINY)) * CODE).astype(i32)


def encode_factor(code):
    return jnp.exp(code.astype(f32) * (-1.0 / CODE)) * PEAK


def decode_factor(code):
    return jnp.exp(code.astype(f32) * (1.0 / CODE)) * (1.0 / PEAK)


def pack(re, im):
    a = jnp.round(re).astype(i32)
    b = jnp.round(im).astype(i32)
    return (a << 16) | (b & 0xFFFF)


def unpack(word):
    return (word >> 16).astype(f32), ((word << 16) >> 16).astype(f32)


def tile_max(tiles):
    tiles = [jnp.abs(t) for t in tiles]
    while len(tiles) > 1:
        tiles = [jnp.maximum(a, b) for a, b in zip(tiles[0::2], tiles[1::2])] + (
            tiles[-1:] if len(tiles) % 2 else []
        )
    return tiles[0]


def mm(a, b):
    return jnp.dot(a, b, preferred_element_type=f32)


def mm_t(a, b):
    return lax.dot_general(a, b, (((1,), (1,)), ((), ())), preferred_element_type=f32)


def rows(start, size):
    return pl.ds(pl.multiple_of(start, 8), size)


def rows16(start, size):
    return pl.ds(pl.multiple_of(start, 16), size)


def spectral_kernel(
    noise, spec, tz, yf, yi, xf, xi, tyc, tys, tx, own2, mir, flips, owner, cell, assay, pencils, loads, join,
    out, got, numbers, flag,
    zre, zim, ws, wr, bh, bl, big, big2, ns, nr, lh, ll, ms, mr, us,
    ear, bsp, vs, vr, vc, wf, weights, parts, asend, arecv, psend, precv, bsend, brecv,
    w_send, w_recv, n_send, n_recv, m_send, m_recv, u_send, u_recv, v_send, v_recv,
    a_send, a_recv, p_send, p_recv, b_send, b_recv, g_sem,
):
    me_w = lax.axis_index("wide")
    me_n = lax.axis_index("narrow")
    special = me_w == 0
    edge = special & ((me_n == 0) | (me_n == 4))

    barrier = pltpu.get_barrier_semaphore()

    def greet_wide(i, _):
        pl.semaphore_signal(
            barrier, inc=1, device_id={"wide": lax.rem(me_w + i, WIDE)}, device_id_type=MESH
        )
        return 0

    def greet_narrow(i, _):
        pl.semaphore_signal(
            barrier, inc=1, device_id={"narrow": lax.rem(me_n + i, NARROW)}, device_id_type=MESH
        )
        return 0

    lax.fori_loop(1, WIDE, greet_wide, 0)
    lax.fori_loop(1, NARROW, greet_narrow, 0)

    def wide_copy(src, dst, sends, recvs, s, peer, slot):
        return pltpu.make_async_remote_copy(
            src_ref=src.at[s, peer], dst_ref=dst.at[s, slot], send_sem=sends.at[s, peer],
            recv_sem=recvs.at[s, slot], device_id={"wide": peer}, device_id_type=MESH,
        )

    def narrow_copy(src, dst, sends, recvs, s, peer, slot):
        return pltpu.make_async_remote_copy(
            src_ref=src.at[s, peer], dst_ref=dst.at[s, slot], send_sem=sends.at[s, peer],
            recv_sem=recvs.at[s, slot], device_id={"narrow": peer}, device_id_type=MESH,
        )

    def send_all(make, count, me, args, s):
        def one(i, _):
            make(*args, s, lax.rem(me + i, count), me).start()
            return 0

        lax.fori_loop(1, count, one, 0)

    def recv_all(make, count, me, args, s):
        def one(i, _):
            peer = lax.rem(me + i, count)
            make(*args, s, peer, peer).wait_recv()
            return 0

        lax.fori_loop(1, count, one, 0)

    def sent_all(make, count, me, args, s):
        def one(i, _):
            peer = lax.rem(me + i, count)
            make(*args, s, peer, peer).wait_send()
            return 0

        lax.fori_loop(1, count, one, 0)

    w_args = (ws, wr, w_send, w_recv)
    n_args = (ns, nr, n_send, n_recv)
    m_args = (ms, mr, m_send, m_recv)
    u_args = (us, out, u_send, u_recv)

    late = special & (me_n >= 4)
    own_slots = (jnp.where(late, 2, 0), 1)
    mir_slots = (jnp.where(special & (me_n < 4), 2, jnp.where(special, 0, 2)), 3)

    def spectrum_rows(slot, e):
        return halves(spec[pl.ds(slot * 1024 + e, 128, stride=8), :])

    for e in range(8):
        back = (8 - e) % 8
        flip = flips[0 if e == 0 else 1]
        codes = []
        for s in range(SLOTS):
            h, l = spectrum_rows(own_slots[s], e)
            ear[s, e] = mm_t(own2[...], jnp.concatenate([h, l], axis=1))
            h, l = spectrum_rows(mir_slots[s], back)
            gh = mm_t(mir[...], h).astype(bf16)
            gl = mm_t(mir[...], l).astype(bf16)
            v = mm(jnp.concatenate([gh, gl], axis=1), flip)
            q = jnp.round((jnp.log(v) - SPEC_LOW) * SPEC_CODE - 32500.0)
            codes.append(jnp.clip(q, -32767.0, 32767.0))
        vs[e] = pack(codes[0], codes[1])

    v_main = pltpu.make_async_remote_copy(
        src_ref=vs, dst_ref=vr, send_sem=v_send.at[0], recv_sem=v_recv.at[0],
        device_id={"narrow": 7 - me_n}, device_id_type=MESH,
    )
    v_side = pltpu.make_async_remote_copy(
        src_ref=vs.at[:, pl.ds(0, 8), :], dst_ref=vc, send_sem=v_send.at[1], recv_sem=v_recv.at[1],
        device_id={"narrow": lax.rem(8 - me_n, 8)}, device_id_type=MESH,
    )

    alone = (me_n == 0) | (me_n == 4)

    @pl.when(alone)
    def _():
        vc[...] = vs[:, 0:8, :]

    room = asend.shape[1]
    count = owner.shape[1]
    owners = owner[...]
    cells = cell[...]
    narrow_of = (owners & 7).astype(f32)
    diagonal = lax.broadcasted_iota(i32, (128, 128), 0) == lax.broadcasted_iota(i32, (128, 128), 1)

    def column(line):
        pieces = []
        for k in range(count // 128):
            piece = jnp.broadcast_to(line[:, 128 * k : 128 * k + 128], (128, 128))
            pieces.append(jnp.sum(jnp.where(diagonal, piece, 0.0), axis=1, keepdims=True))
        return jnp.concatenate(pieces, axis=0)

    earlier = lax.broadcasted_iota(i32, (count, count), 0) < lax.broadcasted_iota(i32, (count, count), 1)

    def before(line):
        match = earlier & (column(line) == line)
        return jnp.sum(jnp.where(match, 1.0, 0.0), axis=0, keepdims=True)

    same = before(owners.astype(f32))
    rank = before(narrow_of)
    place = jnp.where(rank < room, narrow_of * room + rank, -1.0).astype(i32)
    over = jnp.max(jnp.where(rank < room, 0.0, 1.0), axis=1, keepdims=True)
    key = (owners >> 3 << 3).astype(f32) + same + 1.0
    part_row = lax.broadcasted_iota(i32, (16, count), 0)
    listed = jnp.zeros((16, count), f32)
    for r, line in (
        (0, key),
        (1, (cells >> 15).astype(f32)),
        (2, ((cells >> 7) & 255).astype(f32)),
        (3, (cells & 127).astype(f32)),
        (12, assay[...].astype(f32)),
        *((4 + 2 * k, (pencils[k : k + 1, :] >> 8).astype(f32)) for k in range(TARGETS)),
        *((5 + 2 * k, (pencils[k : k + 1, :] & 255).astype(f32)) for k in range(TARGETS)),
    ):
        listed = jnp.where(part_row == r, line, listed)
    parts[...] = listed.astype(bf16)
    wf[...] = loads[...].astype(f32)
    for k in range(TARGETS):
        weights[:, 128 * k : 128 * k + 128] = wf[pl.ds(k, count, stride=TARGETS), :].astype(bf16)
    room_row = lax.broadcasted_iota(i32, (room, count), 0)
    flag_row = lax.broadcasted_iota(i32, (16, room), 0) == 13

    def pack_measures(n, _):
        hot = jnp.where(room_row + n * room == place, 1.0, 0.0).astype(bf16)
        asend[n] = mm(hot, weights[...]).astype(bf16)
        psend[n] = jnp.where(flag_row, over, mm_t(parts[...], hot)).astype(bf16)
        return 0

    lax.fori_loop(0, NARROW, pack_measures, 0)
    arecv[me_n] = asend[me_n]
    precv[me_n] = psend[me_n]

    def to_narrow(src, dst, sends, recvs, peer, slot):
        return pltpu.make_async_remote_copy(
            src_ref=src.at[peer], dst_ref=dst.at[slot], send_sem=sends.at[peer],
            recv_sem=recvs.at[slot], device_id={"narrow": peer}, device_id_type=MESH,
        )

    def to_wide(peer, slot):
        return pltpu.make_async_remote_copy(
            src_ref=bsend.at[peer], dst_ref=brecv.at[slot], send_sem=b_send.at[peer],
            recv_sem=b_recv.at[slot], device_id={"wide": peer}, device_id_type=MESH,
        )

    a_args = (asend, arecv, a_send, a_recv)
    p_args = (psend, precv, p_send, p_recv)

    def send_measures(i, _):
        peer = lax.rem(me_n + i, NARROW)
        to_narrow(*p_args, peer, me_n).start()
        to_narrow(*a_args, peer, me_n).start()
        return 0

    def recv_measures(i, _):
        peer = lax.rem(me_n + i, NARROW)
        to_narrow(*p_args, peer, peer).wait_recv()
        to_narrow(*a_args, peer, peer).wait_recv()
        return 0

    def sent_measures(i, _):
        peer = lax.rem(me_n + i, NARROW)
        to_narrow(*p_args, peer, peer).wait_send()
        to_narrow(*a_args, peer, peer).wait_send()
        return 0

    def send_groups(i, _):
        to_wide(lax.rem(me_w + i, WIDE), me_w).start()
        return 0

    def recv_groups(i, _):
        peer = lax.rem(me_w + i, WIDE)
        to_wide(peer, peer).wait_recv()
        return 0

    def sent_groups(i, _):
        peer = lax.rem(me_w + i, WIDE)
        to_wide(peer, peer).wait_send()
        return 0

    pl.semaphore_wait(barrier, WIDE - 1 + NARROW - 1)
    lax.fori_loop(1, NARROW, send_measures, 0)
    v_main.start()

    @pl.when(jnp.logical_not(alone))
    def _():
        v_side.start()

    def depth(y, _):
        cells = [y * 4 + k for k in range(4)]
        pieces = []
        for k in cells:
            h, l = halves(noise[pl.ds(k, 128, stride=32), :])
            pieces.append(jnp.concatenate([h, h, l], axis=1))
        res = mm_t(tz[...], jnp.concatenate(pieces, axis=0))
        for i, k in enumerate(cells):
            zre[pl.ds(k, 64, stride=32), :] = res[:64, 128 * i : 128 * i + 128]
            zim[pl.ds(k, 64, stride=32), :] = res[64:, 128 * i : 128 * i + 128]
        return 0

    lax.fori_loop(0, 8, depth, 0)

    def code_wide(read, dst, s, w, to):
        re, im = read(w)
        m = tile_max([re[8 * t : 8 * t + 8] for t in range(4)] + [im[8 * t : 8 * t + 8] for t in range(4)])
        code = scale_code(m)
        fac = encode_factor(code)
        for t in range(4):
            sl = slice(8 * t, 8 * t + 8)
            dst[s, to, 8 * t : 8 * t + 8, :] = pack(re[sl] * fac, im[sl] * fac)
        dst[s, to, 32:40, :] = code

    for s in range(SLOTS):
        def read_depth(w, s=s):
            at = rows((s * 32 + w) * 32, 32)
            return zre[at, :], zim[at, :]

        def code_one(w, _, s=s, read=read_depth):
            code_wide(read, ws, s, w, w)
            return 0

        lax.fori_loop(0, WIDE, code_one, 0)
        wr[s, me_w] = ws[s, me_w]
        send_all(wide_copy, WIDE, me_w, w_args, s)

    def second_forward(s, p, q, r):
        def group(g, _):
            dec = [decode_factor(wr[s, 4 * b + g, 32:40, :]) for b in range(8)]
            dec = [jnp.concatenate([d, d], axis=0) for d in dec]
            for t in range(2):
                v = []
                for b in range(8):
                    re, im = unpack(wr[s, 4 * b + g, 16 * t : 16 * t + 16, :])
                    re, im = re * dec[b], im * dec[b]
                    if p is not None:
                        re, im = re * p + im * q, im * r
                    v.append((re, im))
                v = dft8(v, -1)
                at = rows16(g * 32 + 16 * t, 16)
                at_im = rows16(128 + g * 32 + 16 * t, 16)
                for c in range(8):
                    w = v[c] if c == 0 else turn(v[c], tyc[c, at, :], tys[c, at, :], -1)
                    lanes = slice(128 * (c % 2), 128 * (c % 2) + 128)
                    for dst, part in ((at, w[0]), (at_im, w[1])):
                        h, l = halves(part)
                        bh[c // 2, dst, lanes] = h
                        bl[c // 2, dst, lanes] = l
            return 0

        lax.fori_loop(0, 4, group, 0)
        for cp in range(4):
            big[cp] = mm(yf[0], bh[cp]) + mm(yf[1], bh[cp]) + mm(yf[0], bl[cp])

    first_row = lax.broadcasted_iota(i32, (8, 128), 0) == 0

    def code_narrow(s, n):
        tiles = []
        for c in range(8):
            lanes = slice(128 * (c % 2), 128 * (c % 2) + 128)
            for t in range(2):
                tiles.append((
                    big[c // 2, rows(16 * n + 8 * t, 8), lanes],
                    big[c // 2, rows(128 + 16 * n + 8 * t, 8), lanes],
                ))
        code = scale_code(tile_max([x for pair in tiles for x in pair]))
        fac = encode_factor(code)
        for k, (re, im) in enumerate(tiles):
            ns[s, n, 8 * k : 8 * k + 8, :] = pack(re * fac, im * fac)
        ns[s, n, 128:136, :] = code

    for s in range(SLOTS):
        recv_all(wide_copy, WIDE, me_w, w_args, s)
        if s == 0:
            one = jnp.where(special, 0.0, 1.0)
            second_forward(s, 1.0, 0.0, one)

            @pl.when(special)
            def _():
                big2[...] = big[...]
                second_forward(0, 0.0, 1.0, 0.0)
                top = big[0, 0:8, 0:128]
                mid = big[0, 64:72, 0:128]
                big[:, 0:64, :] = big2[:, 0:64, :]
                big[:, 128:192, :] = big2[:, 128:192, :]
                big[0, 128:136, 0:128] = jnp.where(first_row, top, big[0, 128:136, 0:128])
                big[0, 192:200, 0:128] = jnp.where(first_row, mid, big[0, 192:200, 0:128])
                big[0, 64:72, 0:128] = jnp.where(first_row, big2[0, 64:72, 0:128], mid)
        else:
            second_forward(s, None, None, None)

        def code_n(n, _, s=s):
            code_narrow(s, n)
            return 0

        lax.fori_loop(0, NARROW, code_n, 0)
        nr[s, me_n] = ns[s, me_n]
        send_all(narrow_copy, NARROW, me_n, n_args, s)


    lax.fori_loop(1, NARROW, recv_measures, 0)
    row = lax.broadcasted_iota(i32, (512, room), 0)
    want = (((row >> 4) << 3) + (row & 7) + 1).astype(f32)
    flags = precv[0].astype(f32)
    for k in range(1, NARROW):
        flags = jnp.maximum(flags, precv[k].astype(f32))
    flags = jnp.max(jnp.where(flag_row, flags, 0.0), axis=1, keepdims=True)
    flags = jnp.max(flags, axis=0, keepdims=True)
    flag_col = lax.broadcasted_iota(i32, (512, 128), 1) == 13
    for q in range(4):
        moved, named = 0.0, 0.0
        for k in range(2):
            key = precv[2 * q + k, 0:1, :].astype(f32)
            match = (((row >> 3) & 1) == k) & (want == key)
            hot = jnp.where(match, 1.0, 0.0).astype(bf16)
            moved = moved + mm(hot, arecv[2 * q + k])
            named = named + mm_t(hot, precv[2 * q + k])
        named = jnp.concatenate([named, jnp.zeros((512, 112), f32)], axis=1)
        named = jnp.where(flag_col, flags, named)
        bsend[:, 16 * q : 16 * q + 16, 0:512] = moved.astype(bf16).reshape(WIDE, 16, 512)
        bsend[:, 16 * q : 16 * q + 16, 512:640] = named.astype(bf16).reshape(WIDE, 16, 128)
    brecv[me_w] = bsend[me_w]
    lax.fori_loop(1, WIDE, send_groups, 0)

    total = 1.0 / (NX * NY * NZ)
    v_main.wait_recv()

    @pl.when(jnp.logical_not(alone))
    def _():
        v_side.wait_recv()

    def decode_spectrum(q):
        return jnp.exp((q + 32500.0) * (1.0 / SPEC_CODE) + SPEC_LOW)

    bsp[...] = jnp.zeros_like(bsp)

    @pl.when(edge)
    def _():
        sigma = jnp.where(me_n == 0, 1.0, -1.0)
        xs, vv = [], []
        for e in range(8):
            xs.append(ear[0, e, 0:8, :])
            vv.append(decode_spectrum(unpack(vc[e])[0]))

        def even(list_of, e):
            h, l = halves(list_of[(8 - e) % 8])
            pair = jnp.concatenate([h, l], axis=1)
            flip = flips[0 if e == 0 else 1]
            return (mm(pair, flip) + list_of[e]) * 0.5

        for e in range(8):
            a, b = even(xs, e), even(vv, e)
            bsp[e, 0:8, :] = jnp.where(first_row, (a - b) * (0.5 * total) * sigma, 0.0)
            big2[0, 8 * e : 8 * e + 8, 0:128] = (a + b) * (0.5 * total)

    for e in range(8):
        m0, m1 = unpack(vr[e])
        s0, s1 = unpack(vc[e])
        for s, m, side in ((0, m0, s0), (1, m1, s1)):
            m, side = decode_spectrum(m), decode_spectrum(side)
            ear_e = ear[s, e]
            lead = jnp.where(first_row, side, m[0:8])
            ear[s, e, 8:128, :] = (ear_e[8:128] + m[8:128]) * (0.5 * total)
            ear[s, e, 0:8, :] = (ear_e[0:8] + lead) * (0.5 * total)

    @pl.when(edge)
    def _():
        for e in range(8):
            ear[0, e, 0:8, :] = jnp.where(
                first_row, big2[0, 8 * e : 8 * e + 8, 0:128], ear[0, e, 0:8, :]
            )

    def first_both(s):
        def decs(n):
            d = decode_factor(nr[s, n, 128:136, :])
            return jnp.concatenate([d, d], axis=0)

        for n in range(8):
            big2[0, 16 * n : 16 * n + 16, 0:128] = decs(n)

        def load(c):
            v = []
            for n in range(8):
                re, im = unpack(nr[s, n, rows16(16 * c, 16), :])
                d = big2[0, 16 * n : 16 * n + 16, 0:128]
                v.append((re * d, im * d))
            return v

        def put(v, at):
            v = dft8(v, -1)
            for e in range(8):
                w = v[e] if e == 0 else turn(v[e], tx[0, e : e + 1, :], tx[1, e : e + 1, :], -1)
                for lanes, part in ((slice(0, 128), w[0]), (slice(128, 256), w[1])):
                    h, l = halves(part)
                    lh[e, at, lanes] = h
                    ll[e, at, lanes] = l

        def block(c, _):
            put(load(c), rows16(16 * c, 16))
            return 0

        lax.fori_loop(0, 8, block, 0)
        if s == 0:
            put([(re, -im) for re, im in load(0)], slice(128, 144))
        count = 144 if s == 0 else 128
        for e in range(8):
            h, l = lh[e, 0:count, :], ll[e, 0:count, :]
            z = mm(h, xf[0]) + mm(h, xf[1]) + mm(l, xf[0])
            fil = jnp.concatenate([ear[s, e], ear[s, e]], axis=1)
            g = z[0:128] * fil
            if s == 0:
                extra = jnp.concatenate([bsp[e], bsp[e]], axis=1)
                g = jnp.concatenate([g[0:16] + z[128:144] * extra, g[16:128]], axis=0)
            h, l = halves(g)
            big[e // 2, 128 * (e % 2) : 128 * (e % 2) + 128, :] = (
                mm(h, xi[0]) + mm(h, xi[1]) + mm(l, xi[0])
            )

        def unblock(c, _):
            v = []
            for e in range(8):
                at = rows16(128 * (e % 2) + 16 * c, 16)
                y = (big[e // 2, at, 0:128], big[e // 2, at, 128:256])
                v.append(y if e == 0 else turn(y, tx[0, e : e + 1, :], tx[1, e : e + 1, :], 1))
            v = dft8(v, 1)
            for n in range(8):
                at = rows16(128 * (n % 2) + 16 * c, 16)
                big2[n // 2, at, 0:128] = v[n][0]
                big2[n // 2, at, 128:256] = v[n][1]
            return 0

        lax.fori_loop(0, 8, unblock, 0)
        for n in range(8):
            base = 128 * (n % 2)
            tiles = [
                (big2[n // 2, base + 8 * k : base + 8 * k + 8, 0:128],
                 big2[n // 2, base + 8 * k : base + 8 * k + 8, 128:256])
                for k in range(16)
            ]
            code = scale_code(tile_max([x for pair in tiles for x in pair]))
            fac = encode_factor(code)
            for k, (re, im) in enumerate(tiles):
                ms[s, n, 8 * k : 8 * k + 8, :] = pack(re * fac, im * fac)
            ms[s, n, 128:136, :] = code

    for s in range(SLOTS):
        recv_all(narrow_copy, NARROW, me_n, n_args, s)
        first_both(s)
        mr[s, me_n] = ms[s, me_n]
        send_all(narrow_copy, NARROW, me_n, m_args, s)

    row16 = lax.broadcasted_iota(i32, (16, 128), 0)

    def second_back(s, part):
        def fill(n, _):
            d = decode_factor(mr[s, n, 128:136, :])
            d = jnp.concatenate([d, d], axis=0)
            if part is not None:
                if part == 0:
                    f = jnp.where(special, jnp.where(n < 4, 2.0, 0.0), 1.0)
                else:
                    f = jnp.where(n < 4, 0.0, 2.0)
                hit = (row16 == 0) & (special & ((n == 0) | (n == 4)))
            for c in range(8):
                re, im = unpack(mr[s, n, 16 * c : 16 * c + 16, :])
                re, im = re * d, im * d
                if part == 0:
                    if c == 0:
                        re, im = jnp.where(hit, re, re * f), jnp.where(hit, 0.0, im * f)
                    else:
                        re, im = re * f, im * f
                elif part == 1:
                    if c == 0:
                        re, im = jnp.where(hit, im, re * f), jnp.where(hit, 0.0, im * f)
                    else:
                        re, im = re * f, im * f
                lanes = slice(128 * (c % 2), 128 * (c % 2) + 128)
                for dst, x in ((rows16(16 * n, 16), re), (rows16(128 + 16 * n, 16), im)):
                    h, l = halves(x)
                    bh[c // 2, dst, lanes] = h
                    bl[c // 2, dst, lanes] = l
            return 0

        lax.fori_loop(0, 8, fill, 0)
        for cp in range(4):
            big[cp] = mm(yi[0], bh[cp]) + mm(yi[1], bh[cp]) + mm(yi[0], bl[cp])

        def spread(t, _):
            v = []
            at = rows16(16 * t, 16)
            for c in range(8):
                lanes = slice(128 * (c % 2), 128 * (c % 2) + 128)
                y = (big[c // 2, at, lanes], big[c // 2, rows16(128 + 16 * t, 16), lanes])
                v.append(y if c == 0 else turn(y, tyc[c, at, :], tys[c, at, :], 1))
            v = dft8(v, 1)
            for b in range(8):
                to = rows16(128 * (b % 2) + 16 * t, 16)
                if part == 1:
                    big2[b // 2, to, 128:256] = v[b][0]
                else:
                    big2[b // 2, to, 0:128] = v[b][0]
                    big2[b // 2, to, 128:256] = v[b][1]
            return 0

        lax.fori_loop(0, 8, spread, 0)

    for s in range(SLOTS):
        recv_all(narrow_copy, NARROW, me_n, m_args, s)
        second_back(s, 0 if s == 0 else None)
        if s == 0:
            @pl.when(special)
            def _():
                second_back(0, 1)

        def read_back(w):
            b = w // 4
            at = rows((b % 2) * 128 + (w % 4) * 32, 32)
            return big2[b // 2, at, 0:128], big2[b // 2, at, 128:256]

        def code_back(w, _, s=s):
            code_wide(read_back, us, s, w, w)
            return 0

        lax.fori_loop(0, WIDE, code_back, 0)
        keep = pltpu.make_async_copy(us.at[s, me_w], out.at[s, me_w], u_recv.at[s, me_w])
        keep.start()
        send_all(wide_copy, WIDE, me_w, u_args, s)

    lax.fori_loop(1, WIDE, recv_groups, 0)
    pltpu.make_async_copy(brecv, got, g_sem.at[0]).start()
    for g in range(16):
        named = jnp.concatenate(
            [brecv[2 * g, :, 512:640], brecv[2 * g + 1, :, 512:640]], axis=0
        )
        listed = jnp.round(mm_t(join[...], named))
        numbers[g] = listed.astype(i32)
        marks = listed if g == 0 else jnp.maximum(marks, listed)
    flag[...] = jnp.broadcast_to(jnp.max(marks, axis=1, keepdims=True), (8, 128)).astype(i32)
    lax.fori_loop(1, WIDE, sent_groups, 0)
    lax.fori_loop(1, NARROW, sent_measures, 0)
    pltpu.make_async_copy(brecv, got, g_sem.at[0]).wait()

    for s in range(SLOTS):
        pltpu.make_async_copy(us.at[s, me_w], out.at[s, me_w], u_recv.at[s, me_w]).wait()
        recv_all(wide_copy, WIDE, me_w, u_args, s)
        sent_all(wide_copy, WIDE, me_w, w_args, s)
        sent_all(narrow_copy, NARROW, me_n, n_args, s)
        sent_all(narrow_copy, NARROW, me_n, m_args, s)
        sent_all(wide_copy, WIDE, me_w, u_args, s)
    v_main.wait_send()

    @pl.when(jnp.logical_not(alone))
    def _():
        v_side.wait_send()


def spectral(noise, spectrum, owner, cell, assay, pencils, loads):
    t = TABLES
    angle = 2 * np.pi * np.arange(8)[:, None] * np.arange(128)[None, :] / 1024
    tyc = np.repeat(np.cos(angle).astype(np.float32)[:, :, None], 128, axis=2)
    tys = np.repeat(np.sin(angle).astype(np.float32)[:, :, None], 128, axis=2)
    vmem = pl.BlockSpec(memory_space=pltpu.VMEM)
    dma = pltpu.SemaphoreType.DMA
    return pl.pallas_call(
        spectral_kernel,
        out_shape=(
            jax.ShapeDtypeStruct((SLOTS, WIDE, 40, 128), i32),
            jax.ShapeDtypeStruct((WIDE, 64, 640), bf16),
            jax.ShapeDtypeStruct((16, 8, 128), i32),
            jax.ShapeDtypeStruct((8, 128), i32),
        ),
        in_specs=[vmem] * 19,
        out_specs=(pl.BlockSpec(memory_space=pl.ANY), pl.BlockSpec(memory_space=pl.ANY), vmem, vmem),
        scratch_shapes=[
            pltpu.VMEM((2048, 128), f32),
            pltpu.VMEM((2048, 128), f32),
            pltpu.VMEM((SLOTS, WIDE, 40, 128), i32),
            pltpu.VMEM((SLOTS, WIDE, 40, 128), i32),
            pltpu.VMEM((4, 256, 256), bf16),
            pltpu.VMEM((4, 256, 256), bf16),
            pltpu.VMEM((4, 256, 256), f32),
            pltpu.VMEM((4, 256, 256), f32),
            pltpu.VMEM((SLOTS, NARROW, 136, 128), i32),
            pltpu.VMEM((SLOTS, NARROW, 136, 128), i32),
            pltpu.VMEM((8, 144, 256), bf16),
            pltpu.VMEM((8, 144, 256), bf16),
            pltpu.VMEM((SLOTS, NARROW, 136, 128), i32),
            pltpu.VMEM((SLOTS, NARROW, 136, 128), i32),
            pltpu.VMEM((SLOTS, WIDE, 40, 128), i32),
            pltpu.VMEM((SLOTS, 8, 128, 128), f32),
            pltpu.VMEM((8, 16, 128), f32),
            pltpu.VMEM((8, 128, 128), i32),
            pltpu.VMEM((8, 128, 128), i32),
            pltpu.VMEM((8, 8, 128), i32),
            pltpu.VMEM((2048, 128), f32),
            pltpu.VMEM((512, 512), bf16),
            pltpu.VMEM((16, 512), bf16),
            pltpu.VMEM((NARROW, ROOM, 512), bf16),
            pltpu.VMEM((NARROW, ROOM, 512), bf16),
            pltpu.VMEM((NARROW, 16, ROOM), bf16),
            pltpu.VMEM((NARROW, 16, ROOM), bf16),
            pltpu.VMEM((WIDE, 64, 640), bf16),
            pltpu.VMEM((WIDE, 64, 640), bf16),
            dma((SLOTS, WIDE)), dma((SLOTS, WIDE)),
            dma((SLOTS, NARROW)), dma((SLOTS, NARROW)),
            dma((SLOTS, NARROW)), dma((SLOTS, NARROW)),
            dma((SLOTS, WIDE)), dma((SLOTS, WIDE)),
            dma((2,)), dma((2,)),
            dma((NARROW,)), dma((NARROW,)), dma((NARROW,)), dma((NARROW,)),
            dma((WIDE,)), dma((WIDE,)), dma((1,)),
        ],
        compiler_params=pltpu.CompilerParams(
            collective_id=0, has_side_effects=True, vmem_limit_bytes=56 * 1024 * 1024
        ),
    )(
        noise.reshape(4096, 128), spectrum.reshape(4096, 128), t["tz"], t["yf"], t["yi"],
        t["xf"], t["xi"], tyc, tys, t["tx"], t["own2"], t["mir"], t["flips"],
        owner, cell, assay, pencils, loads, JOIN,
    )


def finish_kernel(numbers, freq, tzi, held, out, gathered, contrib, *accs):
    for acc in accs:
        acc[...] = jnp.zeros_like(acc)

    def depth(g, _):
        for j in range(4):
            y = g * 4 + j
            re, im = unpack(freq[pl.ds(y, 64, stride=40), :])
            d = decode_factor(freq[pl.ds(32 + lax.rem(y, 8), 64, stride=40), :])
            h, l = halves(jnp.concatenate([re * d, im * d], axis=0))
            u = jnp.concatenate([h, h, l], axis=0)
            out[pl.ds(y, 128, stride=32), :] = lax.dot_general(
                u, tzi[...], (((0,), (0,)), ((), ())), preferred_element_type=f32
            )
        return 0

    lax.fori_loop(0, 8, depth, 0)
    groups = numbers.shape[0]

    def gather(g, _):
        for j in range(128):
            gathered[pl.ds(g * 128 + j, 1), :] = out[pl.ds(numbers[g, 0, j], 1), :]
        return 0

    lax.fori_loop(0, groups, gather, 0)
    lane = lax.broadcasted_iota(i32, (128, 128), 1)

    def residual(g, _):
        at = rows16(g * 128, 128)
        depth_at = held[at, 515:516].astype(i32)
        grade = held[at, 524:525].astype(f32)
        value = jnp.sum(jnp.where(lane == depth_at, gathered[at, :], 0.0), axis=1, keepdims=True)
        resid = grade - value
        for k in range(TARGETS):
            contrib[k, at, :] = resid * held[at, 128 * k : 128 * k + 128].astype(f32)
        return 0

    lax.fori_loop(0, groups, residual, 0)

    def scatter(g, _):
        for j in range(128):
            for t in range(TARGETS):
                acc = accs[t + TARGETS * (j % 2)]
                at = pl.ds(numbers[g, 1 + t, j], 1)
                acc[at, :] = acc[at, :] + contrib[t, pl.ds(g * 128 + j, 1), :]
        return 0

    lax.fori_loop(0, groups, scatter, 0)

    def combine(g, _):
        at = rows(g * 64, 64)
        v = out[at, :]
        for acc in accs:
            v = v + acc[at, :]
        out[at, :] = v
        return 0

    lax.fori_loop(0, 64, combine, 0)


def finish(freq, held, numbers):
    vmem = pl.BlockSpec(memory_space=pltpu.VMEM)
    smem = pl.BlockSpec(memory_space=pltpu.SMEM)
    count = held.shape[0] * held.shape[1]
    return pl.pallas_call(
        finish_kernel,
        out_shape=jax.ShapeDtypeStruct((4096, 128), f32),
        in_specs=[smem] + [vmem] * 3,
        out_specs=vmem,
        scratch_shapes=[pltpu.VMEM((count, 128), f32), pltpu.VMEM((TARGETS, count, 128), f32)]
        + [pltpu.VMEM((4096, 128), f32)] * 8,
        compiler_params=pltpu.CompilerParams(vmem_limit_bytes=56 * 1024 * 1024),
    )(numbers, freq.reshape(-1, 128), TABLES["tzi"], held.reshape(count, -1))


def padded(assay, weights, owner, cell, pencils):
    count = owner.shape[0]
    order = jnp.arange(count, dtype=i32)
    earlier = order[:, None] < order[None, :]
    same = jnp.sum(earlier & (owner[:, None] == owner[None, :]), axis=0, dtype=i32)
    row = cell // NZ
    fields = [jnp.zeros((count,), i32), row // 256, row % 256, cell % NZ]
    for k in range(TARGETS):
        fields += [pencils[:, k] // 256, pencils[:, k] % 256]
    fields = [x.astype(bf16) for x in fields] + [assay]
    parts = jnp.zeros((count, 128), bf16).at[:, : len(fields)].set(jnp.stack(fields, axis=1))
    load = jnp.concatenate([weights, parts], axis=1)
    slots = jnp.arange(WIDE * NARROW * 8, dtype=i32)
    hot = (slots[:, None] == (owner * 8 + same)[None, :]).astype(bf16)
    held = jnp.dot(hot, load, preferred_element_type=f32).astype(bf16)
    held = held.reshape(WIDE, NARROW, 8, -1)
    held = lax.all_to_all(held, "wide", split_axis=0, concat_axis=0, tiled=True)
    held = lax.all_to_all(held, "narrow", split_axis=1, concat_axis=1, tiled=True)
    held = held.reshape(WIDE, 64, -1)
    names = held.reshape(WIDE * 64, -1)[:, TARGETS * NZ :].astype(f32)
    numbers = jnp.einsum("fc,gjc->gfj", jnp.asarray(JOIN, f32), names.reshape(16, 128, 128),
                         precision=lax.Precision.HIGHEST)
    return held, jnp.round(numbers).astype(i32)


def local(noise, spectrum, assay, measure_weights, measure_owner, measure_cell, measure_pencils):
    count = measure_owner.shape[1]
    freq, held, numbers, flag = spectral(
        noise, spectrum, measure_owner, measure_cell, assay, measure_pencils[0].T,
        measure_weights.reshape(count * TARGETS, NZ),
    )

    def roomy(_):
        weights = measure_weights[0].reshape(count, TARGETS * NZ)
        more = padded(assay[0], weights, measure_owner[0], measure_cell[0], measure_pencils[0])
        return finish(freq, *more)

    field = lax.cond(flag[5, 0] > 0, roomy, lambda _: finish(freq, held, numbers), 0)
    return field.reshape(noise.shape)


def solution(mesh):
    placed = (
        P("narrow", "wide", None),
        P("wide", None, "narrow"),
        P(("wide", "narrow"), None),
        P(("wide", "narrow"), None, None, None),
        P(("wide", "narrow"), None),
        P(("wide", "narrow"), None),
        P(("wide", "narrow"), None, None),
    )
    return jax.shard_map(
        local, mesh=mesh, in_specs=placed, out_specs=P("narrow", "wide", None), check_vma=False
    )
```

```python
import math

import jax
import jax.numpy as jnp
import ml_dtypes
import numpy as np
from jax import lax
from jax.experimental import pallas as pl
from jax.experimental.pallas import tpu as pltpu
from jax.sharding import PartitionSpec as P

NX, NY, NZ = 1024, 1024, 128
TARGETS = 4
WIDE, NARROW = 32, 8
SLOTS = 2
MESH = pl.DeviceIdType.MESH
f32, bf16, i32 = jnp.float32, jnp.bfloat16, jnp.int32

LN2 = math.log(2.0)
CODE = 16.0 / LN2
PEAK = 32600.0
TINY = 1e-30
SPEC_LOW = math.log(0.1)
SPEC_CODE = 65000.0 / math.log(85.0)
ROOT_HALF = math.sqrt(0.5)


def split(a):
    high = a.astype(ml_dtypes.bfloat16)
    low = (a - high.astype(np.float64)).astype(ml_dtypes.bfloat16)
    return high, low


def pair_matrix(sign):
    index = np.arange(128)
    angle = 2 * np.pi * (index[:, None] * index[None, :] % 128) / 128
    c, s = np.cos(angle), sign * np.sin(angle)
    return np.block([[c, -s], [s, c]])


def depth_forward():
    kz = 2 * np.arange(32)[None, :] + np.arange(2)[:, None]
    kz = kz.reshape(-1)
    z = np.arange(128)
    angle = 2 * np.pi * (kz[:, None] * z[None, :] % 128) / 128
    re, im = np.cos(angle), -np.sin(angle)
    im[kz == 0] = np.cos(np.pi * z)
    return np.concatenate([re, im], 0)


def depth_inverse():
    kz = (2 * np.arange(32)[None, :] + np.arange(2)[:, None]).reshape(-1)
    z = np.arange(128)
    angle = 2 * np.pi * (kz[:, None] * z[None, :] % 128) / 128
    re, im = 2 * np.cos(angle), -2 * np.sin(angle)
    re[kz == 0] = 1.0
    im[kz == 0] = np.cos(np.pi * z)
    return np.concatenate([re, im], 0)


def make_tables():
    h, l = split(depth_forward())
    tz = np.concatenate([h, l, h], 1)
    h, l = split(depth_inverse())
    pick = [np.r_[32 * s : 32 * s + 32, 64 + 32 * s : 96 + 32 * s] for s in range(SLOTS)]
    tzi = np.stack([np.concatenate([h[r], l[r], h[r]], 0) for r in pick])
    yf = np.stack(split(pair_matrix(-1.0)))
    yi = np.stack(split(pair_matrix(1.0)))
    xf = np.stack(split(pair_matrix(-1.0).T))
    xi = np.stack(split(pair_matrix(1.0).T))
    c = np.arange(8)
    a = np.arange(128)
    angle = 2 * np.pi * c[:, None] * a[None, :] / 1024
    tx = np.stack([np.cos(angle), np.sin(angle)]).astype(np.float32)
    row = np.arange(128)
    lane_of = 8 * (row % 16) + row // 16
    own = np.zeros((128, 128))
    own[row, lane_of] = 1
    mir = np.zeros((128, 128))
    mir[row, (128 - lane_of) % 128] = 1
    own2 = np.concatenate([own, own], 1).astype(ml_dtypes.bfloat16)
    flips = np.zeros((2, 128, 128))
    flips[0, (128 - row) % 128, row] = 1
    flips[1, 127 - row, row] = 1
    flips = np.concatenate([flips, flips], 1).astype(ml_dtypes.bfloat16)
    return dict(
        tz=tz, tzi=tzi, yf=yf, yi=yi, xf=xf, xi=xi, tx=tx, own2=own2,
        mir=mir.astype(ml_dtypes.bfloat16), flips=flips,
    )


TABLES = make_tables()
ROOM = 160


def join_matrix():
    m = np.zeros((8, 128))
    m[0, 1], m[0, 2] = 256, 1
    for k in range(TARGETS):
        m[1 + k, 4 + 2 * k], m[1 + k, 5 + 2 * k] = 256, 1
    m[5, 13] = 1
    return m.astype(ml_dtypes.bfloat16)


JOIN = join_matrix()


def halves(v):
    h = v.astype(bf16)
    return h, (v - h.astype(f32)).astype(bf16)


def times_i(v, sign):
    re, im = v
    return (-im, re) if sign > 0 else (im, -re)


def add(a, b):
    return a[0] + b[0], a[1] + b[1]


def sub(a, b):
    return a[0] - b[0], a[1] - b[1]


def dft4(v, sign):
    s, d = add(v[0], v[2]), sub(v[0], v[2])
    t, u = add(v[1], v[3]), times_i(sub(v[1], v[3]), sign)
    return [add(s, t), add(d, u), sub(s, t), sub(d, u)]


def dft8(v, sign):
    e = dft4(v[0::2], sign)
    o = dft4(v[1::2], sign)
    g = float(sign)
    re, im = o[1]
    o[1] = ((re - g * im) * ROOT_HALF, (im + g * re) * ROOT_HALF)
    o[2] = times_i(o[2], sign)
    re, im = o[3]
    o[3] = ((-re - g * im) * ROOT_HALF, (g * re - im) * ROOT_HALF)
    return [add(e[c], o[c]) for c in range(4)] + [sub(e[c], o[c]) for c in range(4)]


def turn(v, cos, sin, sign):
    re, im = v
    if sign < 0:
        return re * cos + im * sin, im * cos - re * sin
    return re * cos - im * sin, im * cos + re * sin


def scale_code(m):
    return jnp.ceil(jnp.log(jnp.maximum(m, TINY)) * CODE).astype(i32)


def encode_factor(code):
    return jnp.exp(code.astype(f32) * (-1.0 / CODE)) * PEAK


def decode_factor(code):
    return jnp.exp(code.astype(f32) * (1.0 / CODE)) * (1.0 / PEAK)


def pack(re, im):
    a = jnp.round(re).astype(i32)
    b = jnp.round(im).astype(i32)
    return (a << 16) | (b & 0xFFFF)


def unpack(word):
    return (word >> 16).astype(f32), ((word << 16) >> 16).astype(f32)


def tile_max(tiles):
    tiles = [jnp.abs(t) for t in tiles]
    while len(tiles) > 1:
        tiles = [jnp.maximum(a, b) for a, b in zip(tiles[0::2], tiles[1::2])] + (
            tiles[-1:] if len(tiles) % 2 else []
        )
    return tiles[0]


def mm(a, b):
    return jnp.dot(a, b, preferred_element_type=f32)


def mm_t(a, b):
    return lax.dot_general(a, b, (((1,), (1,)), ((), ())), preferred_element_type=f32)


def rows(start, size):
    return pl.ds(pl.multiple_of(start, 8), size)


def rows16(start, size):
    return pl.ds(pl.multiple_of(start, 16), size)


def spectral_kernel(
    noise, spec, tz, yf, yi, xf, xi, tyc, tys, tx, own2, mir, flips, owner, cell, assay, pencils, loads, join, tzi,
    field, got, numbers, flag,
    zre, zim, ws, wr, bh, bl, big, big2, ns, nr, lh, ll, ms, mr, us, ur,
    ear, bsp, vs, vr, vc, wf, weights, parts, asend, arecv, psend, precv, bsend, brecv,
    w_send, w_recv, n_send, n_recv, m_send, m_recv, u_send, u_recv, v_send, v_recv,
    a_send, a_recv, p_send, p_recv, b_send, b_recv, g_sem,
):
    me_w = lax.axis_index("wide")
    me_n = lax.axis_index("narrow")
    special = me_w == 0
    edge = special & ((me_n == 0) | (me_n == 4))

    barrier = pltpu.get_barrier_semaphore()

    def greet_wide(i, _):
        pl.semaphore_signal(
            barrier, inc=1, device_id={"wide": lax.rem(me_w + i, WIDE)}, device_id_type=MESH
        )
        return 0

    def greet_narrow(i, _):
        pl.semaphore_signal(
            barrier, inc=1, device_id={"narrow": lax.rem(me_n + i, NARROW)}, device_id_type=MESH
        )
        return 0

    lax.fori_loop(1, WIDE, greet_wide, 0)
    lax.fori_loop(1, NARROW, greet_narrow, 0)

    def wide_copy(src, dst, sends, recvs, s, peer, slot):
        return pltpu.make_async_remote_copy(
            src_ref=src.at[s, peer], dst_ref=dst.at[s, slot], send_sem=sends.at[s, peer],
            recv_sem=recvs.at[s, slot], device_id={"wide": peer}, device_id_type=MESH,
        )

    def narrow_copy(src, dst, sends, recvs, s, peer, slot):
        return pltpu.make_async_remote_copy(
            src_ref=src.at[s, peer], dst_ref=dst.at[s, slot], send_sem=sends.at[s, peer],
            recv_sem=recvs.at[s, slot], device_id={"narrow": peer}, device_id_type=MESH,
        )

    def send_all(make, count, me, args, s):
        def one(i, _):
            make(*args, s, lax.rem(me + i, count), me).start()
            return 0

        lax.fori_loop(1, count, one, 0)

    def recv_all(make, count, me, args, s):
        def one(i, _):
            peer = lax.rem(me + i, count)
            make(*args, s, peer, peer).wait_recv()
            return 0

        lax.fori_loop(1, count, one, 0)

    def sent_all(make, count, me, args, s):
        def one(i, _):
            peer = lax.rem(me + i, count)
            make(*args, s, peer, peer).wait_send()
            return 0

        lax.fori_loop(1, count, one, 0)

    w_args = (ws, wr, w_send, w_recv)
    n_args = (ns, nr, n_send, n_recv)
    m_args = (ms, mr, m_send, m_recv)
    def back_rows(s, slot):
        return ur.at[rows((s * WIDE + slot) * 40, 40), :]

    def back_copy(s, peer, slot):
        return pltpu.make_async_remote_copy(
            src_ref=us.at[s, peer], dst_ref=back_rows(s, slot), send_sem=u_send.at[s, peer],
            recv_sem=u_recv.at[s, slot], device_id={"wide": peer}, device_id_type=MESH,
        )


    late = special & (me_n >= 4)
    own_slots = (jnp.where(late, 2, 0), 1)
    mir_slots = (jnp.where(special & (me_n < 4), 2, jnp.where(special, 0, 2)), 3)

    def spectrum_rows(slot, e):
        return halves(spec[pl.ds(slot * 1024 + e, 128, stride=8), :])

    for e in range(8):
        back = (8 - e) % 8
        flip = flips[0 if e == 0 else 1]
        codes = []
        for s in range(SLOTS):
            h, l = spectrum_rows(own_slots[s], e)
            ear[s, e] = mm_t(own2[...], jnp.concatenate([h, l], axis=1))
            h, l = spectrum_rows(mir_slots[s], back)
            gh = mm_t(mir[...], h).astype(bf16)
            gl = mm_t(mir[...], l).astype(bf16)
            v = mm(jnp.concatenate([gh, gl], axis=1), flip)
            q = jnp.round((jnp.log(v) - SPEC_LOW) * SPEC_CODE - 32500.0)
            codes.append(jnp.clip(q, -32767.0, 32767.0))
        vs[e] = pack(codes[0], codes[1])

    v_main = pltpu.make_async_remote_copy(
        src_ref=vs, dst_ref=vr, send_sem=v_send.at[0], recv_sem=v_recv.at[0],
        device_id={"narrow": 7 - me_n}, device_id_type=MESH,
    )
    v_side = pltpu.make_async_remote_copy(
        src_ref=vs.at[:, pl.ds(0, 8), :], dst_ref=vc, send_sem=v_send.at[1], recv_sem=v_recv.at[1],
        device_id={"narrow": lax.rem(8 - me_n, 8)}, device_id_type=MESH,
    )

    alone = (me_n == 0) | (me_n == 4)

    @pl.when(alone)
    def _():
        vc[...] = vs[:, 0:8, :]

    pl.semaphore_wait(barrier, WIDE - 1 + NARROW - 1)
    v_main.start()

    @pl.when(jnp.logical_not(alone))
    def _():
        v_side.start()

    def depth(y, _):
        cells = [y * 4 + k for k in range(4)]
        pieces = []
        for k in cells:
            h, l = halves(noise[pl.ds(k, 128, stride=32), :])
            pieces.append(jnp.concatenate([h, h, l], axis=1))
        res = mm_t(tz[...], jnp.concatenate(pieces, axis=0))
        for i, k in enumerate(cells):
            zre[pl.ds(k, 64, stride=32), :] = res[:64, 128 * i : 128 * i + 128]
            zim[pl.ds(k, 64, stride=32), :] = res[64:, 128 * i : 128 * i + 128]
        return 0

    lax.fori_loop(0, 8, depth, 0)

    def code_wide(read, dst, s, w, to):
        re, im = read(w)
        m = tile_max([re[8 * t : 8 * t + 8] for t in range(4)] + [im[8 * t : 8 * t + 8] for t in range(4)])
        code = scale_code(m)
        fac = encode_factor(code)
        for t in range(4):
            sl = slice(8 * t, 8 * t + 8)
            dst[s, to, 8 * t : 8 * t + 8, :] = pack(re[sl] * fac, im[sl] * fac)
        dst[s, to, 32:40, :] = code

    for s in range(SLOTS):
        def read_depth(w, s=s):
            at = rows((s * 32 + w) * 32, 32)
            return zre[at, :], zim[at, :]

        def code_one(w, _, s=s, read=read_depth):
            code_wide(read, ws, s, w, w)
            return 0

        lax.fori_loop(0, WIDE, code_one, 0)
        wr[s, me_w] = ws[s, me_w]
        send_all(wide_copy, WIDE, me_w, w_args, s)

    room = asend.shape[1]
    count = owner.shape[1]
    owners = owner[...]
    cells = cell[...]
    narrow_of = (owners & 7).astype(f32)
    diagonal = lax.broadcasted_iota(i32, (128, 128), 0) == lax.broadcasted_iota(i32, (128, 128), 1)

    def column(line):
        pieces = []
        for k in range(count // 128):
            piece = jnp.broadcast_to(line[:, 128 * k : 128 * k + 128], (128, 128))
            pieces.append(jnp.sum(jnp.where(diagonal, piece, 0.0), axis=1, keepdims=True))
        return jnp.concatenate(pieces, axis=0)

    earlier = lax.broadcasted_iota(i32, (count, count), 0) < lax.broadcasted_iota(i32, (count, count), 1)

    def before(line):
        match = earlier & (column(line) == line)
        return jnp.sum(jnp.where(match, 1.0, 0.0), axis=0, keepdims=True)

    same = before(owners.astype(f32))
    rank = before(narrow_of)
    place = jnp.where(rank < room, narrow_of * room + rank, -1.0).astype(i32)
    over = jnp.max(jnp.where(rank < room, 0.0, 1.0), axis=1, keepdims=True)
    key = (owners >> 3 << 3).astype(f32) + same + 1.0
    part_row = lax.broadcasted_iota(i32, (16, count), 0)
    listed = jnp.zeros((16, count), f32)
    for r, line in (
        (0, key),
        (1, (cells >> 15).astype(f32)),
        (2, ((cells >> 7) & 255).astype(f32)),
        (3, (cells & 127).astype(f32)),
        (12, assay[...].astype(f32)),
        *((4 + 2 * k, (pencils[k : k + 1, :] >> 8).astype(f32)) for k in range(TARGETS)),
        *((5 + 2 * k, (pencils[k : k + 1, :] & 255).astype(f32)) for k in range(TARGETS)),
    ):
        listed = jnp.where(part_row == r, line, listed)
    parts[...] = listed.astype(bf16)
    wf[...] = loads[...].astype(f32)
    for k in range(TARGETS):
        weights[:, 128 * k : 128 * k + 128] = wf[pl.ds(k, count, stride=TARGETS), :].astype(bf16)
    room_row = lax.broadcasted_iota(i32, (room, count), 0)
    flag_row = lax.broadcasted_iota(i32, (16, room), 0) == 13

    def pack_measures(n, _):
        hot = jnp.where(room_row + n * room == place, 1.0, 0.0).astype(bf16)
        asend[n] = mm(hot, weights[...]).astype(bf16)
        psend[n] = jnp.where(flag_row, over, mm_t(parts[...], hot)).astype(bf16)
        return 0

    lax.fori_loop(0, NARROW, pack_measures, 0)
    arecv[me_n] = asend[me_n]
    precv[me_n] = psend[me_n]

    def to_narrow(src, dst, sends, recvs, peer, slot):
        return pltpu.make_async_remote_copy(
            src_ref=src.at[peer], dst_ref=dst.at[slot], send_sem=sends.at[peer],
            recv_sem=recvs.at[slot], device_id={"narrow": peer}, device_id_type=MESH,
        )

    def to_wide(peer, slot):
        return pltpu.make_async_remote_copy(
            src_ref=bsend.at[peer], dst_ref=brecv.at[slot], send_sem=b_send.at[peer],
            recv_sem=b_recv.at[slot], device_id={"wide": peer}, device_id_type=MESH,
        )

    a_args = (asend, arecv, a_send, a_recv)
    p_args = (psend, precv, p_send, p_recv)

    def send_measures(i, _):
        peer = lax.rem(me_n + i, NARROW)
        to_narrow(*p_args, peer, me_n).start()
        to_narrow(*a_args, peer, me_n).start()
        return 0

    def recv_measures(i, _):
        peer = lax.rem(me_n + i, NARROW)
        to_narrow(*p_args, peer, peer).wait_recv()
        to_narrow(*a_args, peer, peer).wait_recv()
        return 0

    def sent_measures(i, _):
        peer = lax.rem(me_n + i, NARROW)
        to_narrow(*p_args, peer, peer).wait_send()
        to_narrow(*a_args, peer, peer).wait_send()
        return 0

    def send_groups(i, _):
        to_wide(lax.rem(me_w + i, WIDE), me_w).start()
        return 0

    def recv_groups(i, _):
        peer = lax.rem(me_w + i, WIDE)
        to_wide(peer, peer).wait_recv()
        return 0

    def sent_groups(i, _):
        peer = lax.rem(me_w + i, WIDE)
        to_wide(peer, peer).wait_send()
        return 0

    lax.fori_loop(1, NARROW, send_measures, 0)

    def second_forward(s, p, q, r):
        def group(g, _):
            dec = [decode_factor(wr[s, 4 * b + g, 32:40, :]) for b in range(8)]
            dec = [jnp.concatenate([d, d], axis=0) for d in dec]
            for t in range(2):
                v = []
                for b in range(8):
                    re, im = unpack(wr[s, 4 * b + g, 16 * t : 16 * t + 16, :])
                    re, im = re * dec[b], im * dec[b]
                    if p is not None:
                        re, im = re * p + im * q, im * r
                    v.append((re, im))
                v = dft8(v, -1)
                at = rows16(g * 32 + 16 * t, 16)
                at_im = rows16(128 + g * 32 + 16 * t, 16)
                for c in range(8):
                    w = v[c] if c == 0 else turn(v[c], tyc[c, at, :], tys[c, at, :], -1)
                    lanes = slice(128 * (c % 2), 128 * (c % 2) + 128)
                    for dst, part in ((at, w[0]), (at_im, w[1])):
                        h, l = halves(part)
                        bh[c // 2, dst, lanes] = h
                        bl[c // 2, dst, lanes] = l
            return 0

        lax.fori_loop(0, 4, group, 0)
        for cp in range(4):
            big[cp] = mm(yf[0], bh[cp]) + mm(yf[1], bh[cp]) + mm(yf[0], bl[cp])

    first_row = lax.broadcasted_iota(i32, (8, 128), 0) == 0

    def code_narrow(s, n):
        tiles = []
        for c in range(8):
            lanes = slice(128 * (c % 2), 128 * (c % 2) + 128)
            for t in range(2):
                tiles.append((
                    big[c // 2, rows(16 * n + 8 * t, 8), lanes],
                    big[c // 2, rows(128 + 16 * n + 8 * t, 8), lanes],
                ))
        code = scale_code(tile_max([x for pair in tiles for x in pair]))
        fac = encode_factor(code)
        for k, (re, im) in enumerate(tiles):
            ns[s, n, 8 * k : 8 * k + 8, :] = pack(re * fac, im * fac)
        ns[s, n, 128:136, :] = code

    for s in range(SLOTS):
        recv_all(wide_copy, WIDE, me_w, w_args, s)
        if s == 0:
            one = jnp.where(special, 0.0, 1.0)
            second_forward(s, 1.0, 0.0, one)

            @pl.when(special)
            def _():
                big2[...] = big[...]
                second_forward(0, 0.0, 1.0, 0.0)
                top = big[0, 0:8, 0:128]
                mid = big[0, 64:72, 0:128]
                big[:, 0:64, :] = big2[:, 0:64, :]
                big[:, 128:192, :] = big2[:, 128:192, :]
                big[0, 128:136, 0:128] = jnp.where(first_row, top, big[0, 128:136, 0:128])
                big[0, 192:200, 0:128] = jnp.where(first_row, mid, big[0, 192:200, 0:128])
                big[0, 64:72, 0:128] = jnp.where(first_row, big2[0, 64:72, 0:128], mid)
        else:
            second_forward(s, None, None, None)

        def code_n(n, _, s=s):
            code_narrow(s, n)
            return 0

        lax.fori_loop(0, NARROW, code_n, 0)
        nr[s, me_n] = ns[s, me_n]
        send_all(narrow_copy, NARROW, me_n, n_args, s)


    lax.fori_loop(1, NARROW, recv_measures, 0)
    row = lax.broadcasted_iota(i32, (512, room), 0)
    want = (((row >> 4) << 3) + (row & 7) + 1).astype(f32)
    flags = precv[0].astype(f32)
    for k in range(1, NARROW):
        flags = jnp.maximum(flags, precv[k].astype(f32))
    flags = jnp.max(jnp.where(flag_row, flags, 0.0), axis=1, keepdims=True)
    flags = jnp.max(flags, axis=0, keepdims=True)
    flag_col = lax.broadcasted_iota(i32, (512, 128), 1) == 13
    for q in range(4):
        moved, named = 0.0, 0.0
        for k in range(2):
            key = precv[2 * q + k, 0:1, :].astype(f32)
            match = (((row >> 3) & 1) == k) & (want == key)
            hot = jnp.where(match, 1.0, 0.0).astype(bf16)
            moved = moved + mm(hot, arecv[2 * q + k])
            named = named + mm_t(hot, precv[2 * q + k])
        named = jnp.concatenate([named, jnp.zeros((512, 112), f32)], axis=1)
        named = jnp.where(flag_col, flags, named)
        bsend[:, 16 * q : 16 * q + 16, 0:512] = moved.astype(bf16).reshape(WIDE, 16, 512)
        bsend[:, 16 * q : 16 * q + 16, 512:640] = named.astype(bf16).reshape(WIDE, 16, 128)
    brecv[me_w] = bsend[me_w]
    lax.fori_loop(1, WIDE, send_groups, 0)

    total = 1.0 / (NX * NY * NZ)
    v_main.wait_recv()

    @pl.when(jnp.logical_not(alone))
    def _():
        v_side.wait_recv()

    def decode_spectrum(q):
        return jnp.exp((q + 32500.0) * (1.0 / SPEC_CODE) + SPEC_LOW)

    bsp[...] = jnp.zeros_like(bsp)

    @pl.when(edge)
    def _():
        sigma = jnp.where(me_n == 0, 1.0, -1.0)
        xs, vv = [], []
        for e in range(8):
            xs.append(ear[0, e, 0:8, :])
            vv.append(decode_spectrum(unpack(vc[e])[0]))

        def even(list_of, e):
            h, l = halves(list_of[(8 - e) % 8])
            pair = jnp.concatenate([h, l], axis=1)
            flip = flips[0 if e == 0 else 1]
            return (mm(pair, flip) + list_of[e]) * 0.5

        for e in range(8):
            a, b = even(xs, e), even(vv, e)
            bsp[e, 0:8, :] = jnp.where(first_row, (a - b) * (0.5 * total) * sigma, 0.0)
            big2[0, 8 * e : 8 * e + 8, 0:128] = (a + b) * (0.5 * total)

    for e in range(8):
        m0, m1 = unpack(vr[e])
        s0, s1 = unpack(vc[e])
        for s, m, side in ((0, m0, s0), (1, m1, s1)):
            m, side = decode_spectrum(m), decode_spectrum(side)
            ear_e = ear[s, e]
            lead = jnp.where(first_row, side, m[0:8])
            ear[s, e, 8:128, :] = (ear_e[8:128] + m[8:128]) * (0.5 * total)
            ear[s, e, 0:8, :] = (ear_e[0:8] + lead) * (0.5 * total)

    @pl.when(edge)
    def _():
        for e in range(8):
            ear[0, e, 0:8, :] = jnp.where(
                first_row, big2[0, 8 * e : 8 * e + 8, 0:128], ear[0, e, 0:8, :]
            )

    def first_both(s):
        def decs(n):
            d = decode_factor(nr[s, n, 128:136, :])
            return jnp.concatenate([d, d], axis=0)

        for n in range(8):
            big2[0, 16 * n : 16 * n + 16, 0:128] = decs(n)

        def load(c):
            v = []
            for n in range(8):
                re, im = unpack(nr[s, n, rows16(16 * c, 16), :])
                d = big2[0, 16 * n : 16 * n + 16, 0:128]
                v.append((re * d, im * d))
            return v

        def put(v, at):
            v = dft8(v, -1)
            for e in range(8):
                w = v[e] if e == 0 else turn(v[e], tx[0, e : e + 1, :], tx[1, e : e + 1, :], -1)
                for lanes, part in ((slice(0, 128), w[0]), (slice(128, 256), w[1])):
                    h, l = halves(part)
                    lh[e, at, lanes] = h
                    ll[e, at, lanes] = l

        def block(c, _):
            put(load(c), rows16(16 * c, 16))
            return 0

        lax.fori_loop(0, 8, block, 0)
        if s == 0:
            put([(re, -im) for re, im in load(0)], slice(128, 144))
        count = 144 if s == 0 else 128
        for e in range(8):
            h, l = lh[e, 0:count, :], ll[e, 0:count, :]
            z = mm(h, xf[0]) + mm(h, xf[1]) + mm(l, xf[0])
            fil = jnp.concatenate([ear[s, e], ear[s, e]], axis=1)
            g = z[0:128] * fil
            if s == 0:
                extra = jnp.concatenate([bsp[e], bsp[e]], axis=1)
                g = jnp.concatenate([g[0:16] + z[128:144] * extra, g[16:128]], axis=0)
            h, l = halves(g)
            big[e // 2, 128 * (e % 2) : 128 * (e % 2) + 128, :] = (
                mm(h, xi[0]) + mm(h, xi[1]) + mm(l, xi[0])
            )

        def unblock(c, _):
            v = []
            for e in range(8):
                at = rows16(128 * (e % 2) + 16 * c, 16)
                y = (big[e // 2, at, 0:128], big[e // 2, at, 128:256])
                v.append(y if e == 0 else turn(y, tx[0, e : e + 1, :], tx[1, e : e + 1, :], 1))
            v = dft8(v, 1)
            for n in range(8):
                at = rows16(128 * (n % 2) + 16 * c, 16)
                big2[n // 2, at, 0:128] = v[n][0]
                big2[n // 2, at, 128:256] = v[n][1]
            return 0

        lax.fori_loop(0, 8, unblock, 0)
        for n in range(8):
            base = 128 * (n % 2)
            tiles = [
                (big2[n // 2, base + 8 * k : base + 8 * k + 8, 0:128],
                 big2[n // 2, base + 8 * k : base + 8 * k + 8, 128:256])
                for k in range(16)
            ]
            code = scale_code(tile_max([x for pair in tiles for x in pair]))
            fac = encode_factor(code)
            for k, (re, im) in enumerate(tiles):
                ms[s, n, 8 * k : 8 * k + 8, :] = pack(re * fac, im * fac)
            ms[s, n, 128:136, :] = code

    for s in range(SLOTS):
        recv_all(narrow_copy, NARROW, me_n, n_args, s)
        first_both(s)
        mr[s, me_n] = ms[s, me_n]
        send_all(narrow_copy, NARROW, me_n, m_args, s)

    row16 = lax.broadcasted_iota(i32, (16, 128), 0)

    def second_back(s, part):
        def fill(n, _):
            d = decode_factor(mr[s, n, 128:136, :])
            d = jnp.concatenate([d, d], axis=0)
            if part is not None:
                if part == 0:
                    f = jnp.where(special, jnp.where(n < 4, 2.0, 0.0), 1.0)
                else:
                    f = jnp.where(n < 4, 0.0, 2.0)
                hit = (row16 == 0) & (special & ((n == 0) | (n == 4)))
            for c in range(8):
                re, im = unpack(mr[s, n, 16 * c : 16 * c + 16, :])
                re, im = re * d, im * d
                if part == 0:
                    if c == 0:
                        re, im = jnp.where(hit, re, re * f), jnp.where(hit, 0.0, im * f)
                    else:
                        re, im = re * f, im * f
                elif part == 1:
                    if c == 0:
                        re, im = jnp.where(hit, im, re * f), jnp.where(hit, 0.0, im * f)
                    else:
                        re, im = re * f, im * f
                lanes = slice(128 * (c % 2), 128 * (c % 2) + 128)
                for dst, x in ((rows16(16 * n, 16), re), (rows16(128 + 16 * n, 16), im)):
                    h, l = halves(x)
                    bh[c // 2, dst, lanes] = h
                    bl[c // 2, dst, lanes] = l
            return 0

        lax.fori_loop(0, 8, fill, 0)
        for cp in range(4):
            big[cp] = mm(yi[0], bh[cp]) + mm(yi[1], bh[cp]) + mm(yi[0], bl[cp])

        def spread(t, _):
            v = []
            at = rows16(16 * t, 16)
            for c in range(8):
                lanes = slice(128 * (c % 2), 128 * (c % 2) + 128)
                y = (big[c // 2, at, lanes], big[c // 2, rows16(128 + 16 * t, 16), lanes])
                v.append(y if c == 0 else turn(y, tyc[c, at, :], tys[c, at, :], 1))
            v = dft8(v, 1)
            for b in range(8):
                to = rows16(128 * (b % 2) + 16 * t, 16)
                if part == 1:
                    big2[b // 2, to, 128:256] = v[b][0]
                else:
                    big2[b // 2, to, 0:128] = v[b][0]
                    big2[b // 2, to, 128:256] = v[b][1]
            return 0

        lax.fori_loop(0, 8, spread, 0)

    for s in range(SLOTS):
        recv_all(narrow_copy, NARROW, me_n, m_args, s)
        second_back(s, 0 if s == 0 else None)
        if s == 0:
            @pl.when(special)
            def _():
                second_back(0, 1)

        def read_back(w):
            b = w // 4
            at = rows((b % 2) * 128 + (w % 4) * 32, 32)
            return big2[b // 2, at, 0:128], big2[b // 2, at, 128:256]

        def code_back(w, _, s=s):
            code_wide(read_back, us, s, w, w)
            return 0

        lax.fori_loop(0, WIDE, code_back, 0)
        back_rows(s, me_w)[...] = us[s, me_w]
        send_all(back_copy, WIDE, me_w, (), s)

    def depth_back(s):
        base = s * WIDE * 40

        def some(g, _):
            for j in range(4):
                y = g * 4 + j
                re, im = unpack(ur[pl.ds(base + y, WIDE, stride=40), :])
                d = decode_factor(ur[pl.ds(base + 32 + lax.rem(y, 8), WIDE, stride=40), :])
                h, l = halves(jnp.concatenate([re * d, im * d], axis=0))
                u = jnp.concatenate([h, h, l], axis=0)
                part = lax.dot_general(
                    u, tzi[s], (((0,), (0,)), ((), ())), preferred_element_type=f32
                )
                at = pl.ds(y, 128, stride=32)
                field[at, :] = part if s == 0 else field[at, :] + part
            return 0

        lax.fori_loop(0, 8, some, 0)

    lax.fori_loop(1, WIDE, recv_groups, 0)
    held = pltpu.make_async_copy(brecv, got, g_sem.at[0])
    held.start()
    for g in range(16):
        named = jnp.concatenate(
            [brecv[2 * g, :, 512:640], brecv[2 * g + 1, :, 512:640]], axis=0
        )
        listed = jnp.round(mm_t(join[...], named))
        numbers[g] = listed.astype(i32)
        marks = listed if g == 0 else jnp.maximum(marks, listed)
    flag[0, 0] = jnp.max(marks[5:6, :]).astype(i32)
    recv_all(back_copy, WIDE, me_w, (), 0)
    depth_back(0)
    recv_all(back_copy, WIDE, me_w, (), 1)
    depth_back(1)
    held.wait()
    lax.fori_loop(1, WIDE, sent_groups, 0)
    lax.fori_loop(1, NARROW, sent_measures, 0)
    for s in range(SLOTS):
        sent_all(wide_copy, WIDE, me_w, w_args, s)
        sent_all(narrow_copy, NARROW, me_n, n_args, s)
        sent_all(narrow_copy, NARROW, me_n, m_args, s)
        sent_all(back_copy, WIDE, me_w, (), s)
    v_main.wait_send()

    @pl.when(jnp.logical_not(alone))
    def _():
        v_side.wait_send()


def spectral(noise, spectrum, owner, cell, assay, pencils, loads):
    t = TABLES
    angle = 2 * np.pi * np.arange(8)[:, None] * np.arange(128)[None, :] / 1024
    tyc = np.repeat(np.cos(angle).astype(np.float32)[:, :, None], 128, axis=2)
    tys = np.repeat(np.sin(angle).astype(np.float32)[:, :, None], 128, axis=2)
    vmem = pl.BlockSpec(memory_space=pltpu.VMEM)
    dma = pltpu.SemaphoreType.DMA
    return pl.pallas_call(
        spectral_kernel,
        out_shape=(
            jax.ShapeDtypeStruct((4096, 128), f32),
            jax.ShapeDtypeStruct((WIDE, 64, 640), bf16),
            jax.ShapeDtypeStruct((16, 8, 128), i32),
            jax.ShapeDtypeStruct((1, 1), i32),
        ),
        in_specs=[vmem] * 20,
        out_specs=(
            vmem, pl.BlockSpec(memory_space=pl.ANY), vmem, pl.BlockSpec(memory_space=pltpu.SMEM),
        ),
        scratch_shapes=[
            pltpu.VMEM((2048, 128), f32),
            pltpu.VMEM((2048, 128), f32),
            pltpu.VMEM((SLOTS, WIDE, 40, 128), i32),
            pltpu.VMEM((SLOTS, WIDE, 40, 128), i32),
            pltpu.VMEM((4, 256, 256), bf16),
            pltpu.VMEM((4, 256, 256), bf16),
            pltpu.VMEM((4, 256, 256), f32),
            pltpu.VMEM((4, 256, 256), f32),
            pltpu.VMEM((SLOTS, NARROW, 136, 128), i32),
            pltpu.VMEM((SLOTS, NARROW, 136, 128), i32),
            pltpu.VMEM((8, 144, 256), bf16),
            pltpu.VMEM((8, 144, 256), bf16),
            pltpu.VMEM((SLOTS, NARROW, 136, 128), i32),
            pltpu.VMEM((SLOTS, NARROW, 136, 128), i32),
            pltpu.VMEM((SLOTS, WIDE, 40, 128), i32),
            pltpu.VMEM((SLOTS * WIDE * 40, 128), i32),
            pltpu.VMEM((SLOTS, 8, 128, 128), f32),
            pltpu.VMEM((8, 16, 128), f32),
            pltpu.VMEM((8, 128, 128), i32),
            pltpu.VMEM((8, 128, 128), i32),
            pltpu.VMEM((8, 8, 128), i32),
            pltpu.VMEM((2048, 128), f32),
            pltpu.VMEM((512, 512), bf16),
            pltpu.VMEM((16, 512), bf16),
            pltpu.VMEM((NARROW, ROOM, 512), bf16),
            pltpu.VMEM((NARROW, ROOM, 512), bf16),
            pltpu.VMEM((NARROW, 16, ROOM), bf16),
            pltpu.VMEM((NARROW, 16, ROOM), bf16),
            pltpu.VMEM((WIDE, 64, 640), bf16),
            pltpu.VMEM((WIDE, 64, 640), bf16),
            dma((SLOTS, WIDE)), dma((SLOTS, WIDE)),
            dma((SLOTS, NARROW)), dma((SLOTS, NARROW)),
            dma((SLOTS, NARROW)), dma((SLOTS, NARROW)),
            dma((SLOTS, WIDE)), dma((SLOTS, WIDE)),
            dma((2,)), dma((2,)),
            dma((NARROW,)), dma((NARROW,)), dma((NARROW,)), dma((NARROW,)),
            dma((WIDE,)), dma((WIDE,)), dma((1,)),
        ],
        compiler_params=pltpu.CompilerParams(
            collective_id=0, has_side_effects=True, vmem_limit_bytes=56 * 1024 * 1024
        ),
    )(
        noise.reshape(4096, 128), spectrum.reshape(4096, 128), t["tz"], t["yf"], t["yi"],
        t["xf"], t["xi"], tyc, tys, t["tx"], t["own2"], t["mir"], t["flips"],
        owner, cell, assay, pencils, loads, JOIN, t["tzi"],
    )


def finish_kernel(numbers, field, held, out, gathered, contrib, sems, *accs):
    for acc in accs:
        acc[...] = jnp.zeros_like(acc)

    groups = numbers.shape[0]

    def gather(g, _):
        for j in range(128):
            gathered[pl.ds(g * 128 + j, 1), :] = field[pl.ds(numbers[g, 0, j], 1), :]
        return 0

    lax.fori_loop(0, groups, gather, 0)
    lane = lax.broadcasted_iota(i32, (128, 128), 1)

    def residual(g, _):
        at = rows16(g * 128, 128)
        depth_at = held[at, 515:516].astype(i32)
        grade = held[at, 524:525].astype(f32)
        value = jnp.sum(jnp.where(lane == depth_at, gathered[at, :], 0.0), axis=1, keepdims=True)
        resid = grade - value
        for k in range(TARGETS):
            contrib[k, at, :] = resid * held[at, 128 * k : 128 * k + 128].astype(f32)
        return 0

    lax.fori_loop(0, groups, residual, 0)

    def scatter(g, _):
        for j in range(128):
            for t in range(TARGETS):
                acc = accs[t + TARGETS * (j % 2)]
                at = pl.ds(numbers[g, 1 + t, j], 1)
                acc[at, :] = acc[at, :] + contrib[t, pl.ds(g * 128 + j, 1), :]
        return 0

    lax.fori_loop(0, groups, scatter, 0)

    def leave(g):
        at = rows(g * 256, 256)
        return pltpu.make_async_copy(accs[0].at[at, :], out.at[at, :], sems.at[g])

    def combine(g, _):
        for j in range(4):
            at = rows(g * 256 + 64 * j, 64)
            v = field[at, :]
            for acc in accs:
                v = v + acc[at, :]
            accs[0][at, :] = v
        leave(g).start()
        return 0

    def left(g, _):
        leave(g).wait()
        return 0

    lax.fori_loop(0, 16, combine, 0)
    lax.fori_loop(0, 16, left, 0)


def finish(field, held, numbers):
    vmem = pl.BlockSpec(memory_space=pltpu.VMEM)
    smem = pl.BlockSpec(memory_space=pltpu.SMEM)
    count = held.shape[0] * held.shape[1]
    return pl.pallas_call(
        finish_kernel,
        out_shape=jax.ShapeDtypeStruct((4096, 128), f32),
        in_specs=[smem, vmem, vmem],
        out_specs=pl.BlockSpec(memory_space=pltpu.HBM),
        scratch_shapes=[
            pltpu.VMEM((count, 128), f32),
            pltpu.VMEM((TARGETS, count, 128), f32),
            pltpu.SemaphoreType.DMA((16,)),
        ]
        + [pltpu.VMEM((4096, 128), f32)] * 8,
        compiler_params=pltpu.CompilerParams(vmem_limit_bytes=56 * 1024 * 1024),
    )(numbers, field, held.reshape(count, -1))


def padded(assay, weights, owner, cell, pencils):
    count = owner.shape[0]
    order = jnp.arange(count, dtype=i32)
    earlier = order[:, None] < order[None, :]
    same = jnp.sum(earlier & (owner[:, None] == owner[None, :]), axis=0, dtype=i32)
    row = cell // NZ
    fields = [jnp.zeros((count,), i32), row // 256, row % 256, cell % NZ]
    for k in range(TARGETS):
        fields += [pencils[:, k] // 256, pencils[:, k] % 256]
    fields = [x.astype(bf16) for x in fields] + [assay]
    parts = jnp.zeros((count, 128), bf16).at[:, : len(fields)].set(jnp.stack(fields, axis=1))
    load = jnp.concatenate([weights, parts], axis=1)
    slots = jnp.arange(WIDE * NARROW * 8, dtype=i32)
    hot = (slots[:, None] == (owner * 8 + same)[None, :]).astype(bf16)
    held = jnp.dot(hot, load, preferred_element_type=f32).astype(bf16)
    held = held.reshape(WIDE, NARROW, 8, -1)
    held = lax.all_to_all(held, "wide", split_axis=0, concat_axis=0, tiled=True)
    held = lax.all_to_all(held, "narrow", split_axis=1, concat_axis=1, tiled=True)
    held = held.reshape(WIDE, 64, -1)
    names = held.reshape(WIDE * 64, -1)[:, TARGETS * NZ :].astype(f32)
    numbers = jnp.einsum("fc,gjc->gfj", jnp.asarray(JOIN, f32), names.reshape(16, 128, 128),
                         precision=lax.Precision.HIGHEST)
    return held, jnp.round(numbers).astype(i32)


def local(noise, spectrum, assay, measure_weights, measure_owner, measure_cell, measure_pencils):
    count = measure_owner.shape[1]
    field, held, numbers, flag = spectral(
        noise, spectrum, measure_owner, measure_cell, assay, measure_pencils[0].T,
        measure_weights.reshape(count * TARGETS, NZ),
    )

    def roomy(_):
        weights = measure_weights[0].reshape(count, TARGETS * NZ)
        more = padded(assay[0], weights, measure_owner[0], measure_cell[0], measure_pencils[0])
        return finish(field, *more)

    done = lax.cond(flag[0, 0] > 0, roomy, lambda _: finish(field, held, numbers), 0)
    return done.reshape(noise.shape)


def solution(mesh):
    placed = (
        P("narrow", "wide", None),
        P("wide", None, "narrow"),
        P(("wide", "narrow"), None),
        P(("wide", "narrow"), None, None, None),
        P(("wide", "narrow"), None),
        P(("wide", "narrow"), None),
        P(("wide", "narrow"), None, None),
    )
    return jax.shard_map(
        local, mesh=mesh, in_specs=placed, out_specs=P("narrow", "wide", None), check_vma=False
    )
```

```python
import math

import jax
import jax.numpy as jnp
import ml_dtypes
import numpy as np
from jax import lax
from jax.experimental import pallas as pl
from jax.experimental.pallas import tpu as pltpu
from jax.sharding import PartitionSpec as P

NX, NY, NZ = 1024, 1024, 128
TARGETS = 4
WIDE, NARROW = 32, 8
SLOTS = 2
MESH = pl.DeviceIdType.MESH
f32, bf16, i32 = jnp.float32, jnp.bfloat16, jnp.int32

LN2 = math.log(2.0)
CODE = 16.0 / LN2
PEAK = 32600.0
TINY = 1e-30
SPEC_LOW = math.log(0.1)
SPEC_CODE = 65000.0 / math.log(85.0)
ROOT_HALF = math.sqrt(0.5)


def split(a):
    high = a.astype(ml_dtypes.bfloat16)
    low = (a - high.astype(np.float64)).astype(ml_dtypes.bfloat16)
    return high, low


def pair_matrix(sign):
    index = np.arange(128)
    angle = 2 * np.pi * (index[:, None] * index[None, :] % 128) / 128
    c, s = np.cos(angle), sign * np.sin(angle)
    return np.block([[c, -s], [s, c]])


def depth_forward():
    kz = 2 * np.arange(32)[None, :] + np.arange(2)[:, None]
    kz = kz.reshape(-1)
    z = np.arange(128)
    angle = 2 * np.pi * (kz[:, None] * z[None, :] % 128) / 128
    re, im = np.cos(angle), -np.sin(angle)
    im[kz == 0] = np.cos(np.pi * z)
    return np.concatenate([re, im], 0)


def depth_inverse():
    kz = (2 * np.arange(32)[None, :] + np.arange(2)[:, None]).reshape(-1)
    z = np.arange(128)
    angle = 2 * np.pi * (kz[:, None] * z[None, :] % 128) / 128
    re, im = 2 * np.cos(angle), -2 * np.sin(angle)
    re[kz == 0] = 1.0
    im[kz == 0] = np.cos(np.pi * z)
    return np.concatenate([re, im], 0)


def make_tables():
    h, l = split(depth_forward())
    tz = np.concatenate([h, l, h], 1)
    h, l = split(depth_inverse())
    tzi = np.concatenate([h, l, h], 0)
    yf = np.stack(split(pair_matrix(-1.0)))
    yi = np.stack(split(pair_matrix(1.0)))
    xf = np.stack(split(pair_matrix(-1.0).T))
    xi = np.stack(split(pair_matrix(1.0).T))
    c = np.arange(8)
    a = np.arange(128)
    angle = 2 * np.pi * c[:, None] * a[None, :] / 1024
    tx = np.stack([np.cos(angle), np.sin(angle)]).astype(np.float32)
    row = np.arange(128)
    lane_of = 8 * (row % 16) + row // 16
    own = np.zeros((128, 128))
    own[row, lane_of] = 1
    mir = np.zeros((128, 128))
    mir[row, (128 - lane_of) % 128] = 1
    own2 = np.concatenate([own, own], 1).astype(ml_dtypes.bfloat16)
    flips = np.zeros((2, 128, 128))
    flips[0, (128 - row) % 128, row] = 1
    flips[1, 127 - row, row] = 1
    flips = np.concatenate([flips, flips], 1).astype(ml_dtypes.bfloat16)
    return dict(
        tz=tz, tzi=tzi, yf=yf, yi=yi, xf=xf, xi=xi, tx=tx, own2=own2,
        mir=mir.astype(ml_dtypes.bfloat16), flips=flips,
    )


TABLES = make_tables()
ROOM = 160


def join_matrix():
    m = np.zeros((8, 128))
    m[0, 1], m[0, 2] = 256, 1
    for k in range(TARGETS):
        m[1 + k, 4 + 2 * k], m[1 + k, 5 + 2 * k] = 256, 1
    m[5, 13] = 1
    return m.astype(ml_dtypes.bfloat16)


JOIN = join_matrix()


def halves(v):
    h = v.astype(bf16)
    return h, (v - h.astype(f32)).astype(bf16)


def times_i(v, sign):
    re, im = v
    return (-im, re) if sign > 0 else (im, -re)


def add(a, b):
    return a[0] + b[0], a[1] + b[1]


def sub(a, b):
    return a[0] - b[0], a[1] - b[1]


def dft4(v, sign):
    s, d = add(v[0], v[2]), sub(v[0], v[2])
    t, u = add(v[1], v[3]), times_i(sub(v[1], v[3]), sign)
    return [add(s, t), add(d, u), sub(s, t), sub(d, u)]


def dft8(v, sign):
    e = dft4(v[0::2], sign)
    o = dft4(v[1::2], sign)
    g = float(sign)
    re, im = o[1]
    o[1] = ((re - g * im) * ROOT_HALF, (im + g * re) * ROOT_HALF)
    o[2] = times_i(o[2], sign)
    re, im = o[3]
    o[3] = ((-re - g * im) * ROOT_HALF, (g * re - im) * ROOT_HALF)
    return [add(e[c], o[c]) for c in range(4)] + [sub(e[c], o[c]) for c in range(4)]


def turn(v, cos, sin, sign):
    re, im = v
    if sign < 0:
        return re * cos + im * sin, im * cos - re * sin
    return re * cos - im * sin, im * cos + re * sin


def scale_code(m):
    return jnp.ceil(jnp.log(jnp.maximum(m, TINY)) * CODE).astype(i32)


def encode_factor(code):
    return jnp.exp(code.astype(f32) * (-1.0 / CODE)) * PEAK


def decode_factor(code):
    return jnp.exp(code.astype(f32) * (1.0 / CODE)) * (1.0 / PEAK)


def pack(re, im):
    a = jnp.round(re).astype(i32)
    b = jnp.round(im).astype(i32)
    return (a << 16) | (b & 0xFFFF)


def unpack(word):
    return (word >> 16).astype(f32), ((word << 16) >> 16).astype(f32)


def tile_max(tiles):
    tiles = [jnp.abs(t) for t in tiles]
    while len(tiles) > 1:
        tiles = [jnp.maximum(a, b) for a, b in zip(tiles[0::2], tiles[1::2])] + (
            tiles[-1:] if len(tiles) % 2 else []
        )
    return tiles[0]


def mm(a, b):
    return jnp.dot(a, b, preferred_element_type=f32)


def mm_t(a, b):
    return lax.dot_general(a, b, (((1,), (1,)), ((), ())), preferred_element_type=f32)


def rows(start, size):
    return pl.ds(pl.multiple_of(start, 8), size)


def rows16(start, size):
    return pl.ds(pl.multiple_of(start, 16), size)


def spectral_kernel(
    noise, spec, tz, yf, yi, xf, xi, tyc, tys, tx, own2, mir, flips, owner, cell, assay, pencils, loads, join,
    out, got, numbers, flag,
    zre, zim, ws, wr, bh, bl, big, big2, ns, nr, lh, ll, ms, mr, us,
    ear, bsp, vs, vr, vc, wf, weights, parts, asend, arecv, psend, precv, bsend, brecv,
    w_send, w_recv, n_send, n_recv, m_send, m_recv, u_send, u_recv, v_send, v_recv,
    a_send, a_recv, p_send, p_recv, b_send, b_recv, g_sem,
):
    me_w = lax.axis_index("wide")
    me_n = lax.axis_index("narrow")
    special = me_w == 0
    edge = special & ((me_n == 0) | (me_n == 4))

    barrier = pltpu.get_barrier_semaphore()

    def greet_wide(i, _):
        pl.semaphore_signal(
            barrier, inc=1, device_id={"wide": lax.rem(me_w + i, WIDE)}, device_id_type=MESH
        )
        return 0

    def greet_narrow(i, _):
        pl.semaphore_signal(
            barrier, inc=1, device_id={"narrow": lax.rem(me_n + i, NARROW)}, device_id_type=MESH
        )
        return 0

    lax.fori_loop(1, WIDE, greet_wide, 0)
    lax.fori_loop(1, NARROW, greet_narrow, 0)

    def wide_copy(src, dst, sends, recvs, s, peer, slot):
        return pltpu.make_async_remote_copy(
            src_ref=src.at[s, peer], dst_ref=dst.at[s, slot], send_sem=sends.at[s, peer],
            recv_sem=recvs.at[s, slot], device_id={"wide": peer}, device_id_type=MESH,
        )

    def narrow_copy(src, dst, sends, recvs, s, peer, slot):
        return pltpu.make_async_remote_copy(
            src_ref=src.at[s, peer], dst_ref=dst.at[s, slot], send_sem=sends.at[s, peer],
            recv_sem=recvs.at[s, slot], device_id={"narrow": peer}, device_id_type=MESH,
        )

    def send_all(make, count, me, args, s):
        def one(i, _):
            make(*args, s, lax.rem(me + i, count), me).start()
            return 0

        lax.fori_loop(1, count, one, 0)

    def recv_all(make, count, me, args, s):
        def one(i, _):
            peer = lax.rem(me + i, count)
            make(*args, s, peer, peer).wait_recv()
            return 0

        lax.fori_loop(1, count, one, 0)

    def sent_all(make, count, me, args, s):
        def one(i, _):
            peer = lax.rem(me + i, count)
            make(*args, s, peer, peer).wait_send()
            return 0

        lax.fori_loop(1, count, one, 0)

    w_args = (ws, wr, w_send, w_recv)
    n_args = (ns, nr, n_send, n_recv)
    m_args = (ms, mr, m_send, m_recv)
    u_args = (us, out, u_send, u_recv)

    room = asend.shape[1]
    count = owner.shape[1]
    owners = owner[...]
    cells = cell[...]
    narrow_of = (owners & 7).astype(f32)
    diagonal = lax.broadcasted_iota(i32, (128, 128), 0) == lax.broadcasted_iota(i32, (128, 128), 1)

    def column(line):
        pieces = []
        for k in range(count // 128):
            piece = jnp.broadcast_to(line[:, 128 * k : 128 * k + 128], (128, 128))
            pieces.append(jnp.sum(jnp.where(diagonal, piece, 0.0), axis=1, keepdims=True))
        return jnp.concatenate(pieces, axis=0)

    earlier = lax.broadcasted_iota(i32, (count, count), 0) < lax.broadcasted_iota(i32, (count, count), 1)

    def before(line):
        match = earlier & (column(line) == line)
        return jnp.sum(jnp.where(match, 1.0, 0.0), axis=0, keepdims=True)

    same = before(owners.astype(f32))
    rank = before(narrow_of)
    place = jnp.where(rank < room, narrow_of * room + rank, -1.0).astype(i32)
    over = jnp.max(jnp.where(rank < room, 0.0, 1.0), axis=1, keepdims=True)
    key = (owners >> 3 << 3).astype(f32) + same + 1.0
    part_row = lax.broadcasted_iota(i32, (16, count), 0)
    listed = jnp.zeros((16, count), f32)
    for r, line in (
        (0, key),
        (1, (cells >> 15).astype(f32)),
        (2, ((cells >> 7) & 255).astype(f32)),
        (3, (cells & 127).astype(f32)),
        (12, assay[...].astype(f32)),
        *((4 + 2 * k, (pencils[k : k + 1, :] >> 8).astype(f32)) for k in range(TARGETS)),
        *((5 + 2 * k, (pencils[k : k + 1, :] & 255).astype(f32)) for k in range(TARGETS)),
    ):
        listed = jnp.where(part_row == r, line, listed)
    parts[...] = listed.astype(bf16)
    wf[...] = loads[...].astype(f32)
    for k in range(TARGETS):
        weights[:, 128 * k : 128 * k + 128] = wf[pl.ds(k, count, stride=TARGETS), :].astype(bf16)
    room_row = lax.broadcasted_iota(i32, (room, count), 0)
    flag_row = lax.broadcasted_iota(i32, (16, room), 0) == 13

    def pack_measures(n, _):
        hot = jnp.where(room_row + n * room == place, 1.0, 0.0).astype(bf16)
        asend[n] = mm(hot, weights[...]).astype(bf16)
        psend[n] = jnp.where(flag_row, over, mm_t(parts[...], hot)).astype(bf16)
        return 0

    lax.fori_loop(0, NARROW, pack_measures, 0)
    arecv[me_n] = asend[me_n]
    precv[me_n] = psend[me_n]

    def to_narrow(src, dst, sends, recvs, peer, slot):
        return pltpu.make_async_remote_copy(
            src_ref=src.at[peer], dst_ref=dst.at[slot], send_sem=sends.at[peer],
            recv_sem=recvs.at[slot], device_id={"narrow": peer}, device_id_type=MESH,
        )

    def to_wide(peer, slot):
        return pltpu.make_async_remote_copy(
            src_ref=bsend.at[peer], dst_ref=brecv.at[slot], send_sem=b_send.at[peer],
            recv_sem=b_recv.at[slot], device_id={"wide": peer}, device_id_type=MESH,
        )

    a_args = (asend, arecv, a_send, a_recv)
    p_args = (psend, precv, p_send, p_recv)

    def send_measures(i, _):
        peer = lax.rem(me_n + i, NARROW)
        to_narrow(*p_args, peer, me_n).start()
        to_narrow(*a_args, peer, me_n).start()
        return 0

    def recv_measures(i, _):
        peer = lax.rem(me_n + i, NARROW)
        to_narrow(*p_args, peer, peer).wait_recv()
        to_narrow(*a_args, peer, peer).wait_recv()
        return 0

    def sent_measures(i, _):
        peer = lax.rem(me_n + i, NARROW)
        to_narrow(*p_args, peer, peer).wait_send()
        to_narrow(*a_args, peer, peer).wait_send()
        return 0

    def send_groups(i, _):
        to_wide(lax.rem(me_w + i, WIDE), me_w).start()
        return 0

    def recv_groups(i, _):
        peer = lax.rem(me_w + i, WIDE)
        to_wide(peer, peer).wait_recv()
        return 0

    def sent_groups(i, _):
        peer = lax.rem(me_w + i, WIDE)
        to_wide(peer, peer).wait_send()
        return 0

    pl.semaphore_wait(barrier, WIDE - 1 + NARROW - 1)
    lax.fori_loop(1, NARROW, send_measures, 0)

    late = special & (me_n >= 4)
    own_slots = (jnp.where(late, 2, 0), 1)
    mir_slots = (jnp.where(special & (me_n < 4), 2, jnp.where(special, 0, 2)), 3)

    def spectrum_rows(slot, e):
        return halves(spec[pl.ds(slot * 1024 + e, 128, stride=8), :])

    for e in range(8):
        back = (8 - e) % 8
        flip = flips[0 if e == 0 else 1]
        codes = []
        for s in range(SLOTS):
            h, l = spectrum_rows(own_slots[s], e)
            ear[s, e] = mm_t(own2[...], jnp.concatenate([h, l], axis=1))
            h, l = spectrum_rows(mir_slots[s], back)
            gh = mm_t(mir[...], h).astype(bf16)
            gl = mm_t(mir[...], l).astype(bf16)
            v = mm(jnp.concatenate([gh, gl], axis=1), flip)
            q = jnp.round((jnp.log(v) - SPEC_LOW) * SPEC_CODE - 32500.0)
            codes.append(jnp.clip(q, -32767.0, 32767.0))
        vs[e] = pack(codes[0], codes[1])

    v_main = pltpu.make_async_remote_copy(
        src_ref=vs, dst_ref=vr, send_sem=v_send.at[0], recv_sem=v_recv.at[0],
        device_id={"narrow": 7 - me_n}, device_id_type=MESH,
    )
    v_side = pltpu.make_async_remote_copy(
        src_ref=vs.at[:, pl.ds(0, 8), :], dst_ref=vc, send_sem=v_send.at[1], recv_sem=v_recv.at[1],
        device_id={"narrow": lax.rem(8 - me_n, 8)}, device_id_type=MESH,
    )

    alone = (me_n == 0) | (me_n == 4)

    @pl.when(alone)
    def _():
        vc[...] = vs[:, 0:8, :]

    v_main.start()

    @pl.when(jnp.logical_not(alone))
    def _():
        v_side.start()

    def depth(y, _):
        cells = [y * 4 + k for k in range(4)]
        pieces = []
        for k in cells:
            h, l = halves(noise[pl.ds(k, 128, stride=32), :])
            pieces.append(jnp.concatenate([h, h, l], axis=1))
        res = mm_t(tz[...], jnp.concatenate(pieces, axis=0))
        for i, k in enumerate(cells):
            zre[pl.ds(k, 64, stride=32), :] = res[:64, 128 * i : 128 * i + 128]
            zim[pl.ds(k, 64, stride=32), :] = res[64:, 128 * i : 128 * i + 128]
        return 0

    lax.fori_loop(0, 8, depth, 0)

    def code_wide(read, dst, s, w, to):
        re, im = read(w)
        m = tile_max([re[8 * t : 8 * t + 8] for t in range(4)] + [im[8 * t : 8 * t + 8] for t in range(4)])
        code = scale_code(m)
        fac = encode_factor(code)
        for t in range(4):
            sl = slice(8 * t, 8 * t + 8)
            dst[s, to, 8 * t : 8 * t + 8, :] = pack(re[sl] * fac, im[sl] * fac)
        dst[s, to, 32:40, :] = code

    for s in range(SLOTS):
        def read_depth(w, s=s):
            at = rows((s * 32 + w) * 32, 32)
            return zre[at, :], zim[at, :]

        def code_one(w, _, s=s, read=read_depth):
            code_wide(read, ws, s, w, w)
            return 0

        lax.fori_loop(0, WIDE, code_one, 0)
        wr[s, me_w] = ws[s, me_w]
        send_all(wide_copy, WIDE, me_w, w_args, s)

    def second_forward(s, p, q, r):
        def group(g, _):
            dec = [decode_factor(wr[s, 4 * b + g, 32:40, :]) for b in range(8)]
            dec = [jnp.concatenate([d, d], axis=0) for d in dec]
            for t in range(2):
                v = []
                for b in range(8):
                    re, im = unpack(wr[s, 4 * b + g, 16 * t : 16 * t + 16, :])
                    re, im = re * dec[b], im * dec[b]
                    if p is not None:
                        re, im = re * p + im * q, im * r
                    v.append((re, im))
                v = dft8(v, -1)
                at = rows16(g * 32 + 16 * t, 16)
                at_im = rows16(128 + g * 32 + 16 * t, 16)
                for c in range(8):
                    w = v[c] if c == 0 else turn(v[c], tyc[c, at, :], tys[c, at, :], -1)
                    lanes = slice(128 * (c % 2), 128 * (c % 2) + 128)
                    for dst, part in ((at, w[0]), (at_im, w[1])):
                        h, l = halves(part)
                        bh[c // 2, dst, lanes] = h
                        bl[c // 2, dst, lanes] = l
            return 0

        lax.fori_loop(0, 4, group, 0)
        for cp in range(4):
            big[cp] = mm(yf[0], bh[cp]) + mm(yf[1], bh[cp]) + mm(yf[0], bl[cp])

    first_row = lax.broadcasted_iota(i32, (8, 128), 0) == 0

    def code_narrow(s, n):
        tiles = []
        for c in range(8):
            lanes = slice(128 * (c % 2), 128 * (c % 2) + 128)
            for t in range(2):
                tiles.append((
                    big[c // 2, rows(16 * n + 8 * t, 8), lanes],
                    big[c // 2, rows(128 + 16 * n + 8 * t, 8), lanes],
                ))
        code = scale_code(tile_max([x for pair in tiles for x in pair]))
        fac = encode_factor(code)
        for k, (re, im) in enumerate(tiles):
            ns[s, n, 8 * k : 8 * k + 8, :] = pack(re * fac, im * fac)
        ns[s, n, 128:136, :] = code

    for s in range(SLOTS):
        recv_all(wide_copy, WIDE, me_w, w_args, s)
        if s == 0:
            one = jnp.where(special, 0.0, 1.0)
            second_forward(s, 1.0, 0.0, one)

            @pl.when(special)
            def _():
                big2[...] = big[...]
                second_forward(0, 0.0, 1.0, 0.0)
                top = big[0, 0:8, 0:128]
                mid = big[0, 64:72, 0:128]
                big[:, 0:64, :] = big2[:, 0:64, :]
                big[:, 128:192, :] = big2[:, 128:192, :]
                big[0, 128:136, 0:128] = jnp.where(first_row, top, big[0, 128:136, 0:128])
                big[0, 192:200, 0:128] = jnp.where(first_row, mid, big[0, 192:200, 0:128])
                big[0, 64:72, 0:128] = jnp.where(first_row, big2[0, 64:72, 0:128], mid)
        else:
            second_forward(s, None, None, None)

        def code_n(n, _, s=s):
            code_narrow(s, n)
            return 0

        lax.fori_loop(0, NARROW, code_n, 0)
        nr[s, me_n] = ns[s, me_n]
        if s == 1:
            sent_all(narrow_copy, NARROW, me_n, n_args, 0)
        send_all(narrow_copy, NARROW, me_n, n_args, s)


    lax.fori_loop(1, NARROW, recv_measures, 0)
    row = lax.broadcasted_iota(i32, (512, room), 0)
    want = (((row >> 4) << 3) + (row & 7) + 1).astype(f32)
    flags = precv[0].astype(f32)
    for k in range(1, NARROW):
        flags = jnp.maximum(flags, precv[k].astype(f32))
    flags = jnp.max(jnp.where(flag_row, flags, 0.0), axis=1, keepdims=True)
    flags = jnp.max(flags, axis=0, keepdims=True)
    flag_col = lax.broadcasted_iota(i32, (512, 128), 1) == 13
    for q in range(4):
        moved, named = 0.0, 0.0
        for k in range(2):
            key = precv[2 * q + k, 0:1, :].astype(f32)
            match = (((row >> 3) & 1) == k) & (want == key)
            hot = jnp.where(match, 1.0, 0.0).astype(bf16)
            moved = moved + mm(hot, arecv[2 * q + k])
            named = named + mm_t(hot, precv[2 * q + k])
        named = jnp.concatenate([named, jnp.zeros((512, 112), f32)], axis=1)
        named = jnp.where(flag_col, flags, named)
        bsend[:, 16 * q : 16 * q + 16, 0:512] = moved.astype(bf16).reshape(WIDE, 16, 512)
        bsend[:, 16 * q : 16 * q + 16, 512:640] = named.astype(bf16).reshape(WIDE, 16, 128)
    brecv[me_w] = bsend[me_w]
    lax.fori_loop(1, WIDE, send_groups, 0)

    total = 1.0 / (NX * NY * NZ)
    v_main.wait_recv()

    @pl.when(jnp.logical_not(alone))
    def _():
        v_side.wait_recv()

    def decode_spectrum(q):
        return jnp.exp((q + 32500.0) * (1.0 / SPEC_CODE) + SPEC_LOW)

    bsp[...] = jnp.zeros_like(bsp)

    @pl.when(edge)
    def _():
        sigma = jnp.where(me_n == 0, 1.0, -1.0)
        xs, vv = [], []
        for e in range(8):
            xs.append(ear[0, e, 0:8, :])
            vv.append(decode_spectrum(unpack(vc[e])[0]))

        def even(list_of, e):
            h, l = halves(list_of[(8 - e) % 8])
            pair = jnp.concatenate([h, l], axis=1)
            flip = flips[0 if e == 0 else 1]
            return (mm(pair, flip) + list_of[e]) * 0.5

        for e in range(8):
            a, b = even(xs, e), even(vv, e)
            bsp[e, 0:8, :] = jnp.where(first_row, (a - b) * (0.5 * total) * sigma, 0.0)
            big2[0, 8 * e : 8 * e + 8, 0:128] = (a + b) * (0.5 * total)

    for e in range(8):
        m0, m1 = unpack(vr[e])
        s0, s1 = unpack(vc[e])
        for s, m, side in ((0, m0, s0), (1, m1, s1)):
            m, side = decode_spectrum(m), decode_spectrum(side)
            ear_e = ear[s, e]
            lead = jnp.where(first_row, side, m[0:8])
            ear[s, e, 8:128, :] = (ear_e[8:128] + m[8:128]) * (0.5 * total)
            ear[s, e, 0:8, :] = (ear_e[0:8] + lead) * (0.5 * total)

    @pl.when(edge)
    def _():
        for e in range(8):
            ear[0, e, 0:8, :] = jnp.where(
                first_row, big2[0, 8 * e : 8 * e + 8, 0:128], ear[0, e, 0:8, :]
            )

    def first_both(s):
        def decs(n):
            d = decode_factor(nr[s, n, 128:136, :])
            return jnp.concatenate([d, d], axis=0)

        for n in range(8):
            big2[0, 16 * n : 16 * n + 16, 0:128] = decs(n)

        def load(c):
            v = []
            for n in range(8):
                re, im = unpack(nr[s, n, rows16(16 * c, 16), :])
                d = big2[0, 16 * n : 16 * n + 16, 0:128]
                v.append((re * d, im * d))
            return v

        def put(v, at):
            v = dft8(v, -1)
            for e in range(8):
                w = v[e] if e == 0 else turn(v[e], tx[0, e : e + 1, :], tx[1, e : e + 1, :], -1)
                for lanes, part in ((slice(0, 128), w[0]), (slice(128, 256), w[1])):
                    h, l = halves(part)
                    lh[e, at, lanes] = h
                    ll[e, at, lanes] = l

        def block(c, _):
            put(load(c), rows16(16 * c, 16))
            return 0

        lax.fori_loop(0, 8, block, 0)
        if s == 0:
            put([(re, -im) for re, im in load(0)], slice(128, 144))
        count = 144 if s == 0 else 128
        for e in range(8):
            h, l = lh[e, 0:count, :], ll[e, 0:count, :]
            z = mm(h, xf[0]) + mm(h, xf[1]) + mm(l, xf[0])
            fil = jnp.concatenate([ear[s, e], ear[s, e]], axis=1)
            g = z[0:128] * fil
            if s == 0:
                extra = jnp.concatenate([bsp[e], bsp[e]], axis=1)
                g = jnp.concatenate([g[0:16] + z[128:144] * extra, g[16:128]], axis=0)
            h, l = halves(g)
            big[e // 2, 128 * (e % 2) : 128 * (e % 2) + 128, :] = (
                mm(h, xi[0]) + mm(h, xi[1]) + mm(l, xi[0])
            )

        def unblock(c, _):
            v = []
            for e in range(8):
                at = rows16(128 * (e % 2) + 16 * c, 16)
                y = (big[e // 2, at, 0:128], big[e // 2, at, 128:256])
                v.append(y if e == 0 else turn(y, tx[0, e : e + 1, :], tx[1, e : e + 1, :], 1))
            v = dft8(v, 1)
            for n in range(8):
                at = rows16(128 * (n % 2) + 16 * c, 16)
                big2[n // 2, at, 0:128] = v[n][0]
                big2[n // 2, at, 128:256] = v[n][1]
            return 0

        lax.fori_loop(0, 8, unblock, 0)
        for n in range(8):
            base = 128 * (n % 2)
            tiles = [
                (big2[n // 2, base + 8 * k : base + 8 * k + 8, 0:128],
                 big2[n // 2, base + 8 * k : base + 8 * k + 8, 128:256])
                for k in range(16)
            ]
            code = scale_code(tile_max([x for pair in tiles for x in pair]))
            fac = encode_factor(code)
            for k, (re, im) in enumerate(tiles):
                ms[s, n, 8 * k : 8 * k + 8, :] = pack(re * fac, im * fac)
            ms[s, n, 128:136, :] = code

    for s in range(SLOTS):
        recv_all(narrow_copy, NARROW, me_n, n_args, s)
        first_both(s)
        mr[s, me_n] = ms[s, me_n]
        send_all(narrow_copy, NARROW, me_n, m_args, s)

    row16 = lax.broadcasted_iota(i32, (16, 128), 0)

    def second_back(s, part):
        def fill(n, _):
            d = decode_factor(mr[s, n, 128:136, :])
            d = jnp.concatenate([d, d], axis=0)
            if part is not None:
                if part == 0:
                    f = jnp.where(special, jnp.where(n < 4, 2.0, 0.0), 1.0)
                else:
                    f = jnp.where(n < 4, 0.0, 2.0)
                hit = (row16 == 0) & (special & ((n == 0) | (n == 4)))
            for c in range(8):
                re, im = unpack(mr[s, n, 16 * c : 16 * c + 16, :])
                re, im = re * d, im * d
                if part == 0:
                    if c == 0:
                        re, im = jnp.where(hit, re, re * f), jnp.where(hit, 0.0, im * f)
                    else:
                        re, im = re * f, im * f
                elif part == 1:
                    if c == 0:
                        re, im = jnp.where(hit, im, re * f), jnp.where(hit, 0.0, im * f)
                    else:
                        re, im = re * f, im * f
                lanes = slice(128 * (c % 2), 128 * (c % 2) + 128)
                for dst, x in ((rows16(16 * n, 16), re), (rows16(128 + 16 * n, 16), im)):
                    h, l = halves(x)
                    bh[c // 2, dst, lanes] = h
                    bl[c // 2, dst, lanes] = l
            return 0

        lax.fori_loop(0, 8, fill, 0)
        for cp in range(4):
            big[cp] = mm(yi[0], bh[cp]) + mm(yi[1], bh[cp]) + mm(yi[0], bl[cp])

        def spread(t, _):
            v = []
            at = rows16(16 * t, 16)
            for c in range(8):
                lanes = slice(128 * (c % 2), 128 * (c % 2) + 128)
                y = (big[c // 2, at, lanes], big[c // 2, rows16(128 + 16 * t, 16), lanes])
                v.append(y if c == 0 else turn(y, tyc[c, at, :], tys[c, at, :], 1))
            v = dft8(v, 1)
            for b in range(8):
                to = rows16(128 * (b % 2) + 16 * t, 16)
                if part == 1:
                    big2[b // 2, to, 128:256] = v[b][0]
                else:
                    big2[b // 2, to, 0:128] = v[b][0]
                    big2[b // 2, to, 128:256] = v[b][1]
            return 0

        lax.fori_loop(0, 8, spread, 0)

    for s in range(SLOTS):
        recv_all(narrow_copy, NARROW, me_n, m_args, s)
        second_back(s, 0 if s == 0 else None)
        if s == 0:
            @pl.when(special)
            def _():
                second_back(0, 1)

        def read_back(w):
            b = w // 4
            at = rows((b % 2) * 128 + (w % 4) * 32, 32)
            return big2[b // 2, at, 0:128], big2[b // 2, at, 128:256]

        def code_back(w, _, s=s):
            code_wide(read_back, us, s, w, w)
            return 0

        lax.fori_loop(0, WIDE, code_back, 0)
        keep = pltpu.make_async_copy(us.at[s, me_w], out.at[s, me_w], u_recv.at[s, me_w])
        keep.start()
        send_all(wide_copy, WIDE, me_w, u_args, s)

    lax.fori_loop(1, WIDE, recv_groups, 0)
    pltpu.make_async_copy(brecv, got, g_sem.at[0]).start()
    for g in range(16):
        named = jnp.concatenate(
            [brecv[2 * g, :, 512:640], brecv[2 * g + 1, :, 512:640]], axis=0
        )
        listed = jnp.round(mm_t(join[...], named))
        numbers[g] = listed.astype(i32)
        marks = listed if g == 0 else jnp.maximum(marks, listed)
    flag[0, 0] = jnp.max(marks[5:6, :]).astype(i32)
    lax.fori_loop(1, WIDE, sent_groups, 0)
    lax.fori_loop(1, NARROW, sent_measures, 0)
    pltpu.make_async_copy(brecv, got, g_sem.at[0]).wait()

    for s in range(SLOTS):
        pltpu.make_async_copy(us.at[s, me_w], out.at[s, me_w], u_recv.at[s, me_w]).wait()
        recv_all(wide_copy, WIDE, me_w, u_args, s)
        sent_all(wide_copy, WIDE, me_w, w_args, s)
        if s == 1:
            sent_all(narrow_copy, NARROW, me_n, n_args, s)
        sent_all(narrow_copy, NARROW, me_n, m_args, s)
        sent_all(wide_copy, WIDE, me_w, u_args, s)
    v_main.wait_send()

    @pl.when(jnp.logical_not(alone))
    def _():
        v_side.wait_send()


def spectral(noise, spectrum, owner, cell, assay, pencils, loads):
    t = TABLES
    angle = 2 * np.pi * np.arange(8)[:, None] * np.arange(128)[None, :] / 1024
    tyc = np.repeat(np.cos(angle).astype(np.float32)[:, :, None], 128, axis=2)
    tys = np.repeat(np.sin(angle).astype(np.float32)[:, :, None], 128, axis=2)
    vmem = pl.BlockSpec(memory_space=pltpu.VMEM)
    dma = pltpu.SemaphoreType.DMA
    return pl.pallas_call(
        spectral_kernel,
        out_shape=(
            jax.ShapeDtypeStruct((SLOTS, WIDE, 40, 128), i32),
            jax.ShapeDtypeStruct((WIDE, 64, 640), bf16),
            jax.ShapeDtypeStruct((16, 8, 128), i32),
            jax.ShapeDtypeStruct((1, 1), i32),
        ),
        in_specs=[vmem] * 19,
        out_specs=(
            pl.BlockSpec(memory_space=pl.ANY), pl.BlockSpec(memory_space=pl.ANY), vmem,
            pl.BlockSpec(memory_space=pltpu.SMEM),
        ),
        scratch_shapes=[
            pltpu.VMEM((2048, 128), f32),
            pltpu.VMEM((2048, 128), f32),
            pltpu.VMEM((SLOTS, WIDE, 40, 128), i32),
            pltpu.VMEM((SLOTS, WIDE, 40, 128), i32),
            pltpu.VMEM((4, 256, 256), bf16),
            pltpu.VMEM((4, 256, 256), bf16),
            pltpu.VMEM((4, 256, 256), f32),
            pltpu.VMEM((4, 256, 256), f32),
            pltpu.VMEM((SLOTS, NARROW, 136, 128), i32),
            pltpu.VMEM((SLOTS, NARROW, 136, 128), i32),
            pltpu.VMEM((8, 144, 256), bf16),
            pltpu.VMEM((8, 144, 256), bf16),
            pltpu.VMEM((SLOTS, NARROW, 136, 128), i32),
            pltpu.VMEM((SLOTS, NARROW, 136, 128), i32),
            pltpu.VMEM((SLOTS, WIDE, 40, 128), i32),
            pltpu.VMEM((SLOTS, 8, 128, 128), f32),
            pltpu.VMEM((8, 16, 128), f32),
            pltpu.VMEM((8, 128, 128), i32),
            pltpu.VMEM((8, 128, 128), i32),
            pltpu.VMEM((8, 8, 128), i32),
            pltpu.VMEM((2048, 128), f32),
            pltpu.VMEM((512, 512), bf16),
            pltpu.VMEM((16, 512), bf16),
            pltpu.VMEM((NARROW, ROOM, 512), bf16),
            pltpu.VMEM((NARROW, ROOM, 512), bf16),
            pltpu.VMEM((NARROW, 16, ROOM), bf16),
            pltpu.VMEM((NARROW, 16, ROOM), bf16),
            pltpu.VMEM((WIDE, 64, 640), bf16),
            pltpu.VMEM((WIDE, 64, 640), bf16),
            dma((SLOTS, WIDE)), dma((SLOTS, WIDE)),
            dma((SLOTS, NARROW)), dma((SLOTS, NARROW)),
            dma((SLOTS, NARROW)), dma((SLOTS, NARROW)),
            dma((SLOTS, WIDE)), dma((SLOTS, WIDE)),
            dma((2,)), dma((2,)),
            dma((NARROW,)), dma((NARROW,)), dma((NARROW,)), dma((NARROW,)),
            dma((WIDE,)), dma((WIDE,)), dma((1,)),
        ],
        compiler_params=pltpu.CompilerParams(
            collective_id=0, has_side_effects=True, vmem_limit_bytes=56 * 1024 * 1024
        ),
    )(
        noise.reshape(4096, 128), spectrum.reshape(4096, 128), t["tz"], t["yf"], t["yi"],
        t["xf"], t["xi"], tyc, tys, t["tx"], t["own2"], t["mir"], t["flips"],
        owner, cell, assay, pencils, loads, JOIN,
    )


def finish_kernel(numbers, freq, tzi, held, out, gathered, contrib, *accs):
    for acc in accs:
        acc[...] = jnp.zeros_like(acc)

    def depth(g, _):
        for j in range(4):
            y = g * 4 + j
            re, im = unpack(freq[pl.ds(y, 64, stride=40), :])
            d = decode_factor(freq[pl.ds(32 + lax.rem(y, 8), 64, stride=40), :])
            h, l = halves(jnp.concatenate([re * d, im * d], axis=0))
            u = jnp.concatenate([h, h, l], axis=0)
            out[pl.ds(y, 128, stride=32), :] = lax.dot_general(
                u, tzi[...], (((0,), (0,)), ((), ())), preferred_element_type=f32
            )
        return 0

    lax.fori_loop(0, 8, depth, 0)
    groups = numbers.shape[0]

    def gather(g, _):
        for j in range(128):
            gathered[pl.ds(g * 128 + j, 1), :] = out[pl.ds(numbers[g, 0, j], 1), :]
        return 0

    lax.fori_loop(0, groups, gather, 0)
    lane = lax.broadcasted_iota(i32, (128, 128), 1)

    def residual(g, _):
        at = rows16(g * 128, 128)
        depth_at = held[at, 515:516].astype(i32)
        grade = held[at, 524:525].astype(f32)
        value = jnp.sum(jnp.where(lane == depth_at, gathered[at, :], 0.0), axis=1, keepdims=True)
        resid = grade - value
        for k in range(TARGETS):
            contrib[k, at, :] = resid * held[at, 128 * k : 128 * k + 128].astype(f32)
        return 0

    lax.fori_loop(0, groups, residual, 0)

    def scatter(g, _):
        for j in range(128):
            for t in range(TARGETS):
                acc = accs[t + TARGETS * (j % 2)]
                at = pl.ds(numbers[g, 1 + t, j], 1)
                acc[at, :] = acc[at, :] + contrib[t, pl.ds(g * 128 + j, 1), :]
        return 0

    lax.fori_loop(0, groups, scatter, 0)

    def combine(g, _):
        at = rows(g * 64, 64)
        v = out[at, :]
        for acc in accs:
            v = v + acc[at, :]
        out[at, :] = v
        return 0

    lax.fori_loop(0, 64, combine, 0)


def finish(freq, held, numbers):
    vmem = pl.BlockSpec(memory_space=pltpu.VMEM)
    smem = pl.BlockSpec(memory_space=pltpu.SMEM)
    count = held.shape[0] * held.shape[1]
    return pl.pallas_call(
        finish_kernel,
        out_shape=jax.ShapeDtypeStruct((4096, 128), f32),
        in_specs=[smem] + [vmem] * 3,
        out_specs=vmem,
        scratch_shapes=[pltpu.VMEM((count, 128), f32), pltpu.VMEM((TARGETS, count, 128), f32)]
        + [pltpu.VMEM((4096, 128), f32)] * 8,
        compiler_params=pltpu.CompilerParams(vmem_limit_bytes=56 * 1024 * 1024),
    )(numbers, freq.reshape(-1, 128), TABLES["tzi"], held.reshape(count, -1))


def padded(assay, weights, owner, cell, pencils):
    count = owner.shape[0]
    order = jnp.arange(count, dtype=i32)
    earlier = order[:, None] < order[None, :]
    same = jnp.sum(earlier & (owner[:, None] == owner[None, :]), axis=0, dtype=i32)
    row = cell // NZ
    fields = [jnp.zeros((count,), i32), row // 256, row % 256, cell % NZ]
    for k in range(TARGETS):
        fields += [pencils[:, k] // 256, pencils[:, k] % 256]
    fields = [x.astype(bf16) for x in fields] + [assay]
    parts = jnp.zeros((count, 128), bf16).at[:, : len(fields)].set(jnp.stack(fields, axis=1))
    load = jnp.concatenate([weights, parts], axis=1)
    slots = jnp.arange(WIDE * NARROW * 8, dtype=i32)
    hot = (slots[:, None] == (owner * 8 + same)[None, :]).astype(bf16)
    held = jnp.dot(hot, load, preferred_element_type=f32).astype(bf16)
    held = held.reshape(WIDE, NARROW, 8, -1)
    held = lax.all_to_all(held, "wide", split_axis=0, concat_axis=0, tiled=True)
    held = lax.all_to_all(held, "narrow", split_axis=1, concat_axis=1, tiled=True)
    held = held.reshape(WIDE, 64, -1)
    names = held.reshape(WIDE * 64, -1)[:, TARGETS * NZ :].astype(f32)
    numbers = jnp.einsum("fc,gjc->gfj", jnp.asarray(JOIN, f32), names.reshape(16, 128, 128),
                         precision=lax.Precision.HIGHEST)
    return held, jnp.round(numbers).astype(i32)


def local(noise, spectrum, assay, measure_weights, measure_owner, measure_cell, measure_pencils):
    count = measure_owner.shape[1]
    freq, held, numbers, flag = spectral(
        noise, spectrum, measure_owner, measure_cell, assay, measure_pencils[0].T,
        measure_weights.reshape(count * TARGETS, NZ),
    )

    def roomy(_):
        weights = measure_weights[0].reshape(count, TARGETS * NZ)
        more = padded(assay[0], weights, measure_owner[0], measure_cell[0], measure_pencils[0])
        return finish(freq, *more)

    field = lax.cond(flag[0, 0] > 0, roomy, lambda _: finish(freq, held, numbers), 0)
    return field.reshape(noise.shape)


def solution(mesh):
    placed = (
        P("narrow", "wide", None),
        P("wide", None, "narrow"),
        P(("wide", "narrow"), None),
        P(("wide", "narrow"), None, None, None),
        P(("wide", "narrow"), None),
        P(("wide", "narrow"), None),
        P(("wide", "narrow"), None, None),
    )
    return jax.shard_map(
        local, mesh=mesh, in_specs=placed, out_specs=P("narrow", "wide", None), check_vma=False
    )
```

```python
import functools
import math

import jax
import jax.numpy as jnp
import ml_dtypes
import numpy as np
from jax import lax
from jax.experimental import pallas as pl
from jax.experimental.pallas import tpu as pltpu
from jax.sharding import PartitionSpec as P

NX, NY, NZ = 1024, 1024, 128
TARGETS = 4
WIDE, NARROW = 32, 8
SLOTS = 2
MESH = pl.DeviceIdType.MESH
f32, bf16, i32 = jnp.float32, jnp.bfloat16, jnp.int32

LN2 = math.log(2.0)
CODE = 16.0 / LN2
PEAK = 32600.0
TINY = 1e-30
SPEC_LOW = math.log(0.1)
SPEC_CODE = 65000.0 / math.log(85.0)
ROOT_HALF = math.sqrt(0.5)


def split(a):
    high = a.astype(ml_dtypes.bfloat16)
    low = (a - high.astype(np.float64)).astype(ml_dtypes.bfloat16)
    return high, low


def pair_matrix(sign):
    index = np.arange(128)
    angle = 2 * np.pi * (index[:, None] * index[None, :] % 128) / 128
    c, s = np.cos(angle), sign * np.sin(angle)
    return np.block([[c, -s], [s, c]])


def depth_forward():
    kz = 2 * np.arange(32)[None, :] + np.arange(2)[:, None]
    kz = kz.reshape(-1)
    z = np.arange(128)
    angle = 2 * np.pi * (kz[:, None] * z[None, :] % 128) / 128
    re, im = np.cos(angle), -np.sin(angle)
    im[kz == 0] = np.cos(np.pi * z)
    return np.concatenate([re, im], 0)


def depth_inverse():
    kz = (2 * np.arange(32)[None, :] + np.arange(2)[:, None]).reshape(-1)
    z = np.arange(128)
    angle = 2 * np.pi * (kz[:, None] * z[None, :] % 128) / 128
    re, im = 2 * np.cos(angle), -2 * np.sin(angle)
    re[kz == 0] = 1.0
    im[kz == 0] = np.cos(np.pi * z)
    return np.concatenate([re, im], 0)


def make_tables():
    h, l = split(depth_forward())
    tz = np.concatenate([h, l, h], 1)
    h, l = split(depth_inverse())
    tzi = np.concatenate([h, l, h], 0)
    yf = np.stack(split(pair_matrix(-1.0)))
    yi = np.stack(split(pair_matrix(1.0)))
    xf = np.stack(split(pair_matrix(-1.0).T))
    xi = np.stack(split(pair_matrix(1.0).T))
    c = np.arange(8)
    a = np.arange(128)
    angle = 2 * np.pi * c[:, None] * a[None, :] / 1024
    tx = np.stack([np.cos(angle), np.sin(angle)]).astype(np.float32)
    row = np.arange(128)
    lane_of = 8 * (row % 16) + row // 16
    own = np.zeros((128, 128))
    own[row, lane_of] = 1
    mir = np.zeros((128, 128))
    mir[row, (128 - lane_of) % 128] = 1
    own2 = np.concatenate([own, own], 1).astype(ml_dtypes.bfloat16)
    flips = np.zeros((2, 128, 128))
    flips[0, (128 - row) % 128, row] = 1
    flips[1, 127 - row, row] = 1
    flips = np.concatenate([flips, flips], 1).astype(ml_dtypes.bfloat16)
    return dict(
        tz=tz, tzi=tzi, yf=yf, yi=yi, xf=xf, xi=xi, tx=tx, own2=own2,
        mir=mir.astype(ml_dtypes.bfloat16), flips=flips,
    )


TABLES = make_tables()
ROOM = 160


def join_matrix():
    m = np.zeros((8, 128))
    m[0, 1], m[0, 2] = 256, 1
    for k in range(TARGETS):
        m[1 + k, 4 + 2 * k], m[1 + k, 5 + 2 * k] = 256, 1
    m[5, 13] = 1
    return m.astype(ml_dtypes.bfloat16)


JOIN = join_matrix()


def halves(v):
    h = v.astype(bf16)
    return h, (v - h.astype(f32)).astype(bf16)


def times_i(v, sign):
    re, im = v
    return (-im, re) if sign > 0 else (im, -re)


def add(a, b):
    return a[0] + b[0], a[1] + b[1]


def sub(a, b):
    return a[0] - b[0], a[1] - b[1]


def dft4(v, sign):
    s, d = add(v[0], v[2]), sub(v[0], v[2])
    t, u = add(v[1], v[3]), times_i(sub(v[1], v[3]), sign)
    return [add(s, t), add(d, u), sub(s, t), sub(d, u)]


def dft8(v, sign):
    e = dft4(v[0::2], sign)
    o = dft4(v[1::2], sign)
    g = float(sign)
    re, im = o[1]
    o[1] = ((re - g * im) * ROOT_HALF, (im + g * re) * ROOT_HALF)
    o[2] = times_i(o[2], sign)
    re, im = o[3]
    o[3] = ((-re - g * im) * ROOT_HALF, (g * re - im) * ROOT_HALF)
    return [add(e[c], o[c]) for c in range(4)] + [sub(e[c], o[c]) for c in range(4)]


def turn(v, cos, sin, sign):
    re, im = v
    if sign < 0:
        return re * cos + im * sin, im * cos - re * sin
    return re * cos - im * sin, im * cos + re * sin


def scale_code(m):
    return jnp.ceil(jnp.log(jnp.maximum(m, TINY)) * CODE).astype(i32)


def encode_factor(code):
    return jnp.exp(code.astype(f32) * (-1.0 / CODE)) * PEAK


def decode_factor(code):
    return jnp.exp(code.astype(f32) * (1.0 / CODE)) * (1.0 / PEAK)


def pack(re, im):
    a = jnp.round(re).astype(i32)
    b = jnp.round(im).astype(i32)
    return (a << 16) | (b & 0xFFFF)


def unpack(word):
    return (word >> 16).astype(f32), ((word << 16) >> 16).astype(f32)


def tile_max(tiles):
    tiles = [jnp.abs(t) for t in tiles]
    while len(tiles) > 1:
        tiles = [jnp.maximum(a, b) for a, b in zip(tiles[0::2], tiles[1::2])] + (
            tiles[-1:] if len(tiles) % 2 else []
        )
    return tiles[0]


def mm(a, b):
    return jnp.dot(a, b, preferred_element_type=f32)


def mm_t(a, b):
    return lax.dot_general(a, b, (((1,), (1,)), ((), ())), preferred_element_type=f32)


def rows(start, size):
    return pl.ds(pl.multiple_of(start, 8), size)


def rows16(start, size):
    return pl.ds(pl.multiple_of(start, 16), size)


def spectral_kernel(
    noise, spec, tz, yf, yi, xf, xi, tyc, tys, tx, own2, mir, flips, owner, cell, assay, pencils, loads, join,
    out, got, numbers, flag,
    zre, zim, ws, wr, bh, bl, big, big2, ns, nr, lh, ll, ms, mr, us,
    ear, bsp, vs, vr, vc, wf, weights, parts, asend, arecv, psend, precv, bsend, brecv,
    w_send, w_recv, n_send, n_recv, m_send, m_recv, u_send, u_recv, v_send, v_recv,
    a_send, a_recv, p_send, p_recv, b_send, b_recv, g_sem,
):
    me_w = lax.axis_index("wide")
    me_n = lax.axis_index("narrow")
    special = me_w == 0
    edge = special & ((me_n == 0) | (me_n == 4))

    barrier = pltpu.get_barrier_semaphore()

    def greet_wide(i, _):
        pl.semaphore_signal(
            barrier, inc=1, device_id={"wide": lax.rem(me_w + i, WIDE)}, device_id_type=MESH
        )
        return 0

    def greet_narrow(i, _):
        pl.semaphore_signal(
            barrier, inc=1, device_id={"narrow": lax.rem(me_n + i, NARROW)}, device_id_type=MESH
        )
        return 0

    lax.fori_loop(1, WIDE, greet_wide, 0)
    lax.fori_loop(1, NARROW, greet_narrow, 0)

    def wide_copy(src, dst, sends, recvs, s, peer, slot):
        return pltpu.make_async_remote_copy(
            src_ref=src.at[s, peer], dst_ref=dst.at[s, slot], send_sem=sends.at[s, peer],
            recv_sem=recvs.at[s, slot], device_id={"wide": peer}, device_id_type=MESH,
        )

    def narrow_copy(src, dst, sends, recvs, s, peer, slot):
        return pltpu.make_async_remote_copy(
            src_ref=src.at[s, peer], dst_ref=dst.at[s, slot], send_sem=sends.at[s, peer],
            recv_sem=recvs.at[s, slot], device_id={"narrow": peer}, device_id_type=MESH,
        )

    def code_and_send(code, make, count, me, args, s):
        def one(i, _):
            peer = lax.rem(me + i, count)
            code(peer)
            make(*args, s, peer, me).start()
            return 0

        lax.fori_loop(1, count, one, 0)
        code(me)

    def recv_all(make, count, me, args, s):
        def one(i, _):
            peer = lax.rem(me + i, count)
            make(*args, s, peer, peer).wait_recv()
            return 0

        lax.fori_loop(1, count, one, 0)

    def sent_all(make, count, me, args, s):
        def one(i, _):
            peer = lax.rem(me + i, count)
            make(*args, s, peer, peer).wait_send()
            return 0

        lax.fori_loop(1, count, one, 0)

    w_args = (ws, wr, w_send, w_recv)
    n_args = (ns, nr, n_send, n_recv)
    m_args = (ms, mr, m_send, m_recv)
    u_args = (us, out, u_send, u_recv)

    late = special & (me_n >= 4)
    own_slots = (jnp.where(late, 2, 0), 1)
    mir_slots = (jnp.where(special & (me_n < 4), 2, jnp.where(special, 0, 2)), 3)

    def spectrum_rows(slot, e):
        return halves(spec[pl.ds(slot * 1024 + e, 128, stride=8), :])

    for e in range(8):
        back = (8 - e) % 8
        flip = flips[0 if e == 0 else 1]
        codes = []
        for s in range(SLOTS):
            h, l = spectrum_rows(own_slots[s], e)
            ear[s, e] = mm_t(own2[...], jnp.concatenate([h, l], axis=1))
            h, l = spectrum_rows(mir_slots[s], back)
            gh = mm_t(mir[...], h).astype(bf16)
            gl = mm_t(mir[...], l).astype(bf16)
            v = mm(jnp.concatenate([gh, gl], axis=1), flip)
            q = jnp.round((jnp.log(v) - SPEC_LOW) * SPEC_CODE - 32500.0)
            codes.append(jnp.clip(q, -32767.0, 32767.0))
        vs[e] = pack(codes[0], codes[1])

    v_main = pltpu.make_async_remote_copy(
        src_ref=vs, dst_ref=vr, send_sem=v_send.at[0], recv_sem=v_recv.at[0],
        device_id={"narrow": 7 - me_n}, device_id_type=MESH,
    )
    v_side = pltpu.make_async_remote_copy(
        src_ref=vs.at[:, pl.ds(0, 8), :], dst_ref=vc, send_sem=v_send.at[1], recv_sem=v_recv.at[1],
        device_id={"narrow": lax.rem(8 - me_n, 8)}, device_id_type=MESH,
    )

    alone = (me_n == 0) | (me_n == 4)

    @pl.when(alone)
    def _():
        vc[...] = vs[:, 0:8, :]

    room = asend.shape[1]
    count = owner.shape[1]
    owners = owner[...]
    cells = cell[...]
    narrow_of = (owners & 7).astype(f32)
    diagonal = lax.broadcasted_iota(i32, (128, 128), 0) == lax.broadcasted_iota(i32, (128, 128), 1)

    def column(line):
        pieces = []
        for k in range(count // 128):
            piece = jnp.broadcast_to(line[:, 128 * k : 128 * k + 128], (128, 128))
            pieces.append(jnp.sum(jnp.where(diagonal, piece, 0.0), axis=1, keepdims=True))
        return jnp.concatenate(pieces, axis=0)

    earlier = lax.broadcasted_iota(i32, (count, count), 0) < lax.broadcasted_iota(i32, (count, count), 1)

    def before(line):
        match = earlier & (column(line) == line)
        return jnp.sum(jnp.where(match, 1.0, 0.0), axis=0, keepdims=True)

    same = before(owners.astype(f32))
    rank = before(narrow_of)
    place = jnp.where(rank < room, narrow_of * room + rank, -1.0).astype(i32)
    over = jnp.max(jnp.where(rank < room, 0.0, 1.0), axis=1, keepdims=True)
    key = (owners >> 3 << 3).astype(f32) + same + 1.0
    part_row = lax.broadcasted_iota(i32, (16, count), 0)
    listed = jnp.zeros((16, count), f32)
    for r, line in (
        (0, key),
        (1, (cells >> 15).astype(f32)),
        (2, ((cells >> 7) & 255).astype(f32)),
        (3, (cells & 127).astype(f32)),
        (12, assay[...].astype(f32)),
        *((4 + 2 * k, (pencils[k : k + 1, :] >> 8).astype(f32)) for k in range(TARGETS)),
        *((5 + 2 * k, (pencils[k : k + 1, :] & 255).astype(f32)) for k in range(TARGETS)),
    ):
        listed = jnp.where(part_row == r, line, listed)
    parts[...] = listed.astype(bf16)
    wf[...] = loads[...].astype(f32)
    for k in range(TARGETS):
        weights[:, 128 * k : 128 * k + 128] = wf[pl.ds(k, count, stride=TARGETS), :].astype(bf16)
    room_row = lax.broadcasted_iota(i32, (room, count), 0)
    flag_row = lax.broadcasted_iota(i32, (16, room), 0) == 13

    def pack_measures(n, _):
        hot = jnp.where(room_row + n * room == place, 1.0, 0.0).astype(bf16)
        asend[n] = mm(hot, weights[...]).astype(bf16)
        psend[n] = jnp.where(flag_row, over, mm_t(parts[...], hot)).astype(bf16)
        return 0

    lax.fori_loop(0, NARROW, pack_measures, 0)
    arecv[me_n] = asend[me_n]
    precv[me_n] = psend[me_n]

    def to_narrow(src, dst, sends, recvs, peer, slot):
        return pltpu.make_async_remote_copy(
            src_ref=src.at[peer], dst_ref=dst.at[slot], send_sem=sends.at[peer],
            recv_sem=recvs.at[slot], device_id={"narrow": peer}, device_id_type=MESH,
        )

    def to_wide(peer, slot):
        return pltpu.make_async_remote_copy(
            src_ref=bsend.at[peer], dst_ref=brecv.at[slot], send_sem=b_send.at[peer],
            recv_sem=b_recv.at[slot], device_id={"wide": peer}, device_id_type=MESH,
        )

    a_args = (asend, arecv, a_send, a_recv)
    p_args = (psend, precv, p_send, p_recv)

    def send_measures(i, _):
        peer = lax.rem(me_n + i, NARROW)
        to_narrow(*p_args, peer, me_n).start()
        to_narrow(*a_args, peer, me_n).start()
        return 0

    def recv_measures(i, _):
        peer = lax.rem(me_n + i, NARROW)
        to_narrow(*p_args, peer, peer).wait_recv()
        to_narrow(*a_args, peer, peer).wait_recv()
        return 0

    def sent_measures(i, _):
        peer = lax.rem(me_n + i, NARROW)
        to_narrow(*p_args, peer, peer).wait_send()
        to_narrow(*a_args, peer, peer).wait_send()
        return 0

    def send_groups(i, _):
        to_wide(lax.rem(me_w + i, WIDE), me_w).start()
        return 0

    def recv_groups(i, _):
        peer = lax.rem(me_w + i, WIDE)
        to_wide(peer, peer).wait_recv()
        return 0

    def sent_groups(i, _):
        peer = lax.rem(me_w + i, WIDE)
        to_wide(peer, peer).wait_send()
        return 0

    pl.semaphore_wait(barrier, WIDE - 1 + NARROW - 1)
    lax.fori_loop(1, NARROW, send_measures, 0)
    v_main.start()

    @pl.when(jnp.logical_not(alone))
    def _():
        v_side.start()

    def depth(y, _):
        cells = [y * 4 + k for k in range(4)]
        pieces = []
        for k in cells:
            h, l = halves(noise[pl.ds(k, 128, stride=32), :])
            pieces.append(jnp.concatenate([h, h, l], axis=1))
        res = mm_t(tz[...], jnp.concatenate(pieces, axis=0))
        for i, k in enumerate(cells):
            zre[pl.ds(k, 64, stride=32), :] = res[:64, 128 * i : 128 * i + 128]
            zim[pl.ds(k, 64, stride=32), :] = res[64:, 128 * i : 128 * i + 128]
        return 0

    lax.fori_loop(0, 8, depth, 0)

    def code_wide(read, dst, s, w, to):
        re, im = read(w)
        m = tile_max([re[8 * t : 8 * t + 8] for t in range(4)] + [im[8 * t : 8 * t + 8] for t in range(4)])
        code = scale_code(m)
        fac = encode_factor(code)
        for t in range(4):
            sl = slice(8 * t, 8 * t + 8)
            dst[s, to, 8 * t : 8 * t + 8, :] = pack(re[sl] * fac, im[sl] * fac)
        dst[s, to, 32:40, :] = code

    for s in range(SLOTS):
        def read_depth(w, s=s):
            at = rows((s * 32 + w) * 32, 32)
            return zre[at, :], zim[at, :]

        def code_one(w, s=s, read=read_depth):
            code_wide(read, ws, s, w, w)

        code_and_send(code_one, wide_copy, WIDE, me_w, w_args, s)
        wr[s, me_w] = ws[s, me_w]

    def second_forward(s, p, q, r):
        def group(g, _):
            dec = [decode_factor(wr[s, 4 * b + g, 32:40, :]) for b in range(8)]
            dec = [jnp.concatenate([d, d], axis=0) for d in dec]
            for t in range(2):
                v = []
                for b in range(8):
                    re, im = unpack(wr[s, 4 * b + g, 16 * t : 16 * t + 16, :])
                    re, im = re * dec[b], im * dec[b]
                    if p is not None:
                        re, im = re * p + im * q, im * r
                    v.append((re, im))
                v = dft8(v, -1)
                at = rows16(g * 32 + 16 * t, 16)
                at_im = rows16(128 + g * 32 + 16 * t, 16)
                for c in range(8):
                    w = v[c] if c == 0 else turn(v[c], tyc[c, at, :], tys[c, at, :], -1)
                    lanes = slice(128 * (c % 2), 128 * (c % 2) + 128)
                    for dst, part in ((at, w[0]), (at_im, w[1])):
                        h, l = halves(part)
                        bh[c // 2, dst, lanes] = h
                        bl[c // 2, dst, lanes] = l
            return 0

        lax.fori_loop(0, 4, group, 0)
        for cp in range(4):
            big[cp] = mm(yf[0], bh[cp]) + mm(yf[1], bh[cp]) + mm(yf[0], bl[cp])

    first_row = lax.broadcasted_iota(i32, (8, 128), 0) == 0

    def code_narrow(s, n):
        tiles = []
        for c in range(8):
            lanes = slice(128 * (c % 2), 128 * (c % 2) + 128)
            for t in range(2):
                tiles.append((
                    big[c // 2, rows(16 * n + 8 * t, 8), lanes],
                    big[c // 2, rows(128 + 16 * n + 8 * t, 8), lanes],
                ))
        code = scale_code(tile_max([x for pair in tiles for x in pair]))
        fac = encode_factor(code)
        for k, (re, im) in enumerate(tiles):
            ns[s, n, 8 * k : 8 * k + 8, :] = pack(re * fac, im * fac)
        ns[s, n, 128:136, :] = code

    for s in range(SLOTS):
        recv_all(wide_copy, WIDE, me_w, w_args, s)
        if s == 0:
            one = jnp.where(special, 0.0, 1.0)
            second_forward(s, 1.0, 0.0, one)

            @pl.when(special)
            def _():
                big2[...] = big[...]
                second_forward(0, 0.0, 1.0, 0.0)
                top = big[0, 0:8, 0:128]
                mid = big[0, 64:72, 0:128]
                big[:, 0:64, :] = big2[:, 0:64, :]
                big[:, 128:192, :] = big2[:, 128:192, :]
                big[0, 128:136, 0:128] = jnp.where(first_row, top, big[0, 128:136, 0:128])
                big[0, 192:200, 0:128] = jnp.where(first_row, mid, big[0, 192:200, 0:128])
                big[0, 64:72, 0:128] = jnp.where(first_row, big2[0, 64:72, 0:128], mid)
        else:
            second_forward(s, None, None, None)

        code_and_send(functools.partial(code_narrow, s), narrow_copy, NARROW, me_n, n_args, s)
        nr[s, me_n] = ns[s, me_n]


    def regroup():
        lax.fori_loop(1, NARROW, recv_measures, 0)
        row = lax.broadcasted_iota(i32, (512, room), 0)
        want = (((row >> 4) << 3) + (row & 7) + 1).astype(f32)
        flags = precv[0].astype(f32)
        for k in range(1, NARROW):
            flags = jnp.maximum(flags, precv[k].astype(f32))
        flags = jnp.max(jnp.where(flag_row, flags, 0.0), axis=1, keepdims=True)
        flags = jnp.max(flags, axis=0, keepdims=True)
        flag_col = lax.broadcasted_iota(i32, (512, 128), 1) == 13
        for q in range(4):
            moved, named = 0.0, 0.0
            for k in range(2):
                key = precv[2 * q + k, 0:1, :].astype(f32)
                match = (((row >> 3) & 1) == k) & (want == key)
                hot = jnp.where(match, 1.0, 0.0).astype(bf16)
                moved = moved + mm(hot, arecv[2 * q + k])
                named = named + mm_t(hot, precv[2 * q + k])
            named = jnp.concatenate([named, jnp.zeros((512, 112), f32)], axis=1)
            named = jnp.where(flag_col, flags, named)
            bsend[:, 16 * q : 16 * q + 16, 0:512] = moved.astype(bf16).reshape(WIDE, 16, 512)
            bsend[:, 16 * q : 16 * q + 16, 512:640] = named.astype(bf16).reshape(WIDE, 16, 128)
        brecv[me_w] = bsend[me_w]
        lax.fori_loop(1, WIDE, send_groups, 0)

    total = 1.0 / (NX * NY * NZ)
    v_main.wait_recv()

    @pl.when(jnp.logical_not(alone))
    def _():
        v_side.wait_recv()

    def decode_spectrum(q):
        return jnp.exp((q + 32500.0) * (1.0 / SPEC_CODE) + SPEC_LOW)

    bsp[...] = jnp.zeros_like(bsp)

    @pl.when(edge)
    def _():
        sigma = jnp.where(me_n == 0, 1.0, -1.0)
        xs, vv = [], []
        for e in range(8):
            xs.append(ear[0, e, 0:8, :])
            vv.append(decode_spectrum(unpack(vc[e])[0]))

        def even(list_of, e):
            h, l = halves(list_of[(8 - e) % 8])
            pair = jnp.concatenate([h, l], axis=1)
            flip = flips[0 if e == 0 else 1]
            return (mm(pair, flip) + list_of[e]) * 0.5

        for e in range(8):
            a, b = even(xs, e), even(vv, e)
            bsp[e, 0:8, :] = jnp.where(first_row, (a - b) * (0.5 * total) * sigma, 0.0)
            big2[0, 8 * e : 8 * e + 8, 0:128] = (a + b) * (0.5 * total)

    for e in range(8):
        m0, m1 = unpack(vr[e])
        s0, s1 = unpack(vc[e])
        for s, m, side in ((0, m0, s0), (1, m1, s1)):
            m, side = decode_spectrum(m), decode_spectrum(side)
            ear_e = ear[s, e]
            lead = jnp.where(first_row, side, m[0:8])
            ear[s, e, 8:128, :] = (ear_e[8:128] + m[8:128]) * (0.5 * total)
            ear[s, e, 0:8, :] = (ear_e[0:8] + lead) * (0.5 * total)

    @pl.when(edge)
    def _():
        for e in range(8):
            ear[0, e, 0:8, :] = jnp.where(
                first_row, big2[0, 8 * e : 8 * e + 8, 0:128], ear[0, e, 0:8, :]
            )

    def first_both(s):
        def decs(n):
            d = decode_factor(nr[s, n, 128:136, :])
            return jnp.concatenate([d, d], axis=0)

        for n in range(8):
            big2[0, 16 * n : 16 * n + 16, 0:128] = decs(n)

        def load(c):
            v = []
            for n in range(8):
                re, im = unpack(nr[s, n, rows16(16 * c, 16), :])
                d = big2[0, 16 * n : 16 * n + 16, 0:128]
                v.append((re * d, im * d))
            return v

        def put(v, at):
            v = dft8(v, -1)
            for e in range(8):
                w = v[e] if e == 0 else turn(v[e], tx[0, e : e + 1, :], tx[1, e : e + 1, :], -1)
                for lanes, part in ((slice(0, 128), w[0]), (slice(128, 256), w[1])):
                    h, l = halves(part)
                    lh[e, at, lanes] = h
                    ll[e, at, lanes] = l

        def block(c, _):
            put(load(c), rows16(16 * c, 16))
            return 0

        lax.fori_loop(0, 8, block, 0)
        if s == 0:
            put([(re, -im) for re, im in load(0)], slice(128, 144))
        count = 144 if s == 0 else 128
        for e in range(8):
            h, l = lh[e, 0:count, :], ll[e, 0:count, :]
            z = mm(h, xf[0]) + mm(h, xf[1]) + mm(l, xf[0])
            fil = jnp.concatenate([ear[s, e], ear[s, e]], axis=1)
            g = z[0:128] * fil
            if s == 0:
                extra = jnp.concatenate([bsp[e], bsp[e]], axis=1)
                g = jnp.concatenate([g[0:16] + z[128:144] * extra, g[16:128]], axis=0)
            h, l = halves(g)
            big[e // 2, 128 * (e % 2) : 128 * (e % 2) + 128, :] = (
                mm(h, xi[0]) + mm(h, xi[1]) + mm(l, xi[0])
            )

        def unblock(c, _):
            v = []
            for e in range(8):
                at = rows16(128 * (e % 2) + 16 * c, 16)
                y = (big[e // 2, at, 0:128], big[e // 2, at, 128:256])
                v.append(y if e == 0 else turn(y, tx[0, e : e + 1, :], tx[1, e : e + 1, :], 1))
            v = dft8(v, 1)
            for n in range(8):
                at = rows16(128 * (n % 2) + 16 * c, 16)
                big2[n // 2, at, 0:128] = v[n][0]
                big2[n // 2, at, 128:256] = v[n][1]
            return 0

        lax.fori_loop(0, 8, unblock, 0)

    def code_first(s, n):
        page, base = lax.div(n, 2), 128 * lax.rem(n, 2)
        tiles = []
        for k in range(16):
            at = rows(base + 8 * k, 8)
            tiles.append((big2[page, at, 0:128], big2[page, at, 128:256]))
        code = scale_code(tile_max([x for pair in tiles for x in pair]))
        fac = encode_factor(code)
        for k, (re, im) in enumerate(tiles):
            ms[s, n, 8 * k : 8 * k + 8, :] = pack(re * fac, im * fac)
        ms[s, n, 128:136, :] = code

    for s in range(SLOTS):
        recv_all(narrow_copy, NARROW, me_n, n_args, s)
        first_both(s)
        code_and_send(functools.partial(code_first, s), narrow_copy, NARROW, me_n, m_args, s)
        mr[s, me_n] = ms[s, me_n]
        if s == 0:
            regroup()

    row16 = lax.broadcasted_iota(i32, (16, 128), 0)

    def second_back(s, part):
        def fill(n, _):
            d = decode_factor(mr[s, n, 128:136, :])
            d = jnp.concatenate([d, d], axis=0)
            if part is not None:
                if part == 0:
                    f = jnp.where(special, jnp.where(n < 4, 2.0, 0.0), 1.0)
                else:
                    f = jnp.where(n < 4, 0.0, 2.0)
                hit = (row16 == 0) & (special & ((n == 0) | (n == 4)))
            for c in range(8):
                re, im = unpack(mr[s, n, 16 * c : 16 * c + 16, :])
                re, im = re * d, im * d
                if part == 0:
                    if c == 0:
                        re, im = jnp.where(hit, re, re * f), jnp.where(hit, 0.0, im * f)
                    else:
                        re, im = re * f, im * f
                elif part == 1:
                    if c == 0:
                        re, im = jnp.where(hit, im, re * f), jnp.where(hit, 0.0, im * f)
                    else:
                        re, im = re * f, im * f
                lanes = slice(128 * (c % 2), 128 * (c % 2) + 128)
                for dst, x in ((rows16(16 * n, 16), re), (rows16(128 + 16 * n, 16), im)):
                    h, l = halves(x)
                    bh[c // 2, dst, lanes] = h
                    bl[c // 2, dst, lanes] = l
            return 0

        lax.fori_loop(0, 8, fill, 0)
        for cp in range(4):
            big[cp] = mm(yi[0], bh[cp]) + mm(yi[1], bh[cp]) + mm(yi[0], bl[cp])

        def spread(t, _):
            v = []
            at = rows16(16 * t, 16)
            for c in range(8):
                lanes = slice(128 * (c % 2), 128 * (c % 2) + 128)
                y = (big[c // 2, at, lanes], big[c // 2, rows16(128 + 16 * t, 16), lanes])
                v.append(y if c == 0 else turn(y, tyc[c, at, :], tys[c, at, :], 1))
            v = dft8(v, 1)
            for b in range(8):
                to = rows16(128 * (b % 2) + 16 * t, 16)
                if part == 1:
                    big2[b // 2, to, 128:256] = v[b][0]
                else:
                    big2[b // 2, to, 0:128] = v[b][0]
                    big2[b // 2, to, 128:256] = v[b][1]
            return 0

        lax.fori_loop(0, 8, spread, 0)

    for s in range(SLOTS):
        recv_all(narrow_copy, NARROW, me_n, m_args, s)
        second_back(s, 0 if s == 0 else None)
        if s == 0:
            @pl.when(special)
            def _():
                second_back(0, 1)

        def read_back(w):
            b = w // 4
            at = rows((b % 2) * 128 + (w % 4) * 32, 32)
            return big2[b // 2, at, 0:128], big2[b // 2, at, 128:256]

        def code_back(w, s=s):
            code_wide(read_back, us, s, w, w)

        code_and_send(code_back, wide_copy, WIDE, me_w, u_args, s)
        keep = pltpu.make_async_copy(us.at[s, me_w], out.at[s, me_w], u_recv.at[s, me_w])
        keep.start()

    lax.fori_loop(1, WIDE, recv_groups, 0)
    pltpu.make_async_copy(brecv, got, g_sem.at[0]).start()
    for g in range(16):
        named = jnp.concatenate(
            [brecv[2 * g, :, 512:640], brecv[2 * g + 1, :, 512:640]], axis=0
        )
        listed = jnp.round(mm_t(join[...], named))
        numbers[g] = listed.astype(i32)
        marks = listed if g == 0 else jnp.maximum(marks, listed)
    flag[0, 0] = jnp.max(marks[5:6, :]).astype(i32)
    lax.fori_loop(1, WIDE, sent_groups, 0)
    lax.fori_loop(1, NARROW, sent_measures, 0)
    pltpu.make_async_copy(brecv, got, g_sem.at[0]).wait()

    for s in range(SLOTS):
        pltpu.make_async_copy(us.at[s, me_w], out.at[s, me_w], u_recv.at[s, me_w]).wait()
        recv_all(wide_copy, WIDE, me_w, u_args, s)
        sent_all(wide_copy, WIDE, me_w, w_args, s)
        sent_all(narrow_copy, NARROW, me_n, n_args, s)
        sent_all(narrow_copy, NARROW, me_n, m_args, s)
        sent_all(wide_copy, WIDE, me_w, u_args, s)
    v_main.wait_send()

    @pl.when(jnp.logical_not(alone))
    def _():
        v_side.wait_send()


def spectral(noise, spectrum, owner, cell, assay, pencils, loads):
    t = TABLES
    angle = 2 * np.pi * np.arange(8)[:, None] * np.arange(128)[None, :] / 1024
    tyc = np.repeat(np.cos(angle).astype(np.float32)[:, :, None], 128, axis=2)
    tys = np.repeat(np.sin(angle).astype(np.float32)[:, :, None], 128, axis=2)
    vmem = pl.BlockSpec(memory_space=pltpu.VMEM)
    dma = pltpu.SemaphoreType.DMA
    return pl.pallas_call(
        spectral_kernel,
        out_shape=(
            jax.ShapeDtypeStruct((SLOTS, WIDE, 40, 128), i32),
            jax.ShapeDtypeStruct((WIDE, 64, 640), bf16),
            jax.ShapeDtypeStruct((16, 8, 128), i32),
            jax.ShapeDtypeStruct((1, 1), i32),
        ),
        in_specs=[vmem] * 19,
        out_specs=(
            pl.BlockSpec(memory_space=pl.ANY), pl.BlockSpec(memory_space=pl.ANY), vmem,
            pl.BlockSpec(memory_space=pltpu.SMEM),
        ),
        scratch_shapes=[
            pltpu.VMEM((2048, 128), f32),
            pltpu.VMEM((2048, 128), f32),
            pltpu.VMEM((SLOTS, WIDE, 40, 128), i32),
            pltpu.VMEM((SLOTS, WIDE, 40, 128), i32),
            pltpu.VMEM((4, 256, 256), bf16),
            pltpu.VMEM((4, 256, 256), bf16),
            pltpu.VMEM((4, 256, 256), f32),
            pltpu.VMEM((4, 256, 256), f32),
            pltpu.VMEM((SLOTS, NARROW, 136, 128), i32),
            pltpu.VMEM((SLOTS, NARROW, 136, 128), i32),
            pltpu.VMEM((8, 144, 256), bf16),
            pltpu.VMEM((8, 144, 256), bf16),
            pltpu.VMEM((SLOTS, NARROW, 136, 128), i32),
            pltpu.VMEM((SLOTS, NARROW, 136, 128), i32),
            pltpu.VMEM((SLOTS, WIDE, 40, 128), i32),
            pltpu.VMEM((SLOTS, 8, 128, 128), f32),
            pltpu.VMEM((8, 16, 128), f32),
            pltpu.VMEM((8, 128, 128), i32),
            pltpu.VMEM((8, 128, 128), i32),
            pltpu.VMEM((8, 8, 128), i32),
            pltpu.VMEM((2048, 128), f32),
            pltpu.VMEM((512, 512), bf16),
            pltpu.VMEM((16, 512), bf16),
            pltpu.VMEM((NARROW, ROOM, 512), bf16),
            pltpu.VMEM((NARROW, ROOM, 512), bf16),
            pltpu.VMEM((NARROW, 16, ROOM), bf16),
            pltpu.VMEM((NARROW, 16, ROOM), bf16),
            pltpu.VMEM((WIDE, 64, 640), bf16),
            pltpu.VMEM((WIDE, 64, 640), bf16),
            dma((SLOTS, WIDE)), dma((SLOTS, WIDE)),
            dma((SLOTS, NARROW)), dma((SLOTS, NARROW)),
            dma((SLOTS, NARROW)), dma((SLOTS, NARROW)),
            dma((SLOTS, WIDE)), dma((SLOTS, WIDE)),
            dma((2,)), dma((2,)),
            dma((NARROW,)), dma((NARROW,)), dma((NARROW,)), dma((NARROW,)),
            dma((WIDE,)), dma((WIDE,)), dma((1,)),
        ],
        compiler_params=pltpu.CompilerParams(
            collective_id=0, has_side_effects=True, vmem_limit_bytes=56 * 1024 * 1024
        ),
    )(
        noise.reshape(4096, 128), spectrum.reshape(4096, 128), t["tz"], t["yf"], t["yi"],
        t["xf"], t["xi"], tyc, tys, t["tx"], t["own2"], t["mir"], t["flips"],
        owner, cell, assay, pencils, loads, JOIN,
    )


def finish_kernel(numbers, freq, tzi, held, out, gathered, contrib, *accs):
    for acc in accs:
        acc[...] = jnp.zeros_like(acc)

    def depth(g, _):
        for j in range(4):
            y = g * 4 + j
            re, im = unpack(freq[pl.ds(y, 64, stride=40), :])
            d = decode_factor(freq[pl.ds(32 + lax.rem(y, 8), 64, stride=40), :])
            h, l = halves(jnp.concatenate([re * d, im * d], axis=0))
            u = jnp.concatenate([h, h, l], axis=0)
            out[pl.ds(y, 128, stride=32), :] = lax.dot_general(
                u, tzi[...], (((0,), (0,)), ((), ())), preferred_element_type=f32
            )
        return 0

    lax.fori_loop(0, 8, depth, 0)
    groups = numbers.shape[0]

    def gather(g, _):
        for j in range(128):
            gathered[pl.ds(g * 128 + j, 1), :] = out[pl.ds(numbers[g, 0, j], 1), :]
        return 0

    lax.fori_loop(0, groups, gather, 0)
    lane = lax.broadcasted_iota(i32, (128, 128), 1)

    def residual(g, _):
        at = rows16(g * 128, 128)
        depth_at = held[at, 515:516].astype(i32)
        grade = held[at, 524:525].astype(f32)
        value = jnp.sum(jnp.where(lane == depth_at, gathered[at, :], 0.0), axis=1, keepdims=True)
        resid = grade - value
        for k in range(TARGETS):
            contrib[k, at, :] = resid * held[at, 128 * k : 128 * k + 128].astype(f32)
        return 0

    lax.fori_loop(0, groups, residual, 0)

    def scatter(g, _):
        for j in range(128):
            for t in range(TARGETS):
                acc = accs[t + TARGETS * (j % 2)]
                at = pl.ds(numbers[g, 1 + t, j], 1)
                acc[at, :] = acc[at, :] + contrib[t, pl.ds(g * 128 + j, 1), :]
        return 0

    lax.fori_loop(0, groups, scatter, 0)

    def combine(g, _):
        at = rows(g * 64, 64)
        v = out[at, :]
        for acc in accs:
            v = v + acc[at, :]
        out[at, :] = v
        return 0

    lax.fori_loop(0, 64, combine, 0)


def finish(freq, held, numbers):
    vmem = pl.BlockSpec(memory_space=pltpu.VMEM)
    smem = pl.BlockSpec(memory_space=pltpu.SMEM)
    count = held.shape[0] * held.shape[1]
    return pl.pallas_call(
        finish_kernel,
        out_shape=jax.ShapeDtypeStruct((4096, 128), f32),
        in_specs=[smem] + [vmem] * 3,
        out_specs=vmem,
        scratch_shapes=[pltpu.VMEM((count, 128), f32), pltpu.VMEM((TARGETS, count, 128), f32)]
        + [pltpu.VMEM((4096, 128), f32)] * 8,
        compiler_params=pltpu.CompilerParams(vmem_limit_bytes=56 * 1024 * 1024),
    )(numbers, freq.reshape(-1, 128), TABLES["tzi"], held.reshape(count, -1))


def padded(assay, weights, owner, cell, pencils):
    count = owner.shape[0]
    order = jnp.arange(count, dtype=i32)
    earlier = order[:, None] < order[None, :]
    same = jnp.sum(earlier & (owner[:, None] == owner[None, :]), axis=0, dtype=i32)
    row = cell // NZ
    fields = [jnp.zeros((count,), i32), row // 256, row % 256, cell % NZ]
    for k in range(TARGETS):
        fields += [pencils[:, k] // 256, pencils[:, k] % 256]
    fields = [x.astype(bf16) for x in fields] + [assay]
    parts = jnp.zeros((count, 128), bf16).at[:, : len(fields)].set(jnp.stack(fields, axis=1))
    load = jnp.concatenate([weights, parts], axis=1)
    slots = jnp.arange(WIDE * NARROW * 8, dtype=i32)
    hot = (slots[:, None] == (owner * 8 + same)[None, :]).astype(bf16)
    held = jnp.dot(hot, load, preferred_element_type=f32).astype(bf16)
    held = held.reshape(WIDE, NARROW, 8, -1)
    held = lax.all_to_all(held, "wide", split_axis=0, concat_axis=0, tiled=True)
    held = lax.all_to_all(held, "narrow", split_axis=1, concat_axis=1, tiled=True)
    held = held.reshape(WIDE, 64, -1)
    names = held.reshape(WIDE * 64, -1)[:, TARGETS * NZ :].astype(f32)
    numbers = jnp.einsum("fc,gjc->gfj", jnp.asarray(JOIN, f32), names.reshape(16, 128, 128),
                         precision=lax.Precision.HIGHEST)
    return held, jnp.round(numbers).astype(i32)


def local(noise, spectrum, assay, measure_weights, measure_owner, measure_cell, measure_pencils):
    count = measure_owner.shape[1]
    freq, held, numbers, flag = spectral(
        noise, spectrum, measure_owner, measure_cell, assay, measure_pencils[0].T,
        measure_weights.reshape(count * TARGETS, NZ),
    )

    def roomy(_):
        weights = measure_weights[0].reshape(count, TARGETS * NZ)
        more = padded(assay[0], weights, measure_owner[0], measure_cell[0], measure_pencils[0])
        return finish(freq, *more)

    field = lax.cond(flag[0, 0] > 0, roomy, lambda _: finish(freq, held, numbers), 0)
    return field.reshape(noise.shape)


def solution(mesh):
    placed = (
        P("narrow", "wide", None),
        P("wide", None, "narrow"),
        P(("wide", "narrow"), None),
        P(("wide", "narrow"), None, None, None),
        P(("wide", "narrow"), None),
        P(("wide", "narrow"), None),
        P(("wide", "narrow"), None, None),
    )
    return jax.shard_map(
        local, mesh=mesh, in_specs=placed, out_specs=P("narrow", "wide", None), check_vma=False
    )
```

```python
import functools
import math

import jax
import jax.numpy as jnp
import ml_dtypes
import numpy as np
from jax import lax
from jax.experimental import pallas as pl
from jax.experimental.pallas import tpu as pltpu
from jax.sharding import PartitionSpec as P

NX, NY, NZ = 1024, 1024, 128
TARGETS = 4
WIDE, NARROW = 32, 8
SLOTS = 2
MESH = pl.DeviceIdType.MESH
f32, bf16, i32 = jnp.float32, jnp.bfloat16, jnp.int32

LN2 = math.log(2.0)
CODE = 16.0 / LN2
PEAK = 32600.0
TINY = 1e-30
SPEC_LOW = math.log(0.1)
SPEC_CODE = 65000.0 / math.log(85.0)
ROOT_HALF = math.sqrt(0.5)


def split(a):
    high = a.astype(ml_dtypes.bfloat16)
    low = (a - high.astype(np.float64)).astype(ml_dtypes.bfloat16)
    return high, low


def pair_matrix(sign):
    index = np.arange(128)
    angle = 2 * np.pi * (index[:, None] * index[None, :] % 128) / 128
    c, s = np.cos(angle), sign * np.sin(angle)
    return np.block([[c, -s], [s, c]])


def depth_forward():
    kz = 2 * np.arange(32)[None, :] + np.arange(2)[:, None]
    kz = kz.reshape(-1)
    z = np.arange(128)
    angle = 2 * np.pi * (kz[:, None] * z[None, :] % 128) / 128
    re, im = np.cos(angle), -np.sin(angle)
    im[kz == 0] = np.cos(np.pi * z)
    return np.concatenate([re, im], 0)


def depth_inverse():
    kz = (2 * np.arange(32)[None, :] + np.arange(2)[:, None]).reshape(-1)
    z = np.arange(128)
    angle = 2 * np.pi * (kz[:, None] * z[None, :] % 128) / 128
    re, im = 2 * np.cos(angle), -2 * np.sin(angle)
    re[kz == 0] = 1.0
    im[kz == 0] = np.cos(np.pi * z)
    return np.concatenate([re, im], 0)


def make_tables():
    h, l = split(depth_forward())
    tz = np.concatenate([h, l, h], 1)
    h, l = split(depth_inverse())
    tzi = np.concatenate([h, l, h], 0)
    yf = np.stack(split(pair_matrix(-1.0)))
    yi = np.stack(split(pair_matrix(1.0)))
    xf = np.stack(split(pair_matrix(-1.0).T))
    xi = np.stack(split(pair_matrix(1.0).T))
    c = np.arange(8)
    a = np.arange(128)
    angle = 2 * np.pi * c[:, None] * a[None, :] / 1024
    tx = np.stack([np.cos(angle), np.sin(angle)]).astype(np.float32)
    row = np.arange(128)
    lane_of = 8 * (row % 16) + row // 16
    own = np.zeros((128, 128))
    own[row, lane_of] = 1
    mir = np.zeros((128, 128))
    mir[row, (128 - lane_of) % 128] = 1
    own2 = np.concatenate([own, own], 1).astype(ml_dtypes.bfloat16)
    flips = np.zeros((2, 128, 128))
    flips[0, (128 - row) % 128, row] = 1
    flips[1, 127 - row, row] = 1
    flips = np.concatenate([flips, flips], 1).astype(ml_dtypes.bfloat16)
    return dict(
        tz=tz, tzi=tzi, yf=yf, yi=yi, xf=xf, xi=xi, tx=tx, own2=own2,
        mir=mir.astype(ml_dtypes.bfloat16), flips=flips,
    )


TABLES = make_tables()
ROOM = 160


def join_matrix():
    m = np.zeros((8, 128))
    m[0, 1], m[0, 2] = 256, 1
    for k in range(TARGETS):
        m[1 + k, 4 + 2 * k], m[1 + k, 5 + 2 * k] = 256, 1
    m[5, 13] = 1
    return m.astype(ml_dtypes.bfloat16)


JOIN = join_matrix()


def halves(v):
    h = v.astype(bf16)
    return h, (v - h.astype(f32)).astype(bf16)


def times_i(v, sign):
    re, im = v
    return (-im, re) if sign > 0 else (im, -re)


def add(a, b):
    return a[0] + b[0], a[1] + b[1]


def sub(a, b):
    return a[0] - b[0], a[1] - b[1]


def dft4(v, sign):
    s, d = add(v[0], v[2]), sub(v[0], v[2])
    t, u = add(v[1], v[3]), times_i(sub(v[1], v[3]), sign)
    return [add(s, t), add(d, u), sub(s, t), sub(d, u)]


def dft8(v, sign):
    e = dft4(v[0::2], sign)
    o = dft4(v[1::2], sign)
    g = float(sign)
    re, im = o[1]
    o[1] = ((re - g * im) * ROOT_HALF, (im + g * re) * ROOT_HALF)
    o[2] = times_i(o[2], sign)
    re, im = o[3]
    o[3] = ((-re - g * im) * ROOT_HALF, (g * re - im) * ROOT_HALF)
    return [add(e[c], o[c]) for c in range(4)] + [sub(e[c], o[c]) for c in range(4)]


def turn(v, cos, sin, sign):
    re, im = v
    if sign < 0:
        return re * cos + im * sin, im * cos - re * sin
    return re * cos - im * sin, im * cos + re * sin


def scale_code(m):
    return jnp.ceil(jnp.log(jnp.maximum(m, TINY)) * CODE).astype(i32)


def encode_factor(code):
    return jnp.exp(code.astype(f32) * (-1.0 / CODE)) * PEAK


def decode_factor(code):
    return jnp.exp(code.astype(f32) * (1.0 / CODE)) * (1.0 / PEAK)


def pack(re, im):
    a = jnp.round(re).astype(i32)
    b = jnp.round(im).astype(i32)
    return (a << 16) | (b & 0xFFFF)


def unpack(word):
    return (word >> 16).astype(f32), ((word << 16) >> 16).astype(f32)


def tile_max(tiles):
    tiles = [jnp.abs(t) for t in tiles]
    while len(tiles) > 1:
        tiles = [jnp.maximum(a, b) for a, b in zip(tiles[0::2], tiles[1::2])] + (
            tiles[-1:] if len(tiles) % 2 else []
        )
    return tiles[0]


def mm(a, b):
    return jnp.dot(a, b, preferred_element_type=f32)


def mm_t(a, b):
    return lax.dot_general(a, b, (((1,), (1,)), ((), ())), preferred_element_type=f32)


def rows(start, size):
    return pl.ds(pl.multiple_of(start, 8), size)


def rows16(start, size):
    return pl.ds(pl.multiple_of(start, 16), size)


def spectral_kernel(
    noise, spec, tz, yf, yi, xf, xi, tyc, tys, tx, own2, mir, flips, owner, cell, assay, pencils, loads, join,
    out, got, numbers, flag,
    zre, zim, ws, wr, bh, bl, big, big2, ns, nr, lh, ll, ms, mr, us,
    ear, bsp, vs, vr, vc, wf, weights, parts, asend, arecv, psend, precv, bsend, brecv,
    w_send, w_recv, n_send, n_recv, m_send, m_recv, u_send, u_recv, v_send, v_recv,
    a_send, a_recv, p_send, p_recv, b_send, b_recv, g_sem,
):
    me_w = lax.axis_index("wide")
    me_n = lax.axis_index("narrow")
    special = me_w == 0
    edge = special & ((me_n == 0) | (me_n == 4))

    barrier = pltpu.get_barrier_semaphore()

    def greet_wide(i, _):
        pl.semaphore_signal(
            barrier, inc=1, device_id={"wide": lax.rem(me_w + i, WIDE)}, device_id_type=MESH
        )
        return 0

    def greet_narrow(i, _):
        pl.semaphore_signal(
            barrier, inc=1, device_id={"narrow": lax.rem(me_n + i, NARROW)}, device_id_type=MESH
        )
        return 0

    lax.fori_loop(1, WIDE, greet_wide, 0)
    lax.fori_loop(1, NARROW, greet_narrow, 0)

    def wide_copy(src, dst, sends, recvs, s, peer, slot):
        return pltpu.make_async_remote_copy(
            src_ref=src.at[s, peer], dst_ref=dst.at[s, slot], send_sem=sends.at[s, peer],
            recv_sem=recvs.at[s, slot], device_id={"wide": peer}, device_id_type=MESH,
        )

    def narrow_copy(src, dst, sends, recvs, s, peer, slot):
        return pltpu.make_async_remote_copy(
            src_ref=src.at[s, peer], dst_ref=dst.at[s, slot], send_sem=sends.at[s, peer],
            recv_sem=recvs.at[s, slot], device_id={"narrow": peer}, device_id_type=MESH,
        )

    def code_and_send(code, make, count, me, args, s):
        def one(i, _):
            peer = lax.rem(me + i, count)
            code(peer)
            make(*args, s, peer, me).start()
            return 0

        lax.fori_loop(1, count, one, 0)
        code(me)

    def recv_all(make, count, me, args, s):
        def one(i, _):
            peer = lax.rem(me + i, count)
            make(*args, s, peer, peer).wait_recv()
            return 0

        lax.fori_loop(1, count, one, 0)

    def sent_all(make, count, me, args, s):
        def one(i, _):
            peer = lax.rem(me + i, count)
            make(*args, s, peer, peer).wait_send()
            return 0

        lax.fori_loop(1, count, one, 0)

    w_args = (ws, wr, w_send, w_recv)
    n_args = (ns, nr, n_send, n_recv)
    m_args = (ms, mr, m_send, m_recv)
    u_args = (us, out, u_send, u_recv)

    late = special & (me_n >= 4)
    own_slots = (jnp.where(late, 2, 0), 1)
    mir_slots = (jnp.where(special & (me_n < 4), 2, jnp.where(special, 0, 2)), 3)

    def spectrum_rows(slot, e):
        return halves(spec[pl.ds(slot * 1024 + e, 128, stride=8), :])

    for e in range(8):
        back = (8 - e) % 8
        flip = flips[0 if e == 0 else 1]
        codes = []
        for s in range(SLOTS):
            h, l = spectrum_rows(own_slots[s], e)
            ear[s, e] = mm_t(own2[...], jnp.concatenate([h, l], axis=1))
            h, l = spectrum_rows(mir_slots[s], back)
            gh = mm_t(mir[...], h).astype(bf16)
            gl = mm_t(mir[...], l).astype(bf16)
            v = mm(jnp.concatenate([gh, gl], axis=1), flip)
            q = jnp.round((jnp.log(v) - SPEC_LOW) * SPEC_CODE - 32500.0)
            codes.append(jnp.clip(q, -32767.0, 32767.0))
        vs[e] = pack(codes[0], codes[1])

    v_main = pltpu.make_async_remote_copy(
        src_ref=vs, dst_ref=vr, send_sem=v_send.at[0], recv_sem=v_recv.at[0],
        device_id={"narrow": 7 - me_n}, device_id_type=MESH,
    )
    v_side = pltpu.make_async_remote_copy(
        src_ref=vs.at[:, pl.ds(0, 8), :], dst_ref=vc, send_sem=v_send.at[1], recv_sem=v_recv.at[1],
        device_id={"narrow": lax.rem(8 - me_n, 8)}, device_id_type=MESH,
    )

    alone = (me_n == 0) | (me_n == 4)

    @pl.when(alone)
    def _():
        vc[...] = vs[:, 0:8, :]

    room = asend.shape[1]
    count = owner.shape[1]
    owners = owner[...]
    cells = cell[...]
    narrow_of = (owners & 7).astype(f32)
    diagonal = lax.broadcasted_iota(i32, (128, 128), 0) == lax.broadcasted_iota(i32, (128, 128), 1)

    def column(line):
        pieces = []
        for k in range(count // 128):
            piece = jnp.broadcast_to(line[:, 128 * k : 128 * k + 128], (128, 128))
            pieces.append(jnp.sum(jnp.where(diagonal, piece, 0.0), axis=1, keepdims=True))
        return jnp.concatenate(pieces, axis=0)

    earlier = lax.broadcasted_iota(i32, (count, count), 0) < lax.broadcasted_iota(i32, (count, count), 1)

    def before(line):
        match = earlier & (column(line) == line)
        return jnp.sum(jnp.where(match, 1.0, 0.0), axis=0, keepdims=True)

    same = before(owners.astype(f32))
    rank = before(narrow_of)
    place = jnp.where(rank < room, narrow_of * room + rank, -1.0).astype(i32)
    over = jnp.max(jnp.where(rank < room, 0.0, 1.0), axis=1, keepdims=True)
    key = (owners >> 3 << 3).astype(f32) + same + 1.0
    part_row = lax.broadcasted_iota(i32, (16, count), 0)
    listed = jnp.zeros((16, count), f32)
    for r, line in (
        (0, key),
        (1, (cells >> 15).astype(f32)),
        (2, ((cells >> 7) & 255).astype(f32)),
        (3, (cells & 127).astype(f32)),
        (12, assay[...].astype(f32)),
        *((4 + 2 * k, (pencils[k : k + 1, :] >> 8).astype(f32)) for k in range(TARGETS)),
        *((5 + 2 * k, (pencils[k : k + 1, :] & 255).astype(f32)) for k in range(TARGETS)),
    ):
        listed = jnp.where(part_row == r, line, listed)
    parts[...] = listed.astype(bf16)
    wf[...] = loads[...].astype(f32)
    for k in range(TARGETS):
        weights[:, 128 * k : 128 * k + 128] = wf[pl.ds(k, count, stride=TARGETS), :].astype(bf16)
    room_row = lax.broadcasted_iota(i32, (room, count), 0)
    flag_row = lax.broadcasted_iota(i32, (16, room), 0) == 13

    def pack_measures(n, _):
        hot = jnp.where(room_row + n * room == place, 1.0, 0.0).astype(bf16)
        asend[n] = mm(hot, weights[...]).astype(bf16)
        psend[n] = jnp.where(flag_row, over, mm_t(parts[...], hot)).astype(bf16)
        return 0

    lax.fori_loop(0, NARROW, pack_measures, 0)
    arecv[me_n] = asend[me_n]
    precv[me_n] = psend[me_n]

    def to_narrow(src, dst, sends, recvs, peer, slot):
        return pltpu.make_async_remote_copy(
            src_ref=src.at[peer], dst_ref=dst.at[slot], send_sem=sends.at[peer],
            recv_sem=recvs.at[slot], device_id={"narrow": peer}, device_id_type=MESH,
        )

    def to_wide(peer, slot):
        return pltpu.make_async_remote_copy(
            src_ref=bsend.at[peer], dst_ref=brecv.at[slot], send_sem=b_send.at[peer],
            recv_sem=b_recv.at[slot], device_id={"wide": peer}, device_id_type=MESH,
        )

    a_args = (asend, arecv, a_send, a_recv)
    p_args = (psend, precv, p_send, p_recv)

    def send_measures(i, _):
        peer = lax.rem(me_n + i, NARROW)
        to_narrow(*p_args, peer, me_n).start()
        to_narrow(*a_args, peer, me_n).start()
        return 0

    def recv_measures(i, _):
        peer = lax.rem(me_n + i, NARROW)
        to_narrow(*p_args, peer, peer).wait_recv()
        to_narrow(*a_args, peer, peer).wait_recv()
        return 0

    def sent_measures(i, _):
        peer = lax.rem(me_n + i, NARROW)
        to_narrow(*p_args, peer, peer).wait_send()
        to_narrow(*a_args, peer, peer).wait_send()
        return 0

    def send_groups(i, _):
        to_wide(lax.rem(me_w + i, WIDE), me_w).start()
        return 0

    def recv_groups(i, _):
        peer = lax.rem(me_w + i, WIDE)
        to_wide(peer, peer).wait_recv()
        return 0

    def sent_groups(i, _):
        peer = lax.rem(me_w + i, WIDE)
        to_wide(peer, peer).wait_send()
        return 0

    pl.semaphore_wait(barrier, WIDE - 1 + NARROW - 1)
    lax.fori_loop(1, NARROW, send_measures, 0)
    v_main.start()

    @pl.when(jnp.logical_not(alone))
    def _():
        v_side.start()

    def depth(y, _):
        cells = [y * 4 + k for k in range(4)]
        pieces = []
        for k in cells:
            h, l = halves(noise[pl.ds(k, 128, stride=32), :])
            pieces.append(jnp.concatenate([h, h, l], axis=1))
        res = mm_t(tz[...], jnp.concatenate(pieces, axis=0))
        for i, k in enumerate(cells):
            zre[pl.ds(k, 64, stride=32), :] = res[:64, 128 * i : 128 * i + 128]
            zim[pl.ds(k, 64, stride=32), :] = res[64:, 128 * i : 128 * i + 128]
        return 0

    lax.fori_loop(0, 8, depth, 0)

    def code_wide(read, dst, s, w, to):
        re, im = read(w)
        m = tile_max([re[8 * t : 8 * t + 8] for t in range(4)] + [im[8 * t : 8 * t + 8] for t in range(4)])
        code = scale_code(m)
        fac = encode_factor(code)
        for t in range(4):
            sl = slice(8 * t, 8 * t + 8)
            dst[s, to, 8 * t : 8 * t + 8, :] = pack(re[sl] * fac, im[sl] * fac)
        dst[s, to, 32:40, :] = code

    for s in range(SLOTS):
        def read_depth(w, s=s):
            at = rows((s * 32 + w) * 32, 32)
            return zre[at, :], zim[at, :]

        def code_one(w, s=s, read=read_depth):
            code_wide(read, ws, s, w, w)

        code_and_send(code_one, wide_copy, WIDE, me_w, w_args, s)
        wr[s, me_w] = ws[s, me_w]

    def second_forward(s, p, q, r):
        def group(g, _):
            dec = [decode_factor(wr[s, 4 * b + g, 32:40, :]) for b in range(8)]
            dec = [jnp.concatenate([d, d], axis=0) for d in dec]
            for t in range(2):
                v = []
                for b in range(8):
                    re, im = unpack(wr[s, 4 * b + g, 16 * t : 16 * t + 16, :])
                    re, im = re * dec[b], im * dec[b]
                    if p is not None:
                        re, im = re * p + im * q, im * r
                    v.append((re, im))
                v = dft8(v, -1)
                at = rows16(g * 32 + 16 * t, 16)
                at_im = rows16(128 + g * 32 + 16 * t, 16)
                for c in range(8):
                    w = v[c] if c == 0 else turn(v[c], tyc[c, at, :], tys[c, at, :], -1)
                    lanes = slice(128 * (c % 2), 128 * (c % 2) + 128)
                    for dst, part in ((at, w[0]), (at_im, w[1])):
                        h, l = halves(part)
                        bh[c // 2, dst, lanes] = h
                        bl[c // 2, dst, lanes] = l
            return 0

        lax.fori_loop(0, 4, group, 0)
        for cp in range(4):
            big[cp] = mm(yf[0], bh[cp]) + mm(yf[1], bh[cp]) + mm(yf[0], bl[cp])

    first_row = lax.broadcasted_iota(i32, (8, 128), 0) == 0

    def code_narrow(s, n):
        tiles = []
        for c in range(8):
            lanes = slice(128 * (c % 2), 128 * (c % 2) + 128)
            for t in range(2):
                tiles.append((
                    big[c // 2, rows(16 * n + 8 * t, 8), lanes],
                    big[c // 2, rows(128 + 16 * n + 8 * t, 8), lanes],
                ))
        code = scale_code(tile_max([x for pair in tiles for x in pair]))
        fac = encode_factor(code)
        for k, (re, im) in enumerate(tiles):
            ns[s, n, 8 * k : 8 * k + 8, :] = pack(re * fac, im * fac)
        ns[s, n, 128:136, :] = code

    for s in range(SLOTS):
        recv_all(wide_copy, WIDE, me_w, w_args, s)
        if s == 0:
            one = jnp.where(special, 0.0, 1.0)
            second_forward(s, 1.0, 0.0, one)

            @pl.when(special)
            def _():
                big2[...] = big[...]
                second_forward(0, 0.0, 1.0, 0.0)
                top = big[0, 0:8, 0:128]
                mid = big[0, 64:72, 0:128]
                big[:, 0:64, :] = big2[:, 0:64, :]
                big[:, 128:192, :] = big2[:, 128:192, :]
                big[0, 128:136, 0:128] = jnp.where(first_row, top, big[0, 128:136, 0:128])
                big[0, 192:200, 0:128] = jnp.where(first_row, mid, big[0, 192:200, 0:128])
                big[0, 64:72, 0:128] = jnp.where(first_row, big2[0, 64:72, 0:128], mid)
        else:
            second_forward(s, None, None, None)

        code_and_send(functools.partial(code_narrow, s), narrow_copy, NARROW, me_n, n_args, s)
        nr[s, me_n] = ns[s, me_n]


    def regroup():
        lax.fori_loop(1, NARROW, recv_measures, 0)
        row = lax.broadcasted_iota(i32, (512, room), 0)
        want = (((row >> 4) << 3) + (row & 7) + 1).astype(f32)
        flags = precv[0].astype(f32)
        for k in range(1, NARROW):
            flags = jnp.maximum(flags, precv[k].astype(f32))
        flags = jnp.max(jnp.where(flag_row, flags, 0.0), axis=1, keepdims=True)
        flags = jnp.max(flags, axis=0, keepdims=True)
        flag_col = lax.broadcasted_iota(i32, (512, 128), 1) == 13
        for q in range(4):
            moved, named = 0.0, 0.0
            for k in range(2):
                key = precv[2 * q + k, 0:1, :].astype(f32)
                match = (((row >> 3) & 1) == k) & (want == key)
                hot = jnp.where(match, 1.0, 0.0).astype(bf16)
                moved = moved + mm(hot, arecv[2 * q + k])
                named = named + mm_t(hot, precv[2 * q + k])
            named = jnp.concatenate([named, jnp.zeros((512, 112), f32)], axis=1)
            named = jnp.where(flag_col, flags, named)
            bsend[:, 16 * q : 16 * q + 16, 0:512] = moved.astype(bf16).reshape(WIDE, 16, 512)
            bsend[:, 16 * q : 16 * q + 16, 512:640] = named.astype(bf16).reshape(WIDE, 16, 128)
        brecv[me_w] = bsend[me_w]
        lax.fori_loop(1, WIDE, send_groups, 0)

    regroup()

    total = 1.0 / (NX * NY * NZ)
    v_main.wait_recv()

    @pl.when(jnp.logical_not(alone))
    def _():
        v_side.wait_recv()

    def decode_spectrum(q):
        return jnp.exp((q + 32500.0) * (1.0 / SPEC_CODE) + SPEC_LOW)

    bsp[...] = jnp.zeros_like(bsp)

    @pl.when(edge)
    def _():
        sigma = jnp.where(me_n == 0, 1.0, -1.0)
        xs, vv = [], []
        for e in range(8):
            xs.append(ear[0, e, 0:8, :])
            vv.append(decode_spectrum(unpack(vc[e])[0]))

        def even(list_of, e):
            h, l = halves(list_of[(8 - e) % 8])
            pair = jnp.concatenate([h, l], axis=1)
            flip = flips[0 if e == 0 else 1]
            return (mm(pair, flip) + list_of[e]) * 0.5

        for e in range(8):
            a, b = even(xs, e), even(vv, e)
            bsp[e, 0:8, :] = jnp.where(first_row, (a - b) * (0.5 * total) * sigma, 0.0)
            big2[0, 8 * e : 8 * e + 8, 0:128] = (a + b) * (0.5 * total)

    for e in range(8):
        m0, m1 = unpack(vr[e])
        s0, s1 = unpack(vc[e])
        for s, m, side in ((0, m0, s0), (1, m1, s1)):
            m, side = decode_spectrum(m), decode_spectrum(side)
            ear_e = ear[s, e]
            lead = jnp.where(first_row, side, m[0:8])
            ear[s, e, 8:128, :] = (ear_e[8:128] + m[8:128]) * (0.5 * total)
            ear[s, e, 0:8, :] = (ear_e[0:8] + lead) * (0.5 * total)

    @pl.when(edge)
    def _():
        for e in range(8):
            ear[0, e, 0:8, :] = jnp.where(
                first_row, big2[0, 8 * e : 8 * e + 8, 0:128], ear[0, e, 0:8, :]
            )

    def first_both(s):
        def decs(n):
            d = decode_factor(nr[s, n, 128:136, :])
            return jnp.concatenate([d, d], axis=0)

        for n in range(8):
            big2[0, 16 * n : 16 * n + 16, 0:128] = decs(n)

        def load(c):
            v = []
            for n in range(8):
                re, im = unpack(nr[s, n, rows16(16 * c, 16), :])
                d = big2[0, 16 * n : 16 * n + 16, 0:128]
                v.append((re * d, im * d))
            return v

        def put(v, at):
            v = dft8(v, -1)
            for e in range(8):
                w = v[e] if e == 0 else turn(v[e], tx[0, e : e + 1, :], tx[1, e : e + 1, :], -1)
                for lanes, part in ((slice(0, 128), w[0]), (slice(128, 256), w[1])):
                    h, l = halves(part)
                    lh[e, at, lanes] = h
                    ll[e, at, lanes] = l

        def block(c, _):
            put(load(c), rows16(16 * c, 16))
            return 0

        lax.fori_loop(0, 8, block, 0)
        if s == 0:
            put([(re, -im) for re, im in load(0)], slice(128, 144))
        count = 144 if s == 0 else 128
        for e in range(8):
            h, l = lh[e, 0:count, :], ll[e, 0:count, :]
            z = mm(h, xf[0]) + mm(h, xf[1]) + mm(l, xf[0])
            fil = jnp.concatenate([ear[s, e], ear[s, e]], axis=1)
            g = z[0:128] * fil
            if s == 0:
                extra = jnp.concatenate([bsp[e], bsp[e]], axis=1)
                g = jnp.concatenate([g[0:16] + z[128:144] * extra, g[16:128]], axis=0)
            h, l = halves(g)
            big[e // 2, 128 * (e % 2) : 128 * (e % 2) + 128, :] = (
                mm(h, xi[0]) + mm(h, xi[1]) + mm(l, xi[0])
            )

        def unblock(c, _):
            v = []
            for e in range(8):
                at = rows16(128 * (e % 2) + 16 * c, 16)
                y = (big[e // 2, at, 0:128], big[e // 2, at, 128:256])
                v.append(y if e == 0 else turn(y, tx[0, e : e + 1, :], tx[1, e : e + 1, :], 1))
            v = dft8(v, 1)
            for n in range(8):
                at = rows16(128 * (n % 2) + 16 * c, 16)
                big2[n // 2, at, 0:128] = v[n][0]
                big2[n // 2, at, 128:256] = v[n][1]
            return 0

        lax.fori_loop(0, 8, unblock, 0)

    def code_first(s, n):
        page, base = lax.div(n, 2), 128 * lax.rem(n, 2)
        tiles = []
        for k in range(16):
            at = rows(base + 8 * k, 8)
            tiles.append((big2[page, at, 0:128], big2[page, at, 128:256]))
        code = scale_code(tile_max([x for pair in tiles for x in pair]))
        fac = encode_factor(code)
        for k, (re, im) in enumerate(tiles):
            ms[s, n, 8 * k : 8 * k + 8, :] = pack(re * fac, im * fac)
        ms[s, n, 128:136, :] = code

    for s in range(SLOTS):
        recv_all(narrow_copy, NARROW, me_n, n_args, s)
        first_both(s)
        code_and_send(functools.partial(code_first, s), narrow_copy, NARROW, me_n, m_args, s)
        mr[s, me_n] = ms[s, me_n]

    row16 = lax.broadcasted_iota(i32, (16, 128), 0)

    def second_back(s, part):
        def fill(n, _):
            d = decode_factor(mr[s, n, 128:136, :])
            d = jnp.concatenate([d, d], axis=0)
            if part is not None:
                if part == 0:
                    f = jnp.where(special, jnp.where(n < 4, 2.0, 0.0), 1.0)
                else:
                    f = jnp.where(n < 4, 0.0, 2.0)
                hit = (row16 == 0) & (special & ((n == 0) | (n == 4)))
            for c in range(8):
                re, im = unpack(mr[s, n, 16 * c : 16 * c + 16, :])
                re, im = re * d, im * d
                if part == 0:
                    if c == 0:
                        re, im = jnp.where(hit, re, re * f), jnp.where(hit, 0.0, im * f)
                    else:
                        re, im = re * f, im * f
                elif part == 1:
                    if c == 0:
                        re, im = jnp.where(hit, im, re * f), jnp.where(hit, 0.0, im * f)
                    else:
                        re, im = re * f, im * f
                lanes = slice(128 * (c % 2), 128 * (c % 2) + 128)
                for dst, x in ((rows16(16 * n, 16), re), (rows16(128 + 16 * n, 16), im)):
                    h, l = halves(x)
                    bh[c // 2, dst, lanes] = h
                    bl[c // 2, dst, lanes] = l
            return 0

        lax.fori_loop(0, 8, fill, 0)
        for cp in range(4):
            big[cp] = mm(yi[0], bh[cp]) + mm(yi[1], bh[cp]) + mm(yi[0], bl[cp])

        def spread(t, _):
            v = []
            at = rows16(16 * t, 16)
            for c in range(8):
                lanes = slice(128 * (c % 2), 128 * (c % 2) + 128)
                y = (big[c // 2, at, lanes], big[c // 2, rows16(128 + 16 * t, 16), lanes])
                v.append(y if c == 0 else turn(y, tyc[c, at, :], tys[c, at, :], 1))
            v = dft8(v, 1)
            for b in range(8):
                to = rows16(128 * (b % 2) + 16 * t, 16)
                if part == 1:
                    big2[b // 2, to, 128:256] = v[b][0]
                else:
                    big2[b // 2, to, 0:128] = v[b][0]
                    big2[b // 2, to, 128:256] = v[b][1]
            return 0

        lax.fori_loop(0, 8, spread, 0)

    for s in range(SLOTS):
        recv_all(narrow_copy, NARROW, me_n, m_args, s)
        second_back(s, 0 if s == 0 else None)
        if s == 0:
            @pl.when(special)
            def _():
                second_back(0, 1)

        def read_back(w):
            b = w // 4
            at = rows((b % 2) * 128 + (w % 4) * 32, 32)
            return big2[b // 2, at, 0:128], big2[b // 2, at, 128:256]

        def code_back(w, s=s):
            code_wide(read_back, us, s, w, w)

        code_and_send(code_back, wide_copy, WIDE, me_w, u_args, s)
        keep = pltpu.make_async_copy(us.at[s, me_w], out.at[s, me_w], u_recv.at[s, me_w])
        keep.start()

    lax.fori_loop(1, WIDE, recv_groups, 0)
    pltpu.make_async_copy(brecv, got, g_sem.at[0]).start()
    for g in range(16):
        named = jnp.concatenate(
            [brecv[2 * g, :, 512:640], brecv[2 * g + 1, :, 512:640]], axis=0
        )
        listed = jnp.round(mm_t(join[...], named))
        numbers[g] = listed.astype(i32)
        marks = listed if g == 0 else jnp.maximum(marks, listed)
    flag[0, 0] = jnp.max(marks[5:6, :]).astype(i32)
    lax.fori_loop(1, WIDE, sent_groups, 0)
    lax.fori_loop(1, NARROW, sent_measures, 0)
    pltpu.make_async_copy(brecv, got, g_sem.at[0]).wait()

    for s in range(SLOTS):
        pltpu.make_async_copy(us.at[s, me_w], out.at[s, me_w], u_recv.at[s, me_w]).wait()
        recv_all(wide_copy, WIDE, me_w, u_args, s)
        sent_all(wide_copy, WIDE, me_w, w_args, s)
        sent_all(narrow_copy, NARROW, me_n, n_args, s)
        sent_all(narrow_copy, NARROW, me_n, m_args, s)
        sent_all(wide_copy, WIDE, me_w, u_args, s)
    v_main.wait_send()

    @pl.when(jnp.logical_not(alone))
    def _():
        v_side.wait_send()


def spectral(noise, spectrum, owner, cell, assay, pencils, loads):
    t = TABLES
    angle = 2 * np.pi * np.arange(8)[:, None] * np.arange(128)[None, :] / 1024
    tyc = np.repeat(np.cos(angle).astype(np.float32)[:, :, None], 128, axis=2)
    tys = np.repeat(np.sin(angle).astype(np.float32)[:, :, None], 128, axis=2)
    vmem = pl.BlockSpec(memory_space=pltpu.VMEM)
    dma = pltpu.SemaphoreType.DMA
    return pl.pallas_call(
        spectral_kernel,
        out_shape=(
            jax.ShapeDtypeStruct((SLOTS, WIDE, 40, 128), i32),
            jax.ShapeDtypeStruct((WIDE, 64, 640), bf16),
            jax.ShapeDtypeStruct((16, 8, 128), i32),
            jax.ShapeDtypeStruct((1, 1), i32),
        ),
        in_specs=[vmem] * 19,
        out_specs=(
            pl.BlockSpec(memory_space=pl.ANY), pl.BlockSpec(memory_space=pl.ANY), vmem,
            pl.BlockSpec(memory_space=pltpu.SMEM),
        ),
        scratch_shapes=[
            pltpu.VMEM((2048, 128), f32),
            pltpu.VMEM((2048, 128), f32),
            pltpu.VMEM((SLOTS, WIDE, 40, 128), i32),
            pltpu.VMEM((SLOTS, WIDE, 40, 128), i32),
            pltpu.VMEM((4, 256, 256), bf16),
            pltpu.VMEM((4, 256, 256), bf16),
            pltpu.VMEM((4, 256, 256), f32),
            pltpu.VMEM((4, 256, 256), f32),
            pltpu.VMEM((SLOTS, NARROW, 136, 128), i32),
            pltpu.VMEM((SLOTS, NARROW, 136, 128), i32),
            pltpu.VMEM((8, 144, 256), bf16),
            pltpu.VMEM((8, 144, 256), bf16),
            pltpu.VMEM((SLOTS, NARROW, 136, 128), i32),
            pltpu.VMEM((SLOTS, NARROW, 136, 128), i32),
            pltpu.VMEM((SLOTS, WIDE, 40, 128), i32),
            pltpu.VMEM((SLOTS, 8, 128, 128), f32),
            pltpu.VMEM((8, 16, 128), f32),
            pltpu.VMEM((8, 128, 128), i32),
            pltpu.VMEM((8, 128, 128), i32),
            pltpu.VMEM((8, 8, 128), i32),
            pltpu.VMEM((2048, 128), f32),
            pltpu.VMEM((512, 512), bf16),
            pltpu.VMEM((16, 512), bf16),
            pltpu.VMEM((NARROW, ROOM, 512), bf16),
            pltpu.VMEM((NARROW, ROOM, 512), bf16),
            pltpu.VMEM((NARROW, 16, ROOM), bf16),
            pltpu.VMEM((NARROW, 16, ROOM), bf16),
            pltpu.VMEM((WIDE, 64, 640), bf16),
            pltpu.VMEM((WIDE, 64, 640), bf16),
            dma((SLOTS, WIDE)), dma((SLOTS, WIDE)),
            dma((SLOTS, NARROW)), dma((SLOTS, NARROW)),
            dma((SLOTS, NARROW)), dma((SLOTS, NARROW)),
            dma((SLOTS, WIDE)), dma((SLOTS, WIDE)),
            dma((2,)), dma((2,)),
            dma((NARROW,)), dma((NARROW,)), dma((NARROW,)), dma((NARROW,)),
            dma((WIDE,)), dma((WIDE,)), dma((1,)),
        ],
        compiler_params=pltpu.CompilerParams(
            collective_id=0, has_side_effects=True, vmem_limit_bytes=56 * 1024 * 1024
        ),
    )(
        noise.reshape(4096, 128), spectrum.reshape(4096, 128), t["tz"], t["yf"], t["yi"],
        t["xf"], t["xi"], tyc, tys, t["tx"], t["own2"], t["mir"], t["flips"],
        owner, cell, assay, pencils, loads, JOIN,
    )


def finish_kernel(numbers, freq, tzi, held, out, gathered, contrib, *accs):
    for acc in accs:
        acc[...] = jnp.zeros_like(acc)

    def depth(g, _):
        for j in range(4):
            y = g * 4 + j
            re, im = unpack(freq[pl.ds(y, 64, stride=40), :])
            d = decode_factor(freq[pl.ds(32 + lax.rem(y, 8), 64, stride=40), :])
            h, l = halves(jnp.concatenate([re * d, im * d], axis=0))
            u = jnp.concatenate([h, h, l], axis=0)
            out[pl.ds(y, 128, stride=32), :] = lax.dot_general(
                u, tzi[...], (((0,), (0,)), ((), ())), preferred_element_type=f32
            )
        return 0

    lax.fori_loop(0, 8, depth, 0)
    groups = numbers.shape[0]

    def gather(g, _):
        for j in range(128):
            gathered[pl.ds(g * 128 + j, 1), :] = out[pl.ds(numbers[g, 0, j], 1), :]
        return 0

    lax.fori_loop(0, groups, gather, 0)
    lane = lax.broadcasted_iota(i32, (128, 128), 1)

    def residual(g, _):
        at = rows16(g * 128, 128)
        depth_at = held[at, 515:516].astype(i32)
        grade = held[at, 524:525].astype(f32)
        value = jnp.sum(jnp.where(lane == depth_at, gathered[at, :], 0.0), axis=1, keepdims=True)
        resid = grade - value
        for k in range(TARGETS):
            contrib[k, at, :] = resid * held[at, 128 * k : 128 * k + 128].astype(f32)
        return 0

    lax.fori_loop(0, groups, residual, 0)

    def scatter(g, _):
        for j in range(128):
            for t in range(TARGETS):
                acc = accs[t + TARGETS * (j % 2)]
                at = pl.ds(numbers[g, 1 + t, j], 1)
                acc[at, :] = acc[at, :] + contrib[t, pl.ds(g * 128 + j, 1), :]
        return 0

    lax.fori_loop(0, groups, scatter, 0)

    def combine(g, _):
        at = rows(g * 64, 64)
        v = out[at, :]
        for acc in accs:
            v = v + acc[at, :]
        out[at, :] = v
        return 0

    lax.fori_loop(0, 64, combine, 0)


def finish(freq, held, numbers):
    vmem = pl.BlockSpec(memory_space=pltpu.VMEM)
    smem = pl.BlockSpec(memory_space=pltpu.SMEM)
    count = held.shape[0] * held.shape[1]
    return pl.pallas_call(
        finish_kernel,
        out_shape=jax.ShapeDtypeStruct((4096, 128), f32),
        in_specs=[smem] + [vmem] * 3,
        out_specs=vmem,
        scratch_shapes=[pltpu.VMEM((count, 128), f32), pltpu.VMEM((TARGETS, count, 128), f32)]
        + [pltpu.VMEM((4096, 128), f32)] * 8,
        compiler_params=pltpu.CompilerParams(vmem_limit_bytes=56 * 1024 * 1024),
    )(numbers, freq.reshape(-1, 128), TABLES["tzi"], held.reshape(count, -1))


def padded(assay, weights, owner, cell, pencils):
    count = owner.shape[0]
    order = jnp.arange(count, dtype=i32)
    earlier = order[:, None] < order[None, :]
    same = jnp.sum(earlier & (owner[:, None] == owner[None, :]), axis=0, dtype=i32)
    row = cell // NZ
    fields = [jnp.zeros((count,), i32), row // 256, row % 256, cell % NZ]
    for k in range(TARGETS):
        fields += [pencils[:, k] // 256, pencils[:, k] % 256]
    fields = [x.astype(bf16) for x in fields] + [assay]
    parts = jnp.zeros((count, 128), bf16).at[:, : len(fields)].set(jnp.stack(fields, axis=1))
    load = jnp.concatenate([weights, parts], axis=1)
    slots = jnp.arange(WIDE * NARROW * 8, dtype=i32)
    hot = (slots[:, None] == (owner * 8 + same)[None, :]).astype(bf16)
    held = jnp.dot(hot, load, preferred_element_type=f32).astype(bf16)
    held = held.reshape(WIDE, NARROW, 8, -1)
    held = lax.all_to_all(held, "wide", split_axis=0, concat_axis=0, tiled=True)
    held = lax.all_to_all(held, "narrow", split_axis=1, concat_axis=1, tiled=True)
    held = held.reshape(WIDE, 64, -1)
    names = held.reshape(WIDE * 64, -1)[:, TARGETS * NZ :].astype(f32)
    numbers = jnp.einsum("fc,gjc->gfj", jnp.asarray(JOIN, f32), names.reshape(16, 128, 128),
                         precision=lax.Precision.HIGHEST)
    return held, jnp.round(numbers).astype(i32)


def local(noise, spectrum, assay, measure_weights, measure_owner, measure_cell, measure_pencils):
    count = measure_owner.shape[1]
    freq, held, numbers, flag = spectral(
        noise, spectrum, measure_owner, measure_cell, assay, measure_pencils[0].T,
        measure_weights.reshape(count * TARGETS, NZ),
    )

    def roomy(_):
        weights = measure_weights[0].reshape(count, TARGETS * NZ)
        more = padded(assay[0], weights, measure_owner[0], measure_cell[0], measure_pencils[0])
        return finish(freq, *more)

    field = lax.cond(flag[0, 0] > 0, roomy, lambda _: finish(freq, held, numbers), 0)
    return field.reshape(noise.shape)


def solution(mesh):
    placed = (
        P("narrow", "wide", None),
        P("wide", None, "narrow"),
        P(("wide", "narrow"), None),
        P(("wide", "narrow"), None, None, None),
        P(("wide", "narrow"), None),
        P(("wide", "narrow"), None),
        P(("wide", "narrow"), None, None),
    )
    return jax.shard_map(
        local, mesh=mesh, in_specs=placed, out_specs=P("narrow", "wide", None), check_vma=False
    )
```

```python
import functools
import math

import jax
import jax.numpy as jnp
import ml_dtypes
import numpy as np
from jax import lax
from jax.experimental import pallas as pl
from jax.experimental.pallas import tpu as pltpu
from jax.sharding import PartitionSpec as P

NX, NY, NZ = 1024, 1024, 128
TARGETS = 4
WIDE, NARROW = 32, 8
SLOTS = 2
MESH = pl.DeviceIdType.MESH
f32, bf16, i32 = jnp.float32, jnp.bfloat16, jnp.int32

LN2 = math.log(2.0)
CODE = 16.0 / LN2
PEAK = 32600.0
TINY = 1e-30
SPEC_LOW = math.log(0.1)
SPEC_CODE = 65000.0 / math.log(85.0)
ROOT_HALF = math.sqrt(0.5)


def split(a):
    high = a.astype(ml_dtypes.bfloat16)
    low = (a - high.astype(np.float64)).astype(ml_dtypes.bfloat16)
    return high, low


def pair_matrix(sign):
    index = np.arange(128)
    angle = 2 * np.pi * (index[:, None] * index[None, :] % 128) / 128
    c, s = np.cos(angle), sign * np.sin(angle)
    return np.block([[c, -s], [s, c]])


def depth_forward():
    kz = 2 * np.arange(32)[None, :] + np.arange(2)[:, None]
    kz = kz.reshape(-1)
    z = np.arange(128)
    angle = 2 * np.pi * (kz[:, None] * z[None, :] % 128) / 128
    re, im = np.cos(angle), -np.sin(angle)
    im[kz == 0] = np.cos(np.pi * z)
    return np.concatenate([re, im], 0)


def depth_inverse():
    kz = (2 * np.arange(32)[None, :] + np.arange(2)[:, None]).reshape(-1)
    z = np.arange(128)
    angle = 2 * np.pi * (kz[:, None] * z[None, :] % 128) / 128
    re, im = 2 * np.cos(angle), -2 * np.sin(angle)
    re[kz == 0] = 1.0
    im[kz == 0] = np.cos(np.pi * z)
    return np.concatenate([re, im], 0)


def make_tables():
    h, l = split(depth_forward())
    tz = np.concatenate([h, l, h], 1)
    h, l = split(depth_inverse())
    tzi = np.concatenate([h, l, h], 0)
    yf = np.stack(split(pair_matrix(-1.0)))
    yi = np.stack(split(pair_matrix(1.0)))
    xf = np.stack(split(pair_matrix(-1.0).T))
    xi = np.stack(split(pair_matrix(1.0).T))
    c = np.arange(8)
    a = np.arange(128)
    angle = 2 * np.pi * c[:, None] * a[None, :] / 1024
    tx = np.stack([np.cos(angle), np.sin(angle)]).astype(np.float32)
    row = np.arange(128)
    lane_of = 8 * (row % 16) + row // 16
    own = np.zeros((128, 128))
    own[row, lane_of] = 1
    mir = np.zeros((128, 128))
    mir[row, (128 - lane_of) % 128] = 1
    own2 = np.concatenate([own, own], 1).astype(ml_dtypes.bfloat16)
    flips = np.zeros((2, 128, 128))
    flips[0, (128 - row) % 128, row] = 1
    flips[1, 127 - row, row] = 1
    flips = np.concatenate([flips, flips], 1).astype(ml_dtypes.bfloat16)
    return dict(
        tz=tz, tzi=tzi, yf=yf, yi=yi, xf=xf, xi=xi, tx=tx, own2=own2,
        mir=mir.astype(ml_dtypes.bfloat16), flips=flips,
    )


TABLES = make_tables()
ROOM = 160


def join_matrix():
    m = np.zeros((8, 128))
    m[0, 1], m[0, 2] = 256, 1
    for k in range(TARGETS):
        m[1 + k, 4 + 2 * k], m[1 + k, 5 + 2 * k] = 256, 1
    m[5, 13] = 1
    return m.astype(ml_dtypes.bfloat16)


JOIN = join_matrix()


def halves(v):
    h = v.astype(bf16)
    return h, (v - h.astype(f32)).astype(bf16)


def times_i(v, sign):
    re, im = v
    return (-im, re) if sign > 0 else (im, -re)


def add(a, b):
    return a[0] + b[0], a[1] + b[1]


def sub(a, b):
    return a[0] - b[0], a[1] - b[1]


def dft4(v, sign):
    s, d = add(v[0], v[2]), sub(v[0], v[2])
    t, u = add(v[1], v[3]), times_i(sub(v[1], v[3]), sign)
    return [add(s, t), add(d, u), sub(s, t), sub(d, u)]


def dft8(v, sign):
    e = dft4(v[0::2], sign)
    o = dft4(v[1::2], sign)
    g = float(sign)
    re, im = o[1]
    o[1] = ((re - g * im) * ROOT_HALF, (im + g * re) * ROOT_HALF)
    o[2] = times_i(o[2], sign)
    re, im = o[3]
    o[3] = ((-re - g * im) * ROOT_HALF, (g * re - im) * ROOT_HALF)
    return [add(e[c], o[c]) for c in range(4)] + [sub(e[c], o[c]) for c in range(4)]


def turn(v, cos, sin, sign):
    re, im = v
    if sign < 0:
        return re * cos + im * sin, im * cos - re * sin
    return re * cos - im * sin, im * cos + re * sin


def scale_code(m):
    return jnp.ceil(jnp.log(jnp.maximum(m, TINY)) * CODE).astype(i32)


def encode_factor(code):
    return jnp.exp(code.astype(f32) * (-1.0 / CODE)) * PEAK


def decode_factor(code):
    return jnp.exp(code.astype(f32) * (1.0 / CODE)) * (1.0 / PEAK)


def pack(re, im):
    a = jnp.round(re).astype(i32)
    b = jnp.round(im).astype(i32)
    return (a << 16) | (b & 0xFFFF)


def unpack(word):
    return (word >> 16).astype(f32), ((word << 16) >> 16).astype(f32)


def tile_max(tiles):
    tiles = [jnp.abs(t) for t in tiles]
    while len(tiles) > 1:
        tiles = [jnp.maximum(a, b) for a, b in zip(tiles[0::2], tiles[1::2])] + (
            tiles[-1:] if len(tiles) % 2 else []
        )
    return tiles[0]


def mm(a, b):
    return jnp.dot(a, b, preferred_element_type=f32)


def mm_t(a, b):
    return lax.dot_general(a, b, (((1,), (1,)), ((), ())), preferred_element_type=f32)


def rows(start, size):
    return pl.ds(pl.multiple_of(start, 8), size)


def rows16(start, size):
    return pl.ds(pl.multiple_of(start, 16), size)


def spectral_kernel(
    noise, spec, tz, yf, yi, xf, xi, tyc, tys, tx, own2, mir, flips, owner, cell, assay, pencils, loads, join,
    out, got, numbers, flag,
    zre, zim, ws, wr, bh, bl, big, big2, ns, nr, lh, ll, ms, mr, us,
    ear, bsp, vs, vr, vc, wf, weights, parts, asend, arecv, psend, precv, bsend, brecv,
    w_send, w_recv, n_send, n_recv, m_send, m_recv, u_send, u_recv, v_send, v_recv,
    a_send, a_recv, p_send, p_recv, b_send, b_recv, g_sem,
):
    me_w = lax.axis_index("wide")
    me_n = lax.axis_index("narrow")
    special = me_w == 0
    edge = special & ((me_n == 0) | (me_n == 4))

    barrier = pltpu.get_barrier_semaphore()

    def greet_wide(i, _):
        pl.semaphore_signal(
            barrier, inc=1, device_id={"wide": lax.rem(me_w + i, WIDE)}, device_id_type=MESH
        )
        return 0

    def greet_narrow(i, _):
        pl.semaphore_signal(
            barrier, inc=1, device_id={"narrow": lax.rem(me_n + i, NARROW)}, device_id_type=MESH
        )
        return 0

    lax.fori_loop(1, WIDE, greet_wide, 0)
    lax.fori_loop(1, NARROW, greet_narrow, 0)

    def wide_copy(src, dst, sends, recvs, s, peer, slot):
        return pltpu.make_async_remote_copy(
            src_ref=src.at[s, peer], dst_ref=dst.at[s, slot], send_sem=sends.at[s, peer],
            recv_sem=recvs.at[s, slot], device_id={"wide": peer}, device_id_type=MESH,
        )

    def narrow_copy(src, dst, sends, recvs, s, peer, slot):
        return pltpu.make_async_remote_copy(
            src_ref=src.at[s, peer], dst_ref=dst.at[s, slot], send_sem=sends.at[s, peer],
            recv_sem=recvs.at[s, slot], device_id={"narrow": peer}, device_id_type=MESH,
        )

    def code_and_send(code, make, count, me, args, s):
        def one(i, _):
            peer = lax.rem(me + i, count)
            code(peer)
            make(*args, s, peer, me).start()
            return 0

        lax.fori_loop(1, count, one, 0)
        code(me)

    def recv_all(make, count, me, args, s):
        def one(i, _):
            peer = lax.rem(me + i, count)
            make(*args, s, peer, peer).wait_recv()
            return 0

        lax.fori_loop(1, count, one, 0)

    def sent_all(make, count, me, args, s):
        def one(i, _):
            peer = lax.rem(me + i, count)
            make(*args, s, peer, peer).wait_send()
            return 0

        lax.fori_loop(1, count, one, 0)

    w_args = (ws, wr, w_send, w_recv)
    n_args = (ns, nr, n_send, n_recv)
    m_args = (ms, mr, m_send, m_recv)
    u_args = (us, out, u_send, u_recv)

    room = asend.shape[1]
    count = owner.shape[1]
    owners = owner[...]
    cells = cell[...]
    narrow_of = (owners & 7).astype(f32)
    diagonal = lax.broadcasted_iota(i32, (128, 128), 0) == lax.broadcasted_iota(i32, (128, 128), 1)

    def column(line):
        pieces = []
        for k in range(count // 128):
            piece = jnp.broadcast_to(line[:, 128 * k : 128 * k + 128], (128, 128))
            pieces.append(jnp.sum(jnp.where(diagonal, piece, 0.0), axis=1, keepdims=True))
        return jnp.concatenate(pieces, axis=0)

    earlier = lax.broadcasted_iota(i32, (count, count), 0) < lax.broadcasted_iota(i32, (count, count), 1)

    def before(line):
        match = earlier & (column(line) == line)
        return jnp.sum(jnp.where(match, 1.0, 0.0), axis=0, keepdims=True)

    same = before(owners.astype(f32))
    rank = before(narrow_of)
    place = jnp.where(rank < room, narrow_of * room + rank, -1.0).astype(i32)
    over = jnp.max(jnp.where(rank < room, 0.0, 1.0), axis=1, keepdims=True)
    key = (owners >> 3 << 3).astype(f32) + same + 1.0
    part_row = lax.broadcasted_iota(i32, (16, count), 0)
    listed = jnp.zeros((16, count), f32)
    for r, line in (
        (0, key),
        (1, (cells >> 15).astype(f32)),
        (2, ((cells >> 7) & 255).astype(f32)),
        (3, (cells & 127).astype(f32)),
        (12, assay[...].astype(f32)),
        *((4 + 2 * k, (pencils[k : k + 1, :] >> 8).astype(f32)) for k in range(TARGETS)),
        *((5 + 2 * k, (pencils[k : k + 1, :] & 255).astype(f32)) for k in range(TARGETS)),
    ):
        listed = jnp.where(part_row == r, line, listed)
    parts[...] = listed.astype(bf16)
    wf[...] = loads[...].astype(f32)
    for k in range(TARGETS):
        weights[:, 128 * k : 128 * k + 128] = wf[pl.ds(k, count, stride=TARGETS), :].astype(bf16)
    room_row = lax.broadcasted_iota(i32, (room, count), 0)
    flag_row = lax.broadcasted_iota(i32, (16, room), 0) == 13

    def pack_measures(n, _):
        hot = jnp.where(room_row + n * room == place, 1.0, 0.0).astype(bf16)
        asend[n] = mm(hot, weights[...]).astype(bf16)
        psend[n] = jnp.where(flag_row, over, mm_t(parts[...], hot)).astype(bf16)
        return 0

    lax.fori_loop(0, NARROW, pack_measures, 0)
    arecv[me_n] = asend[me_n]
    precv[me_n] = psend[me_n]

    def to_narrow(src, dst, sends, recvs, peer, slot):
        return pltpu.make_async_remote_copy(
            src_ref=src.at[peer], dst_ref=dst.at[slot], send_sem=sends.at[peer],
            recv_sem=recvs.at[slot], device_id={"narrow": peer}, device_id_type=MESH,
        )

    def to_wide(peer, slot):
        return pltpu.make_async_remote_copy(
            src_ref=bsend.at[peer], dst_ref=brecv.at[slot], send_sem=b_send.at[peer],
            recv_sem=b_recv.at[slot], device_id={"wide": peer}, device_id_type=MESH,
        )

    a_args = (asend, arecv, a_send, a_recv)
    p_args = (psend, precv, p_send, p_recv)

    def send_measures(i, _):
        peer = lax.rem(me_n + i, NARROW)
        to_narrow(*p_args, peer, me_n).start()
        to_narrow(*a_args, peer, me_n).start()
        return 0

    def recv_measures(i, _):
        peer = lax.rem(me_n + i, NARROW)
        to_narrow(*p_args, peer, peer).wait_recv()
        to_narrow(*a_args, peer, peer).wait_recv()
        return 0

    def sent_measures(i, _):
        peer = lax.rem(me_n + i, NARROW)
        to_narrow(*p_args, peer, peer).wait_send()
        to_narrow(*a_args, peer, peer).wait_send()
        return 0

    def send_groups(i, _):
        to_wide(lax.rem(me_w + i, WIDE), me_w).start()
        return 0

    def recv_groups(i, _):
        peer = lax.rem(me_w + i, WIDE)
        to_wide(peer, peer).wait_recv()
        return 0

    def sent_groups(i, _):
        peer = lax.rem(me_w + i, WIDE)
        to_wide(peer, peer).wait_send()
        return 0

    pl.semaphore_wait(barrier, WIDE - 1 + NARROW - 1)
    lax.fori_loop(1, NARROW, send_measures, 0)

    late = special & (me_n >= 4)
    own_slots = (jnp.where(late, 2, 0), 1)
    mir_slots = (jnp.where(special & (me_n < 4), 2, jnp.where(special, 0, 2)), 3)

    def spectrum_rows(slot, e):
        return halves(spec[pl.ds(slot * 1024 + e, 128, stride=8), :])

    for e in range(8):
        back = (8 - e) % 8
        flip = flips[0 if e == 0 else 1]
        codes = []
        for s in range(SLOTS):
            h, l = spectrum_rows(own_slots[s], e)
            ear[s, e] = mm_t(own2[...], jnp.concatenate([h, l], axis=1))
            h, l = spectrum_rows(mir_slots[s], back)
            gh = mm_t(mir[...], h).astype(bf16)
            gl = mm_t(mir[...], l).astype(bf16)
            v = mm(jnp.concatenate([gh, gl], axis=1), flip)
            q = jnp.round((jnp.log(v) - SPEC_LOW) * SPEC_CODE - 32500.0)
            codes.append(jnp.clip(q, -32767.0, 32767.0))
        vs[e] = pack(codes[0], codes[1])

    v_main = pltpu.make_async_remote_copy(
        src_ref=vs, dst_ref=vr, send_sem=v_send.at[0], recv_sem=v_recv.at[0],
        device_id={"narrow": 7 - me_n}, device_id_type=MESH,
    )
    v_side = pltpu.make_async_remote_copy(
        src_ref=vs.at[:, pl.ds(0, 8), :], dst_ref=vc, send_sem=v_send.at[1], recv_sem=v_recv.at[1],
        device_id={"narrow": lax.rem(8 - me_n, 8)}, device_id_type=MESH,
    )

    alone = (me_n == 0) | (me_n == 4)

    @pl.when(alone)
    def _():
        vc[...] = vs[:, 0:8, :]

    v_main.start()

    @pl.when(jnp.logical_not(alone))
    def _():
        v_side.start()

    def depth(y, _):
        cells = [y * 4 + k for k in range(4)]
        pieces = []
        for k in cells:
            h, l = halves(noise[pl.ds(k, 128, stride=32), :])
            pieces.append(jnp.concatenate([h, h, l], axis=1))
        res = mm_t(tz[...], jnp.concatenate(pieces, axis=0))
        for i, k in enumerate(cells):
            zre[pl.ds(k, 64, stride=32), :] = res[:64, 128 * i : 128 * i + 128]
            zim[pl.ds(k, 64, stride=32), :] = res[64:, 128 * i : 128 * i + 128]
        return 0

    lax.fori_loop(0, 8, depth, 0)

    def code_wide(read, dst, s, w, to):
        re, im = read(w)
        m = tile_max([re[8 * t : 8 * t + 8] for t in range(4)] + [im[8 * t : 8 * t + 8] for t in range(4)])
        code = scale_code(m)
        fac = encode_factor(code)
        for t in range(4):
            sl = slice(8 * t, 8 * t + 8)
            dst[s, to, 8 * t : 8 * t + 8, :] = pack(re[sl] * fac, im[sl] * fac)
        dst[s, to, 32:40, :] = code

    for s in range(SLOTS):
        def read_depth(w, s=s):
            at = rows((s * 32 + w) * 32, 32)
            return zre[at, :], zim[at, :]

        def code_one(w, s=s, read=read_depth):
            code_wide(read, ws, s, w, w)

        code_and_send(code_one, wide_copy, WIDE, me_w, w_args, s)
        wr[s, me_w] = ws[s, me_w]

    def second_forward(s, p, q, r):
        def group(g, _):
            dec = [decode_factor(wr[s, 4 * b + g, 32:40, :]) for b in range(8)]
            dec = [jnp.concatenate([d, d], axis=0) for d in dec]
            for t in range(2):
                v = []
                for b in range(8):
                    re, im = unpack(wr[s, 4 * b + g, 16 * t : 16 * t + 16, :])
                    re, im = re * dec[b], im * dec[b]
                    if p is not None:
                        re, im = re * p + im * q, im * r
                    v.append((re, im))
                v = dft8(v, -1)
                at = rows16(g * 32 + 16 * t, 16)
                at_im = rows16(128 + g * 32 + 16 * t, 16)
                for c in range(8):
                    w = v[c] if c == 0 else turn(v[c], tyc[c, at, :], tys[c, at, :], -1)
                    lanes = slice(128 * (c % 2), 128 * (c % 2) + 128)
                    for dst, part in ((at, w[0]), (at_im, w[1])):
                        h, l = halves(part)
                        bh[c // 2, dst, lanes] = h
                        bl[c // 2, dst, lanes] = l
            return 0

        lax.fori_loop(0, 4, group, 0)
        for cp in range(4):
            big[cp] = mm(yf[0], bh[cp]) + mm(yf[1], bh[cp]) + mm(yf[0], bl[cp])

    first_row = lax.broadcasted_iota(i32, (8, 128), 0) == 0

    def code_narrow(s, n):
        tiles = []
        for c in range(8):
            lanes = slice(128 * (c % 2), 128 * (c % 2) + 128)
            for t in range(2):
                tiles.append((
                    big[c // 2, rows(16 * n + 8 * t, 8), lanes],
                    big[c // 2, rows(128 + 16 * n + 8 * t, 8), lanes],
                ))
        code = scale_code(tile_max([x for pair in tiles for x in pair]))
        fac = encode_factor(code)
        for k, (re, im) in enumerate(tiles):
            ns[s, n, 8 * k : 8 * k + 8, :] = pack(re * fac, im * fac)
        ns[s, n, 128:136, :] = code

    for s in range(SLOTS):
        recv_all(wide_copy, WIDE, me_w, w_args, s)
        if s == 0:
            one = jnp.where(special, 0.0, 1.0)
            second_forward(s, 1.0, 0.0, one)

            @pl.when(special)
            def _():
                big2[...] = big[...]
                second_forward(0, 0.0, 1.0, 0.0)
                top = big[0, 0:8, 0:128]
                mid = big[0, 64:72, 0:128]
                big[:, 0:64, :] = big2[:, 0:64, :]
                big[:, 128:192, :] = big2[:, 128:192, :]
                big[0, 128:136, 0:128] = jnp.where(first_row, top, big[0, 128:136, 0:128])
                big[0, 192:200, 0:128] = jnp.where(first_row, mid, big[0, 192:200, 0:128])
                big[0, 64:72, 0:128] = jnp.where(first_row, big2[0, 64:72, 0:128], mid)
        else:
            second_forward(s, None, None, None)

        code_and_send(functools.partial(code_narrow, s), narrow_copy, NARROW, me_n, n_args, s)
        nr[s, me_n] = ns[s, me_n]


    def regroup():
        lax.fori_loop(1, NARROW, recv_measures, 0)
        row = lax.broadcasted_iota(i32, (512, room), 0)
        want = (((row >> 4) << 3) + (row & 7) + 1).astype(f32)
        flags = precv[0].astype(f32)
        for k in range(1, NARROW):
            flags = jnp.maximum(flags, precv[k].astype(f32))
        flags = jnp.max(jnp.where(flag_row, flags, 0.0), axis=1, keepdims=True)
        flags = jnp.max(flags, axis=0, keepdims=True)
        flag_col = lax.broadcasted_iota(i32, (512, 128), 1) == 13
        for q in range(4):
            moved, named = 0.0, 0.0
            for k in range(2):
                key = precv[2 * q + k, 0:1, :].astype(f32)
                match = (((row >> 3) & 1) == k) & (want == key)
                hot = jnp.where(match, 1.0, 0.0).astype(bf16)
                moved = moved + mm(hot, arecv[2 * q + k])
                named = named + mm_t(hot, precv[2 * q + k])
            named = jnp.concatenate([named, jnp.zeros((512, 112), f32)], axis=1)
            named = jnp.where(flag_col, flags, named)
            bsend[:, 16 * q : 16 * q + 16, 0:512] = moved.astype(bf16).reshape(WIDE, 16, 512)
            bsend[:, 16 * q : 16 * q + 16, 512:640] = named.astype(bf16).reshape(WIDE, 16, 128)
        brecv[me_w] = bsend[me_w]
        lax.fori_loop(1, WIDE, send_groups, 0)

    regroup()

    total = 1.0 / (NX * NY * NZ)
    v_main.wait_recv()

    @pl.when(jnp.logical_not(alone))
    def _():
        v_side.wait_recv()

    def decode_spectrum(q):
        return jnp.exp((q + 32500.0) * (1.0 / SPEC_CODE) + SPEC_LOW)

    bsp[...] = jnp.zeros_like(bsp)

    @pl.when(edge)
    def _():
        sigma = jnp.where(me_n == 0, 1.0, -1.0)
        xs, vv = [], []
        for e in range(8):
            xs.append(ear[0, e, 0:8, :])
            vv.append(decode_spectrum(unpack(vc[e])[0]))

        def even(list_of, e):
            h, l = halves(list_of[(8 - e) % 8])
            pair = jnp.concatenate([h, l], axis=1)
            flip = flips[0 if e == 0 else 1]
            return (mm(pair, flip) + list_of[e]) * 0.5

        for e in range(8):
            a, b = even(xs, e), even(vv, e)
            bsp[e, 0:8, :] = jnp.where(first_row, (a - b) * (0.5 * total) * sigma, 0.0)
            big2[0, 8 * e : 8 * e + 8, 0:128] = (a + b) * (0.5 * total)

    for e in range(8):
        m0, m1 = unpack(vr[e])
        s0, s1 = unpack(vc[e])
        for s, m, side in ((0, m0, s0), (1, m1, s1)):
            m, side = decode_spectrum(m), decode_spectrum(side)
            ear_e = ear[s, e]
            lead = jnp.where(first_row, side, m[0:8])
            ear[s, e, 8:128, :] = (ear_e[8:128] + m[8:128]) * (0.5 * total)
            ear[s, e, 0:8, :] = (ear_e[0:8] + lead) * (0.5 * total)

    @pl.when(edge)
    def _():
        for e in range(8):
            ear[0, e, 0:8, :] = jnp.where(
                first_row, big2[0, 8 * e : 8 * e + 8, 0:128], ear[0, e, 0:8, :]
            )

    def first_both(s):
        def decs(n):
            d = decode_factor(nr[s, n, 128:136, :])
            return jnp.concatenate([d, d], axis=0)

        for n in range(8):
            big2[0, 16 * n : 16 * n + 16, 0:128] = decs(n)

        def load(c):
            v = []
            for n in range(8):
                re, im = unpack(nr[s, n, rows16(16 * c, 16), :])
                d = big2[0, 16 * n : 16 * n + 16, 0:128]
                v.append((re * d, im * d))
            return v

        def put(v, at):
            v = dft8(v, -1)
            for e in range(8):
                w = v[e] if e == 0 else turn(v[e], tx[0, e : e + 1, :], tx[1, e : e + 1, :], -1)
                for lanes, part in ((slice(0, 128), w[0]), (slice(128, 256), w[1])):
                    h, l = halves(part)
                    lh[e, at, lanes] = h
                    ll[e, at, lanes] = l

        def block(c, _):
            put(load(c), rows16(16 * c, 16))
            return 0

        lax.fori_loop(0, 8, block, 0)
        if s == 0:
            put([(re, -im) for re, im in load(0)], slice(128, 144))
        count = 144 if s == 0 else 128
        for e in range(8):
            h, l = lh[e, 0:count, :], ll[e, 0:count, :]
            z = mm(h, xf[0]) + mm(h, xf[1]) + mm(l, xf[0])
            fil = jnp.concatenate([ear[s, e], ear[s, e]], axis=1)
            g = z[0:128] * fil
            if s == 0:
                extra = jnp.concatenate([bsp[e], bsp[e]], axis=1)
                g = jnp.concatenate([g[0:16] + z[128:144] * extra, g[16:128]], axis=0)
            h, l = halves(g)
            big[e // 2, 128 * (e % 2) : 128 * (e % 2) + 128, :] = (
                mm(h, xi[0]) + mm(h, xi[1]) + mm(l, xi[0])
            )

        def unblock(c, _):
            v = []
            for e in range(8):
                at = rows16(128 * (e % 2) + 16 * c, 16)
                y = (big[e // 2, at, 0:128], big[e // 2, at, 128:256])
                v.append(y if e == 0 else turn(y, tx[0, e : e + 1, :], tx[1, e : e + 1, :], 1))
            v = dft8(v, 1)
            for n in range(8):
                at = rows16(128 * (n % 2) + 16 * c, 16)
                big2[n // 2, at, 0:128] = v[n][0]
                big2[n // 2, at, 128:256] = v[n][1]
            return 0

        lax.fori_loop(0, 8, unblock, 0)

    def code_first(s, n):
        page, base = lax.div(n, 2), 128 * lax.rem(n, 2)
        tiles = []
        for k in range(16):
            at = rows(base + 8 * k, 8)
            tiles.append((big2[page, at, 0:128], big2[page, at, 128:256]))
        code = scale_code(tile_max([x for pair in tiles for x in pair]))
        fac = encode_factor(code)
        for k, (re, im) in enumerate(tiles):
            ms[s, n, 8 * k : 8 * k + 8, :] = pack(re * fac, im * fac)
        ms[s, n, 128:136, :] = code

    for s in range(SLOTS):
        recv_all(narrow_copy, NARROW, me_n, n_args, s)
        first_both(s)
        code_and_send(functools.partial(code_first, s), narrow_copy, NARROW, me_n, m_args, s)
        mr[s, me_n] = ms[s, me_n]

    row16 = lax.broadcasted_iota(i32, (16, 128), 0)

    def second_back(s, part):
        def fill(n, _):
            d = decode_factor(mr[s, n, 128:136, :])
            d = jnp.concatenate([d, d], axis=0)
            if part is not None:
                if part == 0:
                    f = jnp.where(special, jnp.where(n < 4, 2.0, 0.0), 1.0)
                else:
                    f = jnp.where(n < 4, 0.0, 2.0)
                hit = (row16 == 0) & (special & ((n == 0) | (n == 4)))
            for c in range(8):
                re, im = unpack(mr[s, n, 16 * c : 16 * c + 16, :])
                re, im = re * d, im * d
                if part == 0:
                    if c == 0:
                        re, im = jnp.where(hit, re, re * f), jnp.where(hit, 0.0, im * f)
                    else:
                        re, im = re * f, im * f
                elif part == 1:
                    if c == 0:
                        re, im = jnp.where(hit, im, re * f), jnp.where(hit, 0.0, im * f)
                    else:
                        re, im = re * f, im * f
                lanes = slice(128 * (c % 2), 128 * (c % 2) + 128)
                for dst, x in ((rows16(16 * n, 16), re), (rows16(128 + 16 * n, 16), im)):
                    h, l = halves(x)
                    bh[c // 2, dst, lanes] = h
                    bl[c // 2, dst, lanes] = l
            return 0

        lax.fori_loop(0, 8, fill, 0)
        for cp in range(4):
            big[cp] = mm(yi[0], bh[cp]) + mm(yi[1], bh[cp]) + mm(yi[0], bl[cp])

        def spread(t, _):
            v = []
            at = rows16(16 * t, 16)
            for c in range(8):
                lanes = slice(128 * (c % 2), 128 * (c % 2) + 128)
                y = (big[c // 2, at, lanes], big[c // 2, rows16(128 + 16 * t, 16), lanes])
                v.append(y if c == 0 else turn(y, tyc[c, at, :], tys[c, at, :], 1))
            v = dft8(v, 1)
            for b in range(8):
                to = rows16(128 * (b % 2) + 16 * t, 16)
                if part == 1:
                    big2[b // 2, to, 128:256] = v[b][0]
                else:
                    big2[b // 2, to, 0:128] = v[b][0]
                    big2[b // 2, to, 128:256] = v[b][1]
            return 0

        lax.fori_loop(0, 8, spread, 0)

    for s in range(SLOTS):
        recv_all(narrow_copy, NARROW, me_n, m_args, s)
        second_back(s, 0 if s == 0 else None)
        if s == 0:
            @pl.when(special)
            def _():
                second_back(0, 1)

        def read_back(w):
            b = w // 4
            at = rows((b % 2) * 128 + (w % 4) * 32, 32)
            return big2[b // 2, at, 0:128], big2[b // 2, at, 128:256]

        def code_back(w, s=s):
            code_wide(read_back, us, s, w, w)

        code_and_send(code_back, wide_copy, WIDE, me_w, u_args, s)
        keep = pltpu.make_async_copy(us.at[s, me_w], out.at[s, me_w], u_recv.at[s, me_w])
        keep.start()

    lax.fori_loop(1, WIDE, recv_groups, 0)
    pltpu.make_async_copy(brecv, got, g_sem.at[0]).start()
    for g in range(16):
        named = jnp.concatenate(
            [brecv[2 * g, :, 512:640], brecv[2 * g + 1, :, 512:640]], axis=0
        )
        listed = jnp.round(mm_t(join[...], named))
        numbers[g] = listed.astype(i32)
        marks = listed if g == 0 else jnp.maximum(marks, listed)
    flag[0, 0] = jnp.max(marks[5:6, :]).astype(i32)
    lax.fori_loop(1, WIDE, sent_groups, 0)
    lax.fori_loop(1, NARROW, sent_measures, 0)
    pltpu.make_async_copy(brecv, got, g_sem.at[0]).wait()

    for s in range(SLOTS):
        pltpu.make_async_copy(us.at[s, me_w], out.at[s, me_w], u_recv.at[s, me_w]).wait()
        recv_all(wide_copy, WIDE, me_w, u_args, s)
        sent_all(wide_copy, WIDE, me_w, w_args, s)
        sent_all(narrow_copy, NARROW, me_n, n_args, s)
        sent_all(narrow_copy, NARROW, me_n, m_args, s)
        sent_all(wide_copy, WIDE, me_w, u_args, s)
    v_main.wait_send()

    @pl.when(jnp.logical_not(alone))
    def _():
        v_side.wait_send()


def spectral(noise, spectrum, owner, cell, assay, pencils, loads):
    t = TABLES
    angle = 2 * np.pi * np.arange(8)[:, None] * np.arange(128)[None, :] / 1024
    tyc = np.repeat(np.cos(angle).astype(np.float32)[:, :, None], 128, axis=2)
    tys = np.repeat(np.sin(angle).astype(np.float32)[:, :, None], 128, axis=2)
    vmem = pl.BlockSpec(memory_space=pltpu.VMEM)
    dma = pltpu.SemaphoreType.DMA
    return pl.pallas_call(
        spectral_kernel,
        out_shape=(
            jax.ShapeDtypeStruct((SLOTS, WIDE, 40, 128), i32),
            jax.ShapeDtypeStruct((WIDE, 64, 640), bf16),
            jax.ShapeDtypeStruct((16, 8, 128), i32),
            jax.ShapeDtypeStruct((1, 1), i32),
        ),
        in_specs=[vmem] * 19,
        out_specs=(
            pl.BlockSpec(memory_space=pl.ANY), pl.BlockSpec(memory_space=pl.ANY), vmem,
            pl.BlockSpec(memory_space=pltpu.SMEM),
        ),
        scratch_shapes=[
            pltpu.VMEM((2048, 128), f32),
            pltpu.VMEM((2048, 128), f32),
            pltpu.VMEM((SLOTS, WIDE, 40, 128), i32),
            pltpu.VMEM((SLOTS, WIDE, 40, 128), i32),
            pltpu.VMEM((4, 256, 256), bf16),
            pltpu.VMEM((4, 256, 256), bf16),
            pltpu.VMEM((4, 256, 256), f32),
            pltpu.VMEM((4, 256, 256), f32),
            pltpu.VMEM((SLOTS, NARROW, 136, 128), i32),
            pltpu.VMEM((SLOTS, NARROW, 136, 128), i32),
            pltpu.VMEM((8, 144, 256), bf16),
            pltpu.VMEM((8, 144, 256), bf16),
            pltpu.VMEM((SLOTS, NARROW, 136, 128), i32),
            pltpu.VMEM((SLOTS, NARROW, 136, 128), i32),
            pltpu.VMEM((SLOTS, WIDE, 40, 128), i32),
            pltpu.VMEM((SLOTS, 8, 128, 128), f32),
            pltpu.VMEM((8, 16, 128), f32),
            pltpu.VMEM((8, 128, 128), i32),
            pltpu.VMEM((8, 128, 128), i32),
            pltpu.VMEM((8, 8, 128), i32),
            pltpu.VMEM((2048, 128), f32),
            pltpu.VMEM((512, 512), bf16),
            pltpu.VMEM((16, 512), bf16),
            pltpu.VMEM((NARROW, ROOM, 512), bf16),
            pltpu.VMEM((NARROW, ROOM, 512), bf16),
            pltpu.VMEM((NARROW, 16, ROOM), bf16),
            pltpu.VMEM((NARROW, 16, ROOM), bf16),
            pltpu.VMEM((WIDE, 64, 640), bf16),
            pltpu.VMEM((WIDE, 64, 640), bf16),
            dma((SLOTS, WIDE)), dma((SLOTS, WIDE)),
            dma((SLOTS, NARROW)), dma((SLOTS, NARROW)),
            dma((SLOTS, NARROW)), dma((SLOTS, NARROW)),
            dma((SLOTS, WIDE)), dma((SLOTS, WIDE)),
            dma((2,)), dma((2,)),
            dma((NARROW,)), dma((NARROW,)), dma((NARROW,)), dma((NARROW,)),
            dma((WIDE,)), dma((WIDE,)), dma((1,)),
        ],
        compiler_params=pltpu.CompilerParams(
            collective_id=0, has_side_effects=True, vmem_limit_bytes=56 * 1024 * 1024
        ),
    )(
        noise.reshape(4096, 128), spectrum.reshape(4096, 128), t["tz"], t["yf"], t["yi"],
        t["xf"], t["xi"], tyc, tys, t["tx"], t["own2"], t["mir"], t["flips"],
        owner, cell, assay, pencils, loads, JOIN,
    )


def finish_kernel(numbers, freq, tzi, held, out, gathered, contrib, *accs):
    for acc in accs:
        acc[...] = jnp.zeros_like(acc)

    def depth(g, _):
        pieces = []
        for j in range(4):
            y = g * 4 + j
            re, im = unpack(freq[pl.ds(y, 64, stride=40), :])
            d = decode_factor(freq[pl.ds(32 + lax.rem(y, 8), 64, stride=40), :])
            h, l = halves(jnp.concatenate([re * d, im * d], axis=0))
            pieces.append(jnp.concatenate([h, h, l], axis=0))
        cells = lax.dot_general(
            jnp.concatenate(pieces, axis=1), tzi[...], (((0,), (0,)), ((), ())),
            preferred_element_type=f32,
        )
        for j in range(4):
            out[pl.ds(g * 4 + j, 128, stride=32), :] = cells[128 * j : 128 * j + 128]
        return 0

    lax.fori_loop(0, 8, depth, 0)
    groups = numbers.shape[0]

    def gather(g, _):
        for j in range(128):
            gathered[pl.ds(g * 128 + j, 1), :] = out[pl.ds(numbers[g, 0, j], 1), :]
        return 0

    lax.fori_loop(0, groups, gather, 0)
    lane = lax.broadcasted_iota(i32, (128, 128), 1)

    def residual(g, _):
        at = rows16(g * 128, 128)
        depth_at = held[at, 515:516].astype(i32)
        grade = held[at, 524:525].astype(f32)
        value = jnp.sum(jnp.where(lane == depth_at, gathered[at, :], 0.0), axis=1, keepdims=True)
        resid = grade - value
        for k in range(TARGETS):
            contrib[k, at, :] = resid * held[at, 128 * k : 128 * k + 128].astype(f32)
        return 0

    lax.fori_loop(0, groups, residual, 0)

    def scatter(g, _):
        for j in range(128):
            for t in range(TARGETS):
                acc = accs[t + TARGETS * (j % 2)]
                at = pl.ds(numbers[g, 1 + t, j], 1)
                acc[at, :] = acc[at, :] + contrib[t, pl.ds(g * 128 + j, 1), :]
        return 0

    lax.fori_loop(0, groups, scatter, 0)

    def combine(g, _):
        at = rows(g * 64, 64)
        v = out[at, :]
        for acc in accs:
            v = v + acc[at, :]
        out[at, :] = v
        return 0

    lax.fori_loop(0, 64, combine, 0)


def finish(freq, held, numbers):
    vmem = pl.BlockSpec(memory_space=pltpu.VMEM)
    smem = pl.BlockSpec(memory_space=pltpu.SMEM)
    count = held.shape[0] * held.shape[1]
    return pl.pallas_call(
        finish_kernel,
        out_shape=jax.ShapeDtypeStruct((4096, 128), f32),
        in_specs=[smem] + [vmem] * 3,
        out_specs=vmem,
        scratch_shapes=[pltpu.VMEM((count, 128), f32), pltpu.VMEM((TARGETS, count, 128), f32)]
        + [pltpu.VMEM((4096, 128), f32)] * 8,
        compiler_params=pltpu.CompilerParams(vmem_limit_bytes=56 * 1024 * 1024),
    )(numbers, freq.reshape(-1, 128), TABLES["tzi"], held.reshape(count, -1))


def padded(assay, weights, owner, cell, pencils):
    count = owner.shape[0]
    order = jnp.arange(count, dtype=i32)
    earlier = order[:, None] < order[None, :]
    same = jnp.sum(earlier & (owner[:, None] == owner[None, :]), axis=0, dtype=i32)
    row = cell // NZ
    fields = [jnp.zeros((count,), i32), row // 256, row % 256, cell % NZ]
    for k in range(TARGETS):
        fields += [pencils[:, k] // 256, pencils[:, k] % 256]
    fields = [x.astype(bf16) for x in fields] + [assay]
    parts = jnp.zeros((count, 128), bf16).at[:, : len(fields)].set(jnp.stack(fields, axis=1))
    load = jnp.concatenate([weights, parts], axis=1)
    slots = jnp.arange(WIDE * NARROW * 8, dtype=i32)
    hot = (slots[:, None] == (owner * 8 + same)[None, :]).astype(bf16)
    held = jnp.dot(hot, load, preferred_element_type=f32).astype(bf16)
    held = held.reshape(WIDE, NARROW, 8, -1)
    held = lax.all_to_all(held, "wide", split_axis=0, concat_axis=0, tiled=True)
    held = lax.all_to_all(held, "narrow", split_axis=1, concat_axis=1, tiled=True)
    held = held.reshape(WIDE, 64, -1)
    names = held.reshape(WIDE * 64, -1)[:, TARGETS * NZ :].astype(f32)
    numbers = jnp.einsum("fc,gjc->gfj", jnp.asarray(JOIN, f32), names.reshape(16, 128, 128),
                         precision=lax.Precision.HIGHEST)
    return held, jnp.round(numbers).astype(i32)


def local(noise, spectrum, assay, measure_weights, measure_owner, measure_cell, measure_pencils):
    count = measure_owner.shape[1]
    freq, held, numbers, flag = spectral(
        noise, spectrum, measure_owner, measure_cell, assay, measure_pencils[0].T,
        measure_weights.reshape(count * TARGETS, NZ),
    )

    def roomy(_):
        weights = measure_weights[0].reshape(count, TARGETS * NZ)
        more = padded(assay[0], weights, measure_owner[0], measure_cell[0], measure_pencils[0])
        return finish(freq, *more)

    field = lax.cond(flag[0, 0] > 0, roomy, lambda _: finish(freq, held, numbers), 0)
    return field.reshape(noise.shape)


def solution(mesh):
    placed = (
        P("narrow", "wide", None),
        P("wide", None, "narrow"),
        P(("wide", "narrow"), None),
        P(("wide", "narrow"), None, None, None),
        P(("wide", "narrow"), None),
        P(("wide", "narrow"), None),
        P(("wide", "narrow"), None, None),
    )
    return jax.shard_map(
        local, mesh=mesh, in_specs=placed, out_specs=P("narrow", "wide", None), check_vma=False
    )
```

```python
import functools
import math

import jax
import jax.numpy as jnp
import ml_dtypes
import numpy as np
from jax import lax
from jax.experimental import pallas as pl
from jax.experimental.pallas import tpu as pltpu
from jax.sharding import PartitionSpec as P

NX, NY, NZ = 1024, 1024, 128
TARGETS = 4
WIDE, NARROW = 32, 8
SLOTS = 2
MESH = pl.DeviceIdType.MESH
f32, bf16, i32 = jnp.float32, jnp.bfloat16, jnp.int32

LN2 = math.log(2.0)
CODE = 16.0 / LN2
PEAK = 32600.0
TINY = 1e-30
SPEC_LOW = math.log(0.1)
SPEC_CODE = 65000.0 / math.log(85.0)
ROOT_HALF = math.sqrt(0.5)


def split(a):
    high = a.astype(ml_dtypes.bfloat16)
    low = (a - high.astype(np.float64)).astype(ml_dtypes.bfloat16)
    return high, low


def pair_matrix(sign):
    index = np.arange(128)
    angle = 2 * np.pi * (index[:, None] * index[None, :] % 128) / 128
    c, s = np.cos(angle), sign * np.sin(angle)
    return np.block([[c, -s], [s, c]])


def depth_forward():
    kz = 2 * np.arange(32)[None, :] + np.arange(2)[:, None]
    kz = kz.reshape(-1)
    z = np.arange(128)
    angle = 2 * np.pi * (kz[:, None] * z[None, :] % 128) / 128
    re, im = np.cos(angle), -np.sin(angle)
    im[kz == 0] = np.cos(np.pi * z)
    return np.concatenate([re, im], 0)


def depth_inverse():
    kz = (2 * np.arange(32)[None, :] + np.arange(2)[:, None]).reshape(-1)
    z = np.arange(128)
    angle = 2 * np.pi * (kz[:, None] * z[None, :] % 128) / 128
    re, im = 2 * np.cos(angle), -2 * np.sin(angle)
    re[kz == 0] = 1.0
    im[kz == 0] = np.cos(np.pi * z)
    return np.concatenate([re, im], 0)


def make_tables():
    h, l = split(depth_forward())
    tz = np.concatenate([h, l, h], 1)
    h, l = split(depth_inverse())
    tzi = np.concatenate([h, l, h], 0)
    yf = np.stack(split(pair_matrix(-1.0)))
    yi = np.stack(split(pair_matrix(1.0)))
    xf = np.stack(split(pair_matrix(-1.0).T))
    xi = np.stack(split(pair_matrix(1.0).T))
    c = np.arange(8)
    a = np.arange(128)
    angle = 2 * np.pi * c[:, None] * a[None, :] / 1024
    tx = np.stack([np.cos(angle), np.sin(angle)]).astype(np.float32)
    row = np.arange(128)
    lane_of = 8 * (row % 16) + row // 16
    own = np.zeros((128, 128))
    own[row, lane_of] = 1
    mir = np.zeros((128, 128))
    mir[row, (128 - lane_of) % 128] = 1
    own2 = np.concatenate([own, own], 1).astype(ml_dtypes.bfloat16)
    flips = np.zeros((2, 128, 128))
    flips[0, (128 - row) % 128, row] = 1
    flips[1, 127 - row, row] = 1
    flips = np.concatenate([flips, flips], 1).astype(ml_dtypes.bfloat16)
    return dict(
        tz=tz, tzi=tzi, yf=yf, yi=yi, xf=xf, xi=xi, tx=tx, own2=own2,
        mir=mir.astype(ml_dtypes.bfloat16), flips=flips,
    )


TABLES = make_tables()
ROOM = 160


def join_matrix():
    m = np.zeros((8, 128))
    m[0, 1], m[0, 2] = 256, 1
    for k in range(TARGETS):
        m[1 + k, 4 + 2 * k], m[1 + k, 5 + 2 * k] = 256, 1
    m[5, 13] = 1
    return m.astype(ml_dtypes.bfloat16)


JOIN = join_matrix()


def halves(v):
    h = v.astype(bf16)
    return h, (v - h.astype(f32)).astype(bf16)


def times_i(v, sign):
    re, im = v
    return (-im, re) if sign > 0 else (im, -re)


def add(a, b):
    return a[0] + b[0], a[1] + b[1]


def sub(a, b):
    return a[0] - b[0], a[1] - b[1]


def dft4(v, sign):
    s, d = add(v[0], v[2]), sub(v[0], v[2])
    t, u = add(v[1], v[3]), times_i(sub(v[1], v[3]), sign)
    return [add(s, t), add(d, u), sub(s, t), sub(d, u)]


def dft8(v, sign):
    e = dft4(v[0::2], sign)
    o = dft4(v[1::2], sign)
    g = float(sign)
    re, im = o[1]
    o[1] = ((re - g * im) * ROOT_HALF, (im + g * re) * ROOT_HALF)
    o[2] = times_i(o[2], sign)
    re, im = o[3]
    o[3] = ((-re - g * im) * ROOT_HALF, (g * re - im) * ROOT_HALF)
    return [add(e[c], o[c]) for c in range(4)] + [sub(e[c], o[c]) for c in range(4)]


def turn(v, cos, sin, sign):
    re, im = v
    if sign < 0:
        return re * cos + im * sin, im * cos - re * sin
    return re * cos - im * sin, im * cos + re * sin


def scale_code(m):
    return jnp.ceil(jnp.log(jnp.maximum(m, TINY)) * CODE).astype(i32)


def encode_factor(code):
    return jnp.exp(code.astype(f32) * (-1.0 / CODE)) * PEAK


def decode_factor(code):
    return jnp.exp(code.astype(f32) * (1.0 / CODE)) * (1.0 / PEAK)


def pack(re, im):
    a = jnp.round(re).astype(i32)
    b = jnp.round(im).astype(i32)
    return (a << 16) | (b & 0xFFFF)


def unpack(word):
    return (word >> 16).astype(f32), ((word << 16) >> 16).astype(f32)


def tile_max(tiles):
    tiles = [jnp.abs(t) for t in tiles]
    while len(tiles) > 1:
        tiles = [jnp.maximum(a, b) for a, b in zip(tiles[0::2], tiles[1::2])] + (
            tiles[-1:] if len(tiles) % 2 else []
        )
    return tiles[0]


def mm(a, b):
    return jnp.dot(a, b, preferred_element_type=f32)


def mm_t(a, b):
    return lax.dot_general(a, b, (((1,), (1,)), ((), ())), preferred_element_type=f32)


def rows(start, size):
    return pl.ds(pl.multiple_of(start, 8), size)


def rows16(start, size):
    return pl.ds(pl.multiple_of(start, 16), size)


def spectral_kernel(
    noise, spec, tz, yf, yi, xf, xi, tyc, tys, tx, own2, mir, flips, owner, cell, assay, pencils, loads, join,
    out, got, numbers, flag,
    zre, zim, ws, wr, bh, bl, big, big2, ns, nr, lh, ll, ms, mr, us,
    ear, bsp, vs, vr, vc, wf, weights, parts, asend, arecv, psend, precv, bsend, brecv,
    w_send, w_recv, n_send, n_recv, m_send, m_recv, u_send, u_recv, v_send, v_recv,
    a_send, a_recv, p_send, p_recv, b_send, b_recv, g_sem,
):
    me_w = lax.axis_index("wide")
    me_n = lax.axis_index("narrow")
    special = me_w == 0
    edge = special & ((me_n == 0) | (me_n == 4))

    barrier = pltpu.get_barrier_semaphore()

    def greet_wide(i, _):
        pl.semaphore_signal(
            barrier, inc=1, device_id={"wide": lax.rem(me_w + i, WIDE)}, device_id_type=MESH
        )
        return 0

    def greet_narrow(i, _):
        pl.semaphore_signal(
            barrier, inc=1, device_id={"narrow": lax.rem(me_n + i, NARROW)}, device_id_type=MESH
        )
        return 0

    lax.fori_loop(1, WIDE, greet_wide, 0)
    lax.fori_loop(1, NARROW, greet_narrow, 0)

    def wide_copy(src, dst, sends, recvs, s, peer, slot):
        return pltpu.make_async_remote_copy(
            src_ref=src.at[s, peer], dst_ref=dst.at[s, slot], send_sem=sends.at[s, peer],
            recv_sem=recvs.at[s, slot], device_id={"wide": peer}, device_id_type=MESH,
        )

    def narrow_copy(src, dst, sends, recvs, s, peer, slot):
        return pltpu.make_async_remote_copy(
            src_ref=src.at[s, peer], dst_ref=dst.at[s, slot], send_sem=sends.at[s, peer],
            recv_sem=recvs.at[s, slot], device_id={"narrow": peer}, device_id_type=MESH,
        )

    def code_and_send(code, make, count, me, args, s):
        def one(i, _):
            peer = lax.rem(me + i, count)
            code(peer)
            make(*args, s, peer, me).start()
            return 0

        lax.fori_loop(1, count, one, 0)
        code(me)

    def recv_all(make, count, me, args, s):
        def one(i, _):
            peer = lax.rem(me + i, count)
            make(*args, s, peer, peer).wait_recv()
            return 0

        lax.fori_loop(1, count, one, 0)

    def sent_all(make, count, me, args, s):
        def one(i, _):
            peer = lax.rem(me + i, count)
            make(*args, s, peer, peer).wait_send()
            return 0

        lax.fori_loop(1, count, one, 0)

    w_args = (ws, wr, w_send, w_recv)
    n_args = (ns, nr, n_send, n_recv)
    m_args = (ms, mr, m_send, m_recv)
    u_args = (us, out, u_send, u_recv)

    room = asend.shape[1]
    count = owner.shape[1]
    owners = owner[...]
    cells = cell[...]
    narrow_of = (owners & 7).astype(f32)
    diagonal = lax.broadcasted_iota(i32, (128, 128), 0) == lax.broadcasted_iota(i32, (128, 128), 1)

    def column(line):
        pieces = []
        for k in range(count // 128):
            piece = jnp.broadcast_to(line[:, 128 * k : 128 * k + 128], (128, 128))
            pieces.append(jnp.sum(jnp.where(diagonal, piece, 0.0), axis=1, keepdims=True))
        return jnp.concatenate(pieces, axis=0)

    earlier = lax.broadcasted_iota(i32, (count, count), 0) < lax.broadcasted_iota(i32, (count, count), 1)

    def before(line):
        match = earlier & (column(line) == line)
        return jnp.sum(jnp.where(match, 1.0, 0.0), axis=0, keepdims=True)

    same = before(owners.astype(f32))
    rank = before(narrow_of)
    place = jnp.where(rank < room, narrow_of * room + rank, -1.0).astype(i32)
    over = jnp.max(jnp.where(rank < room, 0.0, 1.0), axis=1, keepdims=True)
    key = (owners >> 3 << 3).astype(f32) + same + 1.0
    part_row = lax.broadcasted_iota(i32, (16, count), 0)
    listed = jnp.zeros((16, count), f32)
    for r, line in (
        (0, key),
        (1, (cells >> 15).astype(f32)),
        (2, ((cells >> 7) & 255).astype(f32)),
        (3, (cells & 127).astype(f32)),
        (12, assay[...].astype(f32)),
        *((4 + 2 * k, (pencils[k : k + 1, :] >> 8).astype(f32)) for k in range(TARGETS)),
        *((5 + 2 * k, (pencils[k : k + 1, :] & 255).astype(f32)) for k in range(TARGETS)),
    ):
        listed = jnp.where(part_row == r, line, listed)
    parts[...] = listed.astype(bf16)
    wf[...] = loads[...].astype(f32)
    for k in range(TARGETS):
        weights[:, 128 * k : 128 * k + 128] = wf[pl.ds(k, count, stride=TARGETS), :].astype(bf16)
    room_row = lax.broadcasted_iota(i32, (room, count), 0)
    flag_row = lax.broadcasted_iota(i32, (16, room), 0) == 13

    def pack_measures(n, _):
        hot = jnp.where(room_row + n * room == place, 1.0, 0.0).astype(bf16)
        asend[n] = mm(hot, weights[...]).astype(bf16)
        psend[n] = jnp.where(flag_row, over, mm_t(parts[...], hot)).astype(bf16)
        return 0

    lax.fori_loop(0, NARROW, pack_measures, 0)
    arecv[me_n] = asend[me_n]
    precv[me_n] = psend[me_n]

    def to_narrow(src, dst, sends, recvs, peer, slot):
        return pltpu.make_async_remote_copy(
            src_ref=src.at[peer], dst_ref=dst.at[slot], send_sem=sends.at[peer],
            recv_sem=recvs.at[slot], device_id={"narrow": peer}, device_id_type=MESH,
        )

    def to_wide(peer, slot):
        return pltpu.make_async_remote_copy(
            src_ref=bsend.at[peer], dst_ref=brecv.at[slot], send_sem=b_send.at[peer],
            recv_sem=b_recv.at[slot], device_id={"wide": peer}, device_id_type=MESH,
        )

    a_args = (asend, arecv, a_send, a_recv)
    p_args = (psend, precv, p_send, p_recv)

    def send_measures(i, _):
        peer = lax.rem(me_n + i, NARROW)
        to_narrow(*p_args, peer, me_n).start()
        to_narrow(*a_args, peer, me_n).start()
        return 0

    def recv_measures(i, _):
        peer = lax.rem(me_n + i, NARROW)
        to_narrow(*p_args, peer, peer).wait_recv()
        to_narrow(*a_args, peer, peer).wait_recv()
        return 0

    def sent_measures(i, _):
        peer = lax.rem(me_n + i, NARROW)
        to_narrow(*p_args, peer, peer).wait_send()
        to_narrow(*a_args, peer, peer).wait_send()
        return 0

    def send_groups(i, _):
        to_wide(lax.rem(me_w + i, WIDE), me_w).start()
        return 0

    def recv_groups(i, _):
        peer = lax.rem(me_w + i, WIDE)
        to_wide(peer, peer).wait_recv()
        return 0

    def sent_groups(i, _):
        peer = lax.rem(me_w + i, WIDE)
        to_wide(peer, peer).wait_send()
        return 0

    pl.semaphore_wait(barrier, WIDE - 1 + NARROW - 1)
    lax.fori_loop(1, NARROW, send_measures, 0)

    late = special & (me_n >= 4)
    own_slots = (jnp.where(late, 2, 0), 1)
    mir_slots = (jnp.where(special & (me_n < 4), 2, jnp.where(special, 0, 2)), 3)

    def spectrum_rows(slot, e):
        return halves(spec[pl.ds(slot * 1024 + e, 128, stride=8), :])

    for e in range(8):
        back = (8 - e) % 8
        flip = flips[0 if e == 0 else 1]
        codes = []
        for s in range(SLOTS):
            h, l = spectrum_rows(own_slots[s], e)
            ear[s, e] = mm_t(own2[...], jnp.concatenate([h, l], axis=1))
            h, l = spectrum_rows(mir_slots[s], back)
            gh = mm_t(mir[...], h).astype(bf16)
            gl = mm_t(mir[...], l).astype(bf16)
            v = mm(jnp.concatenate([gh, gl], axis=1), flip)
            q = jnp.round((jnp.log(v) - SPEC_LOW) * SPEC_CODE - 32500.0)
            codes.append(jnp.clip(q, -32767.0, 32767.0))
        vs[e] = pack(codes[0], codes[1])

    v_main = pltpu.make_async_remote_copy(
        src_ref=vs, dst_ref=vr, send_sem=v_send.at[0], recv_sem=v_recv.at[0],
        device_id={"narrow": 7 - me_n}, device_id_type=MESH,
    )
    v_side = pltpu.make_async_remote_copy(
        src_ref=vs.at[:, pl.ds(0, 8), :], dst_ref=vc, send_sem=v_send.at[1], recv_sem=v_recv.at[1],
        device_id={"narrow": lax.rem(8 - me_n, 8)}, device_id_type=MESH,
    )

    alone = (me_n == 0) | (me_n == 4)

    @pl.when(alone)
    def _():
        vc[...] = vs[:, 0:8, :]

    v_main.start()

    @pl.when(jnp.logical_not(alone))
    def _():
        v_side.start()

    def depth(y, _):
        cells = [y * 4 + k for k in range(4)]
        pieces = []
        for k in cells:
            h, l = halves(noise[pl.ds(k, 128, stride=32), :])
            pieces.append(jnp.concatenate([h, h, l], axis=1))
        res = mm_t(tz[...], jnp.concatenate(pieces, axis=0))
        for i, k in enumerate(cells):
            zre[pl.ds(k, 64, stride=32), :] = res[:64, 128 * i : 128 * i + 128]
            zim[pl.ds(k, 64, stride=32), :] = res[64:, 128 * i : 128 * i + 128]
        return 0

    lax.fori_loop(0, 8, depth, 0)

    def code_wide(read, dst, s, w, to):
        re, im = read(w)
        m = tile_max([re[8 * t : 8 * t + 8] for t in range(4)] + [im[8 * t : 8 * t + 8] for t in range(4)])
        code = scale_code(m)
        fac = encode_factor(code)
        for t in range(4):
            sl = slice(8 * t, 8 * t + 8)
            dst[s, to, 8 * t : 8 * t + 8, :] = pack(re[sl] * fac, im[sl] * fac)
        dst[s, to, 32:40, :] = code

    for s in range(SLOTS):
        def read_depth(w, s=s):
            at = rows((s * 32 + w) * 32, 32)
            return zre[at, :], zim[at, :]

        def code_one(w, s=s, read=read_depth):
            code_wide(read, ws, s, w, w)

        code_and_send(code_one, wide_copy, WIDE, me_w, w_args, s)
        wr[s, me_w] = ws[s, me_w]

    def second_forward(s, p, q, r):
        def group(g, _):
            dec = [decode_factor(wr[s, 4 * b + g, 32:40, :]) for b in range(8)]
            dec = [jnp.concatenate([d, d], axis=0) for d in dec]
            for t in range(2):
                v = []
                for b in range(8):
                    re, im = unpack(wr[s, 4 * b + g, 16 * t : 16 * t + 16, :])
                    re, im = re * dec[b], im * dec[b]
                    if p is not None:
                        re, im = re * p + im * q, im * r
                    v.append((re, im))
                v = dft8(v, -1)
                at = rows16(g * 32 + 16 * t, 16)
                at_im = rows16(128 + g * 32 + 16 * t, 16)
                for c in range(8):
                    w = v[c] if c == 0 else turn(v[c], tyc[c, at, :], tys[c, at, :], -1)
                    lanes = slice(128 * (c % 2), 128 * (c % 2) + 128)
                    for dst, part in ((at, w[0]), (at_im, w[1])):
                        h, l = halves(part)
                        bh[c // 2, dst, lanes] = h
                        bl[c // 2, dst, lanes] = l
            return 0

        lax.fori_loop(0, 4, group, 0)
        for cp in range(4):
            big[cp] = mm(yf[0], bh[cp]) + mm(yf[1], bh[cp]) + mm(yf[0], bl[cp])

    first_row = lax.broadcasted_iota(i32, (8, 128), 0) == 0

    def code_narrow(s, n):
        tiles = []
        for c in range(8):
            lanes = slice(128 * (c % 2), 128 * (c % 2) + 128)
            for t in range(2):
                tiles.append((
                    big[c // 2, rows(16 * n + 8 * t, 8), lanes],
                    big[c // 2, rows(128 + 16 * n + 8 * t, 8), lanes],
                ))
        code = scale_code(tile_max([x for pair in tiles for x in pair]))
        fac = encode_factor(code)
        for k, (re, im) in enumerate(tiles):
            ns[s, n, 8 * k : 8 * k + 8, :] = pack(re * fac, im * fac)
        ns[s, n, 128:136, :] = code

    for s in range(SLOTS):
        recv_all(wide_copy, WIDE, me_w, w_args, s)
        if s == 0:
            one = jnp.where(special, 0.0, 1.0)
            second_forward(s, 1.0, 0.0, one)

            @pl.when(special)
            def _():
                big2[...] = big[...]
                second_forward(0, 0.0, 1.0, 0.0)
                top = big[0, 0:8, 0:128]
                mid = big[0, 64:72, 0:128]
                big[:, 0:64, :] = big2[:, 0:64, :]
                big[:, 128:192, :] = big2[:, 128:192, :]
                big[0, 128:136, 0:128] = jnp.where(first_row, top, big[0, 128:136, 0:128])
                big[0, 192:200, 0:128] = jnp.where(first_row, mid, big[0, 192:200, 0:128])
                big[0, 64:72, 0:128] = jnp.where(first_row, big2[0, 64:72, 0:128], mid)
        else:
            second_forward(s, None, None, None)

        code_and_send(functools.partial(code_narrow, s), narrow_copy, NARROW, me_n, n_args, s)
        nr[s, me_n] = ns[s, me_n]


    def regroup():
        lax.fori_loop(1, NARROW, recv_measures, 0)
        row = lax.broadcasted_iota(i32, (512, room), 0)
        want = (((row >> 4) << 3) + (row & 7) + 1).astype(f32)
        flags = precv[0].astype(f32)
        for k in range(1, NARROW):
            flags = jnp.maximum(flags, precv[k].astype(f32))
        flags = jnp.max(jnp.where(flag_row, flags, 0.0), axis=1, keepdims=True)
        flags = jnp.max(flags, axis=0, keepdims=True)
        flag_col = lax.broadcasted_iota(i32, (512, 128), 1) == 13
        for q in range(4):
            moved, named = 0.0, 0.0
            for k in range(2):
                key = precv[2 * q + k, 0:1, :].astype(f32)
                match = (((row >> 3) & 1) == k) & (want == key)
                hot = jnp.where(match, 1.0, 0.0).astype(bf16)
                moved = moved + mm(hot, arecv[2 * q + k])
                named = named + mm_t(hot, precv[2 * q + k])
            named = jnp.concatenate([named, jnp.zeros((512, 112), f32)], axis=1)
            named = jnp.where(flag_col, flags, named)
            bsend[:, 16 * q : 16 * q + 16, 0:512] = moved.astype(bf16).reshape(WIDE, 16, 512)
            bsend[:, 16 * q : 16 * q + 16, 512:640] = named.astype(bf16).reshape(WIDE, 16, 128)
        brecv[me_w] = bsend[me_w]
        lax.fori_loop(1, WIDE, send_groups, 0)

    regroup()

    total = 1.0 / (NX * NY * NZ)
    v_main.wait_recv()

    @pl.when(jnp.logical_not(alone))
    def _():
        v_side.wait_recv()

    def decode_spectrum(q):
        return jnp.exp((q + 32500.0) * (1.0 / SPEC_CODE) + SPEC_LOW)

    bsp[...] = jnp.zeros_like(bsp)

    @pl.when(edge)
    def _():
        sigma = jnp.where(me_n == 0, 1.0, -1.0)
        xs, vv = [], []
        for e in range(8):
            xs.append(ear[0, e, 0:8, :])
            vv.append(decode_spectrum(unpack(vc[e])[0]))

        def even(list_of, e):
            h, l = halves(list_of[(8 - e) % 8])
            pair = jnp.concatenate([h, l], axis=1)
            flip = flips[0 if e == 0 else 1]
            return (mm(pair, flip) + list_of[e]) * 0.5

        for e in range(8):
            a, b = even(xs, e), even(vv, e)
            bsp[e, 0:8, :] = jnp.where(first_row, (a - b) * (0.5 * total) * sigma, 0.0)
            big2[0, 8 * e : 8 * e + 8, 0:128] = (a + b) * (0.5 * total)

    for e in range(8):
        m0, m1 = unpack(vr[e])
        s0, s1 = unpack(vc[e])
        for s, m, side in ((0, m0, s0), (1, m1, s1)):
            m, side = decode_spectrum(m), decode_spectrum(side)
            ear_e = ear[s, e]
            lead = jnp.where(first_row, side, m[0:8])
            ear[s, e, 8:128, :] = (ear_e[8:128] + m[8:128]) * (0.5 * total)
            ear[s, e, 0:8, :] = (ear_e[0:8] + lead) * (0.5 * total)

    @pl.when(edge)
    def _():
        for e in range(8):
            ear[0, e, 0:8, :] = jnp.where(
                first_row, big2[0, 8 * e : 8 * e + 8, 0:128], ear[0, e, 0:8, :]
            )

    def first_both(s):
        def decs(n):
            d = decode_factor(nr[s, n, 128:136, :])
            return jnp.concatenate([d, d], axis=0)

        for n in range(8):
            big2[0, 16 * n : 16 * n + 16, 0:128] = decs(n)

        def load(c):
            v = []
            for n in range(8):
                re, im = unpack(nr[s, n, rows16(16 * c, 16), :])
                d = big2[0, 16 * n : 16 * n + 16, 0:128]
                v.append((re * d, im * d))
            return v

        def put(v, at):
            v = dft8(v, -1)
            for e in range(8):
                w = v[e] if e == 0 else turn(v[e], tx[0, e : e + 1, :], tx[1, e : e + 1, :], -1)
                for lanes, part in ((slice(0, 128), w[0]), (slice(128, 256), w[1])):
                    h, l = halves(part)
                    lh[e, at, lanes] = h
                    ll[e, at, lanes] = l

        def block(c, _):
            put(load(c), rows16(16 * c, 16))
            return 0

        lax.fori_loop(0, 8, block, 0)
        if s == 0:
            put([(re, -im) for re, im in load(0)], slice(128, 144))
        count = 144 if s == 0 else 128
        for e in range(8):
            h, l = lh[e, 0:count, :], ll[e, 0:count, :]
            z = mm(h, xf[0]) + mm(h, xf[1]) + mm(l, xf[0])
            fil = jnp.concatenate([ear[s, e], ear[s, e]], axis=1)
            g = z[0:128] * fil
            if s == 0:
                extra = jnp.concatenate([bsp[e], bsp[e]], axis=1)
                g = jnp.concatenate([g[0:16] + z[128:144] * extra, g[16:128]], axis=0)
            h, l = halves(g)
            big[e // 2, 128 * (e % 2) : 128 * (e % 2) + 128, :] = (
                mm(h, xi[0]) + mm(h, xi[1]) + mm(l, xi[0])
            )

        def unblock(c, _):
            v = []
            for e in range(8):
                at = rows16(128 * (e % 2) + 16 * c, 16)
                y = (big[e // 2, at, 0:128], big[e // 2, at, 128:256])
                v.append(y if e == 0 else turn(y, tx[0, e : e + 1, :], tx[1, e : e + 1, :], 1))
            v = dft8(v, 1)
            for n in range(8):
                at = rows16(128 * (n % 2) + 16 * c, 16)
                big2[n // 2, at, 0:128] = v[n][0]
                big2[n // 2, at, 128:256] = v[n][1]
            return 0

        lax.fori_loop(0, 8, unblock, 0)

    def code_first(s, n):
        page, base = lax.div(n, 2), 128 * lax.rem(n, 2)
        tiles = []
        for k in range(16):
            at = rows(base + 8 * k, 8)
            tiles.append((big2[page, at, 0:128], big2[page, at, 128:256]))
        code = scale_code(tile_max([x for pair in tiles for x in pair]))
        fac = encode_factor(code)
        for k, (re, im) in enumerate(tiles):
            ms[s, n, 8 * k : 8 * k + 8, :] = pack(re * fac, im * fac)
        ms[s, n, 128:136, :] = code

    for s in range(SLOTS):
        recv_all(narrow_copy, NARROW, me_n, n_args, s)
        first_both(s)
        code_and_send(functools.partial(code_first, s), narrow_copy, NARROW, me_n, m_args, s)
        mr[s, me_n] = ms[s, me_n]

    row16 = lax.broadcasted_iota(i32, (16, 128), 0)

    def second_back(s, part):
        def fill(n, _):
            d = decode_factor(mr[s, n, 128:136, :])
            d = jnp.concatenate([d, d], axis=0)
            if part is not None:
                if part == 0:
                    f = jnp.where(special, jnp.where(n < 4, 2.0, 0.0), 1.0)
                else:
                    f = jnp.where(n < 4, 0.0, 2.0)
                hit = (row16 == 0) & (special & ((n == 0) | (n == 4)))
            for c in range(8):
                re, im = unpack(mr[s, n, 16 * c : 16 * c + 16, :])
                re, im = re * d, im * d
                if part == 0:
                    if c == 0:
                        re, im = jnp.where(hit, re, re * f), jnp.where(hit, 0.0, im * f)
                    else:
                        re, im = re * f, im * f
                elif part == 1:
                    if c == 0:
                        re, im = jnp.where(hit, im, re * f), jnp.where(hit, 0.0, im * f)
                    else:
                        re, im = re * f, im * f
                lanes = slice(128 * (c % 2), 128 * (c % 2) + 128)
                for dst, x in ((rows16(16 * n, 16), re), (rows16(128 + 16 * n, 16), im)):
                    h, l = halves(x)
                    bh[c // 2, dst, lanes] = h
                    bl[c // 2, dst, lanes] = l
            return 0

        lax.fori_loop(0, 8, fill, 0)
        for cp in range(4):
            big[cp] = mm(yi[0], bh[cp]) + mm(yi[1], bh[cp]) + mm(yi[0], bl[cp])

        def spread(t, _):
            v = []
            at = rows16(16 * t, 16)
            for c in range(8):
                lanes = slice(128 * (c % 2), 128 * (c % 2) + 128)
                y = (big[c // 2, at, lanes], big[c // 2, rows16(128 + 16 * t, 16), lanes])
                v.append(y if c == 0 else turn(y, tyc[c, at, :], tys[c, at, :], 1))
            v = dft8(v, 1)
            for b in range(8):
                to = rows16(128 * (b % 2) + 16 * t, 16)
                if part == 1:
                    big2[b // 2, to, 128:256] = v[b][0]
                else:
                    big2[b // 2, to, 0:128] = v[b][0]
                    big2[b // 2, to, 128:256] = v[b][1]
            return 0

        lax.fori_loop(0, 8, spread, 0)

    for s in range(SLOTS):
        recv_all(narrow_copy, NARROW, me_n, m_args, s)
        second_back(s, 0 if s == 0 else None)
        if s == 0:
            @pl.when(special)
            def _():
                second_back(0, 1)

        def read_back(w):
            b = w // 4
            at = rows((b % 2) * 128 + (w % 4) * 32, 32)
            return big2[b // 2, at, 0:128], big2[b // 2, at, 128:256]

        def code_back(w, s=s):
            code_wide(read_back, us, s, w, w)

        code_and_send(code_back, wide_copy, WIDE, me_w, u_args, s)
        keep = pltpu.make_async_copy(us.at[s, me_w], out.at[s, me_w], u_recv.at[s, me_w])
        keep.start()

    lax.fori_loop(1, WIDE, recv_groups, 0)
    pltpu.make_async_copy(brecv, got, g_sem.at[0]).start()
    for g in range(16):
        named = jnp.concatenate(
            [brecv[2 * g, :, 512:640], brecv[2 * g + 1, :, 512:640]], axis=0
        )
        listed = jnp.round(mm_t(join[...], named))
        numbers[g] = listed.astype(i32)
        marks = listed if g == 0 else jnp.maximum(marks, listed)
    flag[0, 0] = jnp.max(marks[5:6, :]).astype(i32)
    lax.fori_loop(1, WIDE, sent_groups, 0)
    lax.fori_loop(1, NARROW, sent_measures, 0)
    pltpu.make_async_copy(brecv, got, g_sem.at[0]).wait()

    for s in range(SLOTS):
        pltpu.make_async_copy(us.at[s, me_w], out.at[s, me_w], u_recv.at[s, me_w]).wait()
        recv_all(wide_copy, WIDE, me_w, u_args, s)
        sent_all(wide_copy, WIDE, me_w, w_args, s)
        sent_all(narrow_copy, NARROW, me_n, n_args, s)
        sent_all(narrow_copy, NARROW, me_n, m_args, s)
        sent_all(wide_copy, WIDE, me_w, u_args, s)
    v_main.wait_send()

    @pl.when(jnp.logical_not(alone))
    def _():
        v_side.wait_send()


def spectral(noise, spectrum, owner, cell, assay, pencils, loads):
    t = TABLES
    angle = 2 * np.pi * np.arange(8)[:, None] * np.arange(128)[None, :] / 1024
    tyc = np.repeat(np.cos(angle).astype(np.float32)[:, :, None], 128, axis=2)
    tys = np.repeat(np.sin(angle).astype(np.float32)[:, :, None], 128, axis=2)
    vmem = pl.BlockSpec(memory_space=pltpu.VMEM)
    dma = pltpu.SemaphoreType.DMA
    return pl.pallas_call(
        spectral_kernel,
        out_shape=(
            jax.ShapeDtypeStruct((SLOTS, WIDE, 40, 128), i32),
            jax.ShapeDtypeStruct((WIDE, 64, 640), bf16),
            jax.ShapeDtypeStruct((16, 8, 128), i32),
            jax.ShapeDtypeStruct((1, 1), i32),
        ),
        in_specs=[vmem] * 19,
        out_specs=(
            pl.BlockSpec(memory_space=pl.ANY), pl.BlockSpec(memory_space=pl.ANY), vmem,
            pl.BlockSpec(memory_space=pltpu.SMEM),
        ),
        scratch_shapes=[
            pltpu.VMEM((2048, 128), f32),
            pltpu.VMEM((2048, 128), f32),
            pltpu.VMEM((SLOTS, WIDE, 40, 128), i32),
            pltpu.VMEM((SLOTS, WIDE, 40, 128), i32),
            pltpu.VMEM((4, 256, 256), bf16),
            pltpu.VMEM((4, 256, 256), bf16),
            pltpu.VMEM((4, 256, 256), f32),
            pltpu.VMEM((4, 256, 256), f32),
            pltpu.VMEM((SLOTS, NARROW, 136, 128), i32),
            pltpu.VMEM((SLOTS, NARROW, 136, 128), i32),
            pltpu.VMEM((8, 144, 256), bf16),
            pltpu.VMEM((8, 144, 256), bf16),
            pltpu.VMEM((SLOTS, NARROW, 136, 128), i32),
            pltpu.VMEM((SLOTS, NARROW, 136, 128), i32),
            pltpu.VMEM((SLOTS, WIDE, 40, 128), i32),
            pltpu.VMEM((SLOTS, 8, 128, 128), f32),
            pltpu.VMEM((8, 16, 128), f32),
            pltpu.VMEM((8, 128, 128), i32),
            pltpu.VMEM((8, 128, 128), i32),
            pltpu.VMEM((8, 8, 128), i32),
            pltpu.VMEM((2048, 128), f32),
            pltpu.VMEM((512, 512), bf16),
            pltpu.VMEM((16, 512), bf16),
            pltpu.VMEM((NARROW, ROOM, 512), bf16),
            pltpu.VMEM((NARROW, ROOM, 512), bf16),
            pltpu.VMEM((NARROW, 16, ROOM), bf16),
            pltpu.VMEM((NARROW, 16, ROOM), bf16),
            pltpu.VMEM((WIDE, 64, 640), bf16),
            pltpu.VMEM((WIDE, 64, 640), bf16),
            dma((SLOTS, WIDE)), dma((SLOTS, WIDE)),
            dma((SLOTS, NARROW)), dma((SLOTS, NARROW)),
            dma((SLOTS, NARROW)), dma((SLOTS, NARROW)),
            dma((SLOTS, WIDE)), dma((SLOTS, WIDE)),
            dma((2,)), dma((2,)),
            dma((NARROW,)), dma((NARROW,)), dma((NARROW,)), dma((NARROW,)),
            dma((WIDE,)), dma((WIDE,)), dma((1,)),
        ],
        compiler_params=pltpu.CompilerParams(
            collective_id=0, has_side_effects=True, vmem_limit_bytes=56 * 1024 * 1024
        ),
    )(
        noise.reshape(4096, 128), spectrum.reshape(4096, 128), t["tz"], t["yf"], t["yi"],
        t["xf"], t["xi"], tyc, tys, t["tx"], t["own2"], t["mir"], t["flips"],
        owner, cell, assay, pencils, loads, JOIN,
    )


def finish_kernel(numbers, freq, tzi, held, out, gathered, contrib, *accs):
    def depth(g, _):
        for acc in accs:
            acc[rows(g * 512, 512), :] = jnp.zeros((512, 128), f32)
        pieces = []
        for j in range(4):
            y = g * 4 + j
            re, im = unpack(freq[pl.ds(y, 64, stride=40), :])
            d = decode_factor(freq[pl.ds(32 + lax.rem(y, 8), 64, stride=40), :])
            h, l = halves(jnp.concatenate([re * d, im * d], axis=0))
            pieces.append(jnp.concatenate([h, h, l], axis=0))
        cells = lax.dot_general(
            jnp.concatenate(pieces, axis=1), tzi[...], (((0,), (0,)), ((), ())),
            preferred_element_type=f32,
        )
        for j in range(4):
            out[pl.ds(g * 4 + j, 128, stride=32), :] = cells[128 * j : 128 * j + 128]
        return 0

    lax.fori_loop(0, 8, depth, 0)
    groups = numbers.shape[0]

    def gather(g, _):
        for j in range(128):
            gathered[pl.ds(g * 128 + j, 1), :] = out[pl.ds(numbers[g, 0, j], 1), :]
        return 0

    lax.fori_loop(0, groups, gather, 0)
    lane = lax.broadcasted_iota(i32, (128, 128), 1)

    def residual(g, _):
        at = rows16(g * 128, 128)
        depth_at = held[at, 515:516].astype(i32)
        grade = held[at, 524:525].astype(f32)
        value = jnp.sum(jnp.where(lane == depth_at, gathered[at, :], 0.0), axis=1, keepdims=True)
        resid = grade - value
        for k in range(TARGETS):
            contrib[k, at, :] = resid * held[at, 128 * k : 128 * k + 128].astype(f32)
        return 0

    lax.fori_loop(0, groups, residual, 0)

    def scatter(g, _):
        for j in range(128):
            for t in range(TARGETS):
                acc = accs[t + TARGETS * (j % 2)]
                at = pl.ds(numbers[g, 1 + t, j], 1)
                acc[at, :] = acc[at, :] + contrib[t, pl.ds(g * 128 + j, 1), :]
        return 0

    lax.fori_loop(0, groups, scatter, 0)

    def combine(g, _):
        at = rows(g * 64, 64)
        v = out[at, :]
        for acc in accs:
            v = v + acc[at, :]
        out[at, :] = v
        return 0

    lax.fori_loop(0, 64, combine, 0)


def finish(freq, held, numbers):
    vmem = pl.BlockSpec(memory_space=pltpu.VMEM)
    smem = pl.BlockSpec(memory_space=pltpu.SMEM)
    count = held.shape[0] * held.shape[1]
    return pl.pallas_call(
        finish_kernel,
        out_shape=jax.ShapeDtypeStruct((4096, 128), f32),
        in_specs=[smem] + [vmem] * 3,
        out_specs=vmem,
        scratch_shapes=[pltpu.VMEM((count, 128), f32), pltpu.VMEM((TARGETS, count, 128), f32)]
        + [pltpu.VMEM((4096, 128), f32)] * 8,
        compiler_params=pltpu.CompilerParams(vmem_limit_bytes=56 * 1024 * 1024),
    )(numbers, freq.reshape(-1, 128), TABLES["tzi"], held.reshape(count, -1))


def padded(assay, weights, owner, cell, pencils):
    count = owner.shape[0]
    order = jnp.arange(count, dtype=i32)
    earlier = order[:, None] < order[None, :]
    same = jnp.sum(earlier & (owner[:, None] == owner[None, :]), axis=0, dtype=i32)
    row = cell // NZ
    fields = [jnp.zeros((count,), i32), row // 256, row % 256, cell % NZ]
    for k in range(TARGETS):
        fields += [pencils[:, k] // 256, pencils[:, k] % 256]
    fields = [x.astype(bf16) for x in fields] + [assay]
    parts = jnp.zeros((count, 128), bf16).at[:, : len(fields)].set(jnp.stack(fields, axis=1))
    load = jnp.concatenate([weights, parts], axis=1)
    slots = jnp.arange(WIDE * NARROW * 8, dtype=i32)
    hot = (slots[:, None] == (owner * 8 + same)[None, :]).astype(bf16)
    held = jnp.dot(hot, load, preferred_element_type=f32).astype(bf16)
    held = held.reshape(WIDE, NARROW, 8, -1)
    held = lax.all_to_all(held, "wide", split_axis=0, concat_axis=0, tiled=True)
    held = lax.all_to_all(held, "narrow", split_axis=1, concat_axis=1, tiled=True)
    held = held.reshape(WIDE, 64, -1)
    names = held.reshape(WIDE * 64, -1)[:, TARGETS * NZ :].astype(f32)
    numbers = jnp.einsum("fc,gjc->gfj", jnp.asarray(JOIN, f32), names.reshape(16, 128, 128),
                         precision=lax.Precision.HIGHEST)
    return held, jnp.round(numbers).astype(i32)


def local(noise, spectrum, assay, measure_weights, measure_owner, measure_cell, measure_pencils):
    count = measure_owner.shape[1]
    freq, held, numbers, flag = spectral(
        noise, spectrum, measure_owner, measure_cell, assay, measure_pencils[0].T,
        measure_weights.reshape(count * TARGETS, NZ),
    )

    def roomy(_):
        weights = measure_weights[0].reshape(count, TARGETS * NZ)
        more = padded(assay[0], weights, measure_owner[0], measure_cell[0], measure_pencils[0])
        return finish(freq, *more)

    field = lax.cond(flag[0, 0] > 0, roomy, lambda _: finish(freq, held, numbers), 0)
    return field.reshape(noise.shape)


def solution(mesh):
    placed = (
        P("narrow", "wide", None),
        P("wide", None, "narrow"),
        P(("wide", "narrow"), None),
        P(("wide", "narrow"), None, None, None),
        P(("wide", "narrow"), None),
        P(("wide", "narrow"), None),
        P(("wide", "narrow"), None, None),
    )
    return jax.shard_map(
        local, mesh=mesh, in_specs=placed, out_specs=P("narrow", "wide", None), check_vma=False
    )
```
